128 devices in a mesh: lat: 8 (over x_lo, z), lon: 16 (over y, x_hi, core).
Axes of the slice: x: 4 (x_hi: 2, x_lo: 2; x = x_hi * 2 + x_lo), y: 4, z: 4, core: 2. Of those that a mesh axis runs over, the one named last changes fastest.
Arguments:
- initial: float32 [3, 72, 64, 2048], P(None, None, 'lat', 'lon'), may hold values from -6 to 6
- east_wind: float32 [2, 72, 64, 2048], P(None, None, 'lat', 'lon'), may hold values from -0.3 to 0.3
- north_wind: float32 [2, 72, 64, 2048], P(None, None, 'lat', 'lon'), may hold values from -0.3 to 0.3
- mixing: float32 [2, 72, 64, 2048], P(None, None, 'lat', 'lon'), may hold values from 0.02 to 0.2
- kernel: bfloat16 [16384, 72, 128], P(('lat', 'lon')), may hold values from -0.75 to 0.75
- columns: int32 [16384, 128], P(('lat', 'lon')), may hold values from 0 to 3071
- observed: bfloat16 [16384, 128], P(('lat', 'lon')), may hold values from -6 to 6
- obs_weight: bfloat16 [16384, 128], P(('lat', 'lon')), may hold values from 1 to 8
- counts: int32 [16384], P(('lat', 'lon')), may hold values from 64 to 128
- targets: int32 [16384, 1], P(('lat', 'lon')), may hold values from 0 to 127; in each aligned block of 128 rows (0 to 127, 128 to 255, ...) at most 2 rows name the same one
Outputs:
- gradient: float32 [3, 72, 64, 2048], P(None, None, 'lat', 'lon')
- innovations: float32 [16384, 128], P(('lat', 'lon'))
The draws below stay inside these ranges and needn't reach their ends.
Inputs may be any that keep to these rules, and one draw needn't show every extreme that they name: `targets`: destinations are device indices over lat and lon in mesh order (lat index times the lon devices plus lon index). Among the blocks of one device at most 2 share a destination, and in every draw some device sends exactly 2 blocks to one destination. `columns`: the value is the tracer times 8 * 128 plus the cell's row times 128 plus its column, inside the destination device's block of the grid. The first counts[b] soundings of block b are live.
All inputs are finite; a program needn't handle non-finite values.
Results may differ from the reference program's by a relative error of at most 0.0005.
Values may be sent and summed in bfloat16 or wider, within the bound.
No kernel may reach another device: no remote copies, remote signals or barrier semaphores. Data moves between devices by JAX's collectives and lax.ppermute only.
A program may use at most 128 MiB of HBM per device.

```python
import math
import jax
import jax.numpy as jnp
import numpy as np
from jax import lax

TR = 3
LEV = 72
S = 128
STEPS = 2
CAP = 2
CLAT = 8
CLON = 128
BLK_DEV = 128
NLAT = 64
NLON = 2048
BLOCKS = 16384
N_LON = 16
DEVICES = 128


def with_ends(result, rng, least, high):
    extent = result.shape
    place = [jax.random.randint(jax.random.fold_in(rng, axis), (), 0, extent[axis]) for axis in range(len(extent))]
    result = result.at[tuple(place)].set(least)
    longest = extent.index(max(extent))
    place[longest] = (place[longest] + 1) % extent[longest]
    return result.at[tuple(place)].set(high)


def levels(stream_key, extent, split, least, largest):
    gain, own = 1.0, jax.random.fold_in(stream_key, 6)
    for dim, blocks in split:
        draws = jnp.exp(jax.random.uniform(jax.random.fold_in(own, dim), (blocks,), jnp.float32, least / len(split), largest / len(split)))
        gain = gain * jnp.repeat(draws, extent[dim] // blocks).reshape([-1 if axis == dim else 1 for axis in range(len(extent))])
    return gain


def deal_out(key, own, number, rows, count, top, limit, slope):
    order = jax.random.permutation(key, count)
    crowded, common = shares(count, rows * top, limit, slope, True), shares(count, rows * top, limit, slope, False)
    places = jnp.arange(count)

    def named(tallies, offset_by):
        used = int((tallies > 0).sum())
        fixed = max(1, used // 4)
        passed = fixed + (places - fixed + offset_by * (used - fixed)) % max(1, count - fixed)
        return jnp.zeros((count,), jnp.int32).at[order[jnp.where(places < fixed, places, passed)]].set(jnp.asarray(tallies, jnp.int32))

    tallies = jnp.where(number % 4 == 0, named(crowded, number // 4), named(common, number - number // 4 - 1))
    mixed = jax.random.permutation(jax.random.fold_in(own, 3), count)
    giver, receiver = mixed[0:count // 2 * 2:2], mixed[1:count // 2 * 2:2]
    room = jnp.minimum(tallies[giver] - 1, limit - tallies[receiver]) // 2
    room = jnp.where((giver == order[0]) | (receiver == order[0]) | (tallies[receiver] == 0), 0, jnp.maximum(room, 0))
    passed = jax.random.randint(jax.random.fold_in(own, 4), (count // 2,), 0, 1 << 20) % (room + 1)
    tallies = tallies.at[giver].add(-passed).at[receiver].add(passed)
    members = jnp.searchsorted(jnp.cumsum(tallies), jnp.arange(rows * top), side="right").astype(jnp.int32)
    table = members.reshape(top, rows).T
    table = table[jax.random.permutation(jax.random.fold_in(own, 1), rows)]
    offset_by = jax.random.randint(jax.random.fold_in(own, 2), (rows, 1), 0, top)
    return jnp.take_along_axis(table, (jnp.arange(top)[None, :] + offset_by) % top, axis=1)


def shares(amount, total, most, lean, full):
    portions = [(1 << 20) // math.isqrt(standing ** lean) + 1 for standing in range(1, amount + 1)]
    largest = most if full else min(most, max(-(-total // amount), total * portions[0] // sum(portions)))
    least = 1 if total - largest >= amount - 1 else 0
    given, surplus = [largest] + [least] * (amount - 1), total - largest - least * (amount - 1)
    while surplus > 0:
        movable = [i for i in range(1, amount) if given[i] < largest] or [i for i in range(1, amount) if given[i] < most]
        mass, left = sum([portions[i] for i in movable]), surplus
        for i in movable:
            addition = min(most - given[i], max(1, left * portions[i] // mass), surplus)
            given[i] = given[i] + addition
            surplus = surplus - addition
    return np.array(given)


def bell_draw(own_key, dims, scale, most, split=(), dtype=jnp.bfloat16):
    entries = scale * jax.random.normal(own_key, dims, jnp.float32)
    if split:
        entries = entries * levels(own_key, dims, split, -0.22, 0.18)
    return jnp.clip(entries, -most, most).astype(dtype)


def setup_inputs(seed: int = 0) -> dict:
    key_list = jax.random.split(jax.random.key(seed), 11)
    initial = bell_draw(key_list[0], (TR, LEV, NLAT, NLON), 1.0, 6.0, ((2, 8), (3, 16)), jnp.float32)
    east_wind = jnp.clip(jax.random.uniform(key_list[1], (STEPS, LEV, NLAT, NLON), jnp.float32, -0.3, 0.3) * levels(key_list[1], (STEPS, LEV, NLAT, NLON), ((2, 8), (3, 16)), -0.4, 0.0), -0.3, 0.3)
    north_wind = jnp.clip(jax.random.uniform(key_list[2], (STEPS, LEV, NLAT, NLON), jnp.float32, -0.3, 0.3) * levels(key_list[2], (STEPS, LEV, NLAT, NLON), ((2, 8), (3, 16)), -0.4, 0.0), -0.3, 0.3)
    mixing = jnp.clip(0.02 + 0.18 * jax.random.uniform(key_list[3], (STEPS, LEV, NLAT, NLON), jnp.float32) ** levels(key_list[3], (STEPS, LEV, NLAT, NLON), ((2, 8), (3, 16)), -0.2, 0.2), 0.02, 0.2)
    kernel = bell_draw(key_list[4], (BLOCKS, LEV, S), LEV ** -0.5, 0.75, ((0, 128),))
    columns = with_ends(jax.random.randint(key_list[5], (BLOCKS, S), 0, TR * CLAT * CLON), jax.random.fold_in(key_list[5], 1), 0, (TR * CLAT * CLON) - 1).astype(jnp.int32)
    observed = bell_draw(key_list[6], (BLOCKS, S), 1.0, 6.0, ((0, 128),))
    obs_weight = jnp.clip(jnp.exp(math.log(8.0) - 2.0794415 * jax.random.uniform(key_list[7], (BLOCKS, S), jnp.float32) ** levels(key_list[7], (BLOCKS, S), ((0, 128),), -0.2, 0.2)), 1.0, 8.0).astype(jnp.bfloat16)
    counts = with_ends(jax.random.randint(key_list[8], (BLOCKS,), S // 2, S + 1), jax.random.fold_in(key_list[8], 1), S // 2, S).astype(jnp.int32)
    targets_keys = jax.random.split(jax.random.fold_in(key_list[9], 1), BLOCKS // BLK_DEV)
    targets_turns = jax.random.permutation(jax.random.fold_in(key_list[9], 3), BLOCKS // BLK_DEV)
    targets = jax.vmap(lambda own, number: deal_out(jax.random.fold_in(key_list[9], 2), own, number, BLK_DEV, DEVICES, 1, CAP, 2))(targets_keys, targets_turns).reshape((BLOCKS, 1))
    return dict(initial=initial, east_wind=east_wind, north_wind=north_wind, mixing=mixing, kernel=kernel, columns=columns, observed=observed, obs_weight=obs_weight, counts=counts, targets=targets)


def pad_global(field):
    rows_pad = jnp.pad(field, ((0, 0), (0, 0), (1, 1), (0, 0)))
    return jnp.concatenate([rows_pad[..., -1:], rows_pad, rows_pad[..., :1]], axis=-1)


def vertical_mix(field, coeff):
    above_cells = jnp.concatenate([field[:, 1:], jnp.zeros_like(field[:, :1])], axis=1)
    upward = coeff * (above_cells - field)
    below_flux = jnp.concatenate([jnp.zeros_like(upward[:, :1]), upward[:, :-1]], axis=1)
    return upward - below_flux


def forward_step(padded, east_pos, east_neg, north_pos, north_neg, coeff):
    interior = padded[:, :, 1:-1, 1:-1]
    zonal_flux = east_pos[:, 1:-1, :-1] * padded[:, :, 1:-1, :-1] + east_neg[:, 1:-1, :-1] * padded[:, :, 1:-1, 1:]
    merid_flux = north_pos[:, :-1, 1:-1] * padded[:, :, :-1, 1:-1] + north_neg[:, :-1, 1:-1] * padded[:, :, 1:, 1:-1]
    return (interior - (zonal_flux[..., 1:] - zonal_flux[..., :-1])
            - (merid_flux[:, :, 1:] - merid_flux[:, :, :-1]) + vertical_mix(interior, coeff))


def adjoint_step(padded, east_pos, east_neg, north_pos, north_neg, coeff):
    interior = padded[:, :, 1:-1, 1:-1]
    zonal_term = (east_pos[:, 1:-1, 1:-1] * (padded[:, :, 1:-1, 2:] - interior)
                  + east_neg[:, 1:-1, :-2] * (interior - padded[:, :, 1:-1, :-2]))
    merid_term = (north_pos[:, 1:-1, 1:-1] * (padded[:, :, 2:, 1:-1] - interior)
                  + north_neg[:, :-2, 1:-1] * (interior - padded[:, :, :-2, 1:-1]))
    return interior + zonal_term + merid_term + vertical_mix(interior, coeff)


def reference(initial, east_wind, north_wind, mixing, kernel, columns, observed, obs_weight, counts, targets):
    row_index = lax.broadcasted_iota(jnp.int32, (1, 1, NLAT, 1), 2)
    north_masked = jnp.where(row_index < NLAT - 1, north_wind, jnp.float32(0.0))
    level_index = lax.broadcasted_iota(jnp.int32, (1, LEV, 1, 1), 1)
    coeff_all = jnp.where(level_index < LEV - 1, mixing, jnp.float32(0.0))
    winds = pad_global(jnp.concatenate([east_wind, north_masked], axis=0))
    east_pos = jnp.maximum(winds[:STEPS], 0.0)
    east_neg = jnp.minimum(winds[:STEPS], 0.0)
    north_pos = jnp.maximum(winds[STEPS:], 0.0)
    north_neg = jnp.minimum(winds[STEPS:], 0.0)
    state = initial
    for moment in range(STEPS):
        state = forward_step(pad_global(state), east_pos[moment], east_neg[moment],
                             north_pos[moment], north_neg[moment], coeff_all[moment])
    cells = CLAT * CLON
    target_dev = targets[:, 0]
    lat_dev = target_dev // N_LON
    lon_dev = target_dev % N_LON
    tracer_of = columns // cells
    local_pos = columns % cells
    grid_row = lat_dev[:, None] * CLAT + local_pos // CLON
    grid_col = lon_dev[:, None] * CLON + local_pos % CLON
    flat_index = (tracer_of * (NLAT * NLON) + grid_row * NLON + grid_col).astype(jnp.int32).reshape(-1)
    flat_field = jnp.transpose(state, (1, 0, 2, 3)).reshape(LEV, TR * NLAT * NLON)
    profile = jnp.take(flat_field, flat_index, axis=1).reshape(LEV, BLOCKS, S)
    kernel_wide = kernel.astype(jnp.float32)
    model = jnp.sum(kernel_wide * jnp.swapaxes(profile, 0, 1), axis=1)
    misfit = model - observed.astype(jnp.float32)
    live = lax.broadcasted_iota(jnp.int32, (1, S), 1) < counts[:, None]
    innovations = jnp.where(live, misfit, jnp.float32(0.0))
    forcing = obs_weight.astype(jnp.float32) * innovations
    vectors = jnp.swapaxes(kernel_wide * forcing[:, None, :], 0, 1).reshape(LEV, BLOCKS * S)
    adjoint_flat = jnp.zeros((LEV, TR * NLAT * NLON), jnp.float32).at[:, flat_index].add(vectors)
    adjoint_state = jnp.transpose(adjoint_flat.reshape(LEV, TR, NLAT, NLON), (1, 0, 2, 3))
    for moment in range(STEPS - 1, -1, -1):
        adjoint_state = adjoint_step(pad_global(adjoint_state), east_pos[moment], east_neg[moment],
                                     north_pos[moment], north_neg[moment], coeff_all[moment])
    return adjoint_state, innovations
```

```python
import functools

import jax
import jax.numpy as jnp
from jax import lax
from jax.experimental import pallas as pl
from jax.experimental.pallas import tpu as pltpu
from jax.sharding import PartitionSpec as P

CAP = 2
LEVELS = 72
ROWS = 80
PAIR = 2 * LEVELS
TRACERS = 3
LAT_CELLS = 8
LANES = 128
VMEM_LIMIT = 48 << 20


def lane_index():
    return lax.broadcasted_iota(jnp.int32, (LEVELS, LANES), 1)


def rolled(array, shift, axis):
    shift = shift % array.shape[axis]
    return pltpu.roll(array, shift, axis) if shift else array


def west_of(slab, halo, place):
    return jnp.where(lane_index() == 0, rolled(halo, -place, 1), rolled(slab, 1, 1))


def east_of(slab, halo, place):
    return jnp.where(
        lane_index() == LANES - 1, rolled(halo, LANES - 1 - place, 1), rolled(slab, -1, 1)
    )


def packed_columns(slabs, lane):
    packed = jnp.zeros((LEVELS, LANES), jnp.float32)
    for place, slab in enumerate(slabs):
        packed = jnp.where(lane_index() == place, rolled(slab, place - lane, 1), packed)
    return packed


def mixed(slab, coeff):
    upward = coeff * (rolled(slab, -1, 0) - slab)
    return upward - rolled(upward, 1, 0)


def write_edges(read, north_edge, south_edge, east_edge, west_edge):
    slabs = [read(t, row) for t in range(TRACERS) for row in range(LAT_CELLS)]
    for t in range(TRACERS):
        north_edge[t] = slabs[t * LAT_CELLS + LAT_CELLS - 1]
        south_edge[t] = slabs[t * LAT_CELLS]
    east_edge[...] = packed_columns(slabs, LANES - 1)
    west_edge[...] = packed_columns(slabs, 0)


def prepare_body(
    last_ref, initial_ref, east_ref, north_ref, mixing_ref,
    state_ref, east_out, north_out, mixing_out, north_edge, south_edge, east_edge, west_edge,
):
    steps = east_ref.shape[0]
    top = lax.broadcasted_iota(jnp.int32, (LEVELS, LANES), 0) == LEVELS - 1
    for t in range(TRACERS):
        for row in range(LAT_CELLS):
            state_ref[t, row] = initial_ref[t, :, row, :]
    for m in range(steps):
        for row in range(LAT_CELLS):
            east_out[m, row] = east_ref[m, :, row, :]
            north = north_ref[m, :, row, :]
            if row == LAT_CELLS - 1:
                north = jnp.where(last_ref[0] > 0, jnp.float32(0.0), north)
            north_out[m, row] = north
            mixing_out[m, row] = jnp.where(top, jnp.float32(0.0), mixing_ref[m, :, row, :])
    for t in range(TRACERS):
        north_edge[t] = state_ref[t, LAT_CELLS - 1]
        south_edge[t] = state_ref[t, 0]
    for m in range(steps):
        north_edge[TRACERS + m] = north_out[m, LAT_CELLS - 1]
    slabs = [state_ref[t, row] for t in range(TRACERS) for row in range(LAT_CELLS)]
    winds = [east_out[m, row] for m in range(steps) for row in range(LAT_CELLS)]
    east_edge[...] = packed_columns(slabs + winds, LANES - 1)
    west_edge[...] = packed_columns(slabs, 0)


def wind_west(east, east_halo, m, row):
    return west_of(east, east_halo, TRACERS * LAT_CELLS + m * LAT_CELLS + row)


def forward_slabs(m, state_ref, east_ref, north_ref, mixing_ref, halos, winds):
    from_south, from_north, from_west, from_east = halos
    wind_south, wind_column = winds
    for row in range(LAT_CELLS):
        east = east_ref[m, row]
        before = wind_west(east, wind_column[...], m, row)
        north = north_ref[m, row]
        south = north_ref[m, row - 1] if row else wind_south[TRACERS + m]
        coeff = mixing_ref[m, row]
        for t in range(TRACERS):
            place = t * LAT_CELLS + row
            slab = state_ref[t, row]
            left = west_of(slab, from_west[...], place)
            right = east_of(slab, from_east[...], place)
            above = state_ref[t, row + 1] if row < LAT_CELLS - 1 else from_north[t]
            below = state_ref[t, row - 1] if row else from_south[t]
            zonal = jnp.maximum(east, 0.0) * slab + jnp.minimum(east, 0.0) * right
            zonal_before = jnp.maximum(before, 0.0) * left + jnp.minimum(before, 0.0) * slab
            merid = jnp.maximum(north, 0.0) * slab + jnp.minimum(north, 0.0) * above
            merid_before = jnp.maximum(south, 0.0) * below + jnp.minimum(south, 0.0) * slab
            yield t, row, slab - (zonal - zonal_before) - (merid - merid_before) + mixed(
                slab, coeff
            )


def adjoint_slabs(m, read, east_ref, north_ref, mixing_ref, halos, winds):
    from_south, from_north, from_west, from_east = halos
    wind_south, wind_column = winds
    for row in range(LAT_CELLS):
        east = jnp.maximum(east_ref[m, row], 0.0)
        before = jnp.minimum(wind_west(east_ref[m, row], wind_column[...], m, row), 0.0)
        north = jnp.maximum(north_ref[m, row], 0.0)
        south = jnp.minimum(north_ref[m, row - 1] if row else wind_south[TRACERS + m], 0.0)
        coeff = mixing_ref[m, row]
        for t in range(TRACERS):
            place = t * LAT_CELLS + row
            slab = read(t, row)
            left = west_of(slab, from_west[...], place)
            right = east_of(slab, from_east[...], place)
            above = read(t, row + 1) if row < LAT_CELLS - 1 else from_north[t]
            below = read(t, row - 1) if row else from_south[t]
            yield t, row, (
                slab
                + (east * (right - slab) + before * (slab - left))
                + (north * (above - slab) + south * (slab - below))
                + mixed(slab, coeff)
            )


def forward_first_body(
    state_ref, east_ref, north_ref, mixing_ref, s, n, w, e, out_ref, *edges
):
    for t, row, slab in forward_slabs(
        0, state_ref, east_ref, north_ref, mixing_ref, (s, n, w, e), (s, w)
    ):
        out_ref[t, row] = slab
    write_edges(lambda t, row: out_ref[t, row], *edges)


def forward_last_body(
    state_ref, east_ref, north_ref, mixing_ref, s, n, w, e, wind_s, wind_w, field_ref, after_ref
):
    for t, row, slab in forward_slabs(
        1, state_ref, east_ref, north_ref, mixing_ref, (s, n, w, e), (wind_s, wind_w)
    ):
        after_ref[t, row] = slab
    for i in range(6):
        for low_row in range(2):
            slabs = []
            for p in (2 * i, 2 * i + 1):
                slabs.append(after_ref[p // 4, (p % 4) * 2 + low_row])
            both = jnp.concatenate(slabs, axis=0)
            high = both.astype(jnp.bfloat16)
            low = (both - high.astype(jnp.float32)).astype(jnp.bfloat16)
            rows = slice(i * PAIR, (i + 1) * PAIR)
            field_ref[rows, low_row * LANES : (low_row + 1) * LANES] = high
            field_ref[rows, (2 + low_row) * LANES : (3 + low_row) * LANES] = low


def cell_slab(ref, t, row):
    first = (t * 4 + row // 2) * LEVELS
    return ref[first : first + LEVELS, (row % 2) * LANES : (row % 2 + 1) * LANES]


def adjoint_first_body(
    adjoint_ref, east_ref, north_ref, mixing_ref, s, n, w, e, wind_s, wind_w, out_ref, *edges
):
    for t, row, slab in adjoint_slabs(
        1,
        lambda t, row: cell_slab(adjoint_ref, t, row),
        east_ref, north_ref, mixing_ref, (s, n, w, e), (wind_s, wind_w),
    ):
        out_ref[t, row] = slab
    write_edges(lambda t, row: out_ref[t, row], *edges)


def adjoint_last_body(
    state_ref, east_ref, north_ref, mixing_ref, s, n, w, e, wind_s, wind_w, out_ref
):
    for t, row, slab in adjoint_slabs(
        0,
        lambda t, row: state_ref[t, row],
        east_ref, north_ref, mixing_ref, (s, n, w, e), (wind_s, wind_w),
    ):
        out_ref[t, :, row, :] = slab


STATE = jax.ShapeDtypeStruct((TRACERS, LAT_CELLS, LEVELS, LANES), jnp.float32)
ROW_EDGE = jax.ShapeDtypeStruct((TRACERS, LEVELS, LANES), jnp.float32)
COLUMN_EDGE = jax.ShapeDtypeStruct((LEVELS, LANES), jnp.float32)
EDGES = [ROW_EDGE, ROW_EDGE, COLUMN_EDGE, COLUMN_EDGE]


def whole(body, outs, operands, name, scratch=(), scalars=0):
    vmem = pl.BlockSpec(memory_space=pltpu.VMEM)
    smem = pl.BlockSpec(memory_space=pltpu.SMEM)
    return pl.pallas_call(
        body,
        in_specs=[smem if i < scalars else vmem for i in range(len(operands))],
        out_specs=jax.tree.map(lambda _: vmem, outs),
        out_shape=outs,
        scratch_shapes=list(scratch),
        compiler_params=pltpu.CompilerParams(vmem_limit_bytes=VMEM_LIMIT),
        cost_estimate=pl.CostEstimate(flops=5000000, bytes_accessed=6000000, transcendentals=0),
        name=name,
    )(*operands)


def exchange_edges(edges):
    north_edge, south_edge, east_edge, west_edge = edges
    lat, lon = lax.axis_size("lat"), lax.axis_size("lon")
    up = [(i, i + 1) for i in range(lat - 1)]
    right = [(i, (i + 1) % lon) for i in range(lon)]
    return (
        lax.ppermute(north_edge, "lat", up),
        lax.ppermute(south_edge, "lat", [(j, i) for i, j in up]),
        lax.ppermute(east_edge, "lon", right),
        lax.ppermute(west_edge, "lon", [(j, i) for i, j in right]),
    )


def pack_body(source_ref, kernel_ref, meta_ref, out_ref):
    def one(slot, carry):
        source = source_ref[slot]
        block = jnp.maximum(source, 0)
        meta = jnp.where(source >= 0, meta_ref[block].astype(jnp.float32), jnp.float32(0.0))
        rows = jnp.concatenate([kernel_ref[block].astype(jnp.float32), meta], axis=0)
        out_ref[slot] = rows.astype(jnp.bfloat16)
        return carry

    lax.fori_loop(0, out_ref.shape[0], one, 0, unroll=4)


def pack_blocks(source, kernel, meta):
    count, _, sounds = kernel.shape
    vmem = pl.BlockSpec(memory_space=pltpu.VMEM)
    return pl.pallas_call(
        pack_body,
        in_specs=[pl.BlockSpec(memory_space=pltpu.SMEM), vmem, vmem],
        out_specs=vmem,
        out_shape=jax.ShapeDtypeStruct((count, ROWS, sounds), jnp.bfloat16),
        compiler_params=pltpu.CompilerParams(vmem_limit_bytes=VMEM_LIMIT),
        name="pack_blocks",
    )(source, kernel, meta)


def first_soundings_body(per_step, width, field_ref, block_ref, adjoint_ref, misfit_ref):
    @pl.when(pl.program_id(0) == 0)
    def _():
        adjoint_ref[...] = jnp.zeros_like(adjoint_ref)

    def write_misfit(block, row):
        misfit_ref[block : block + 1, :] = row

    soundings(per_step, width, field_ref, block_ref, adjoint_ref, write_misfit)


def second_soundings_body(
    per_step, width, field_ref, block_ref, earlier_ref, other_ref, adjoint_ref, misfit_ref, *edges
):
    @pl.when(pl.program_id(0) == 0)
    def _():
        adjoint_ref[...] = earlier_ref[...]

    def write_misfit(block, row):
        misfit_ref[2 * block : 2 * block + 1, :] = other_ref[block : block + 1, :]
        misfit_ref[2 * block + 1 : 2 * block + 2, :] = row

    soundings(per_step, width, field_ref, block_ref, adjoint_ref, write_misfit)

    @pl.when(pl.program_id(0) == pl.num_programs(0) - 1)
    def _():
        write_edges(lambda t, row: cell_slab(adjoint_ref, t, row), *edges)


def soundings(per_step, width, field_ref, block_ref, adjoint_ref, write_misfit):

    n = width * 128
    for group in range(per_step // width):
        first = group * width
        blocks = [block_ref[first + i] for i in range(width)]
        profile = jnp.concatenate([b[:LEVELS] for b in blocks], axis=1)
        meta = jnp.concatenate([b[LEVELS:] for b in blocks], axis=1).astype(jnp.float32)
        part, cell, observed, weight = (meta[j : j + 1] for j in range(4))
        hit = lax.broadcasted_iota(jnp.int32, (256, n), 0).astype(jnp.float32) == cell
        pick = jnp.where(hit, 1.0, 0.0).astype(jnp.bfloat16)
        pick_twice = jnp.concatenate([pick, pick], axis=0)
        column = jnp.zeros((LEVELS, n), jnp.float32)
        for i in range(6):
            found = jnp.dot(
                field_ref[i * PAIR : (i + 1) * PAIR, :],
                pick_twice,
                preferred_element_type=jnp.float32,
            )
            column = jnp.where(part == 2.0 * i, found[:LEVELS], column)
            column = jnp.where(part == 2.0 * i + 1.0, found[LEVELS:], column)
        model = jnp.sum(profile.astype(jnp.float32) * column, axis=0, keepdims=True)
        misfit = model - observed
        for i in range(width):
            write_misfit(first + i, misfit[:, i * 128 : (i + 1) * 128])
        forcing = weight * misfit
        high = forcing.astype(jnp.bfloat16).astype(jnp.float32)
        low = forcing - high
        spread = jnp.concatenate(
            [
                jnp.where(hit, high, 0.0).astype(jnp.bfloat16),
                jnp.where(hit, low, 0.0).astype(jnp.bfloat16),
            ],
            axis=1,
        )
        twice = jnp.concatenate([profile, profile], axis=0)
        second = lax.broadcasted_iota(jnp.int32, (PAIR, n), 0) >= LEVELS
        part_row = (part - jnp.where(second, 1.0, 0.0)).astype(jnp.bfloat16)
        for i in range(6):
            left = jnp.where(part_row == jnp.bfloat16(2 * i), twice, jnp.bfloat16(0))
            adjoint_ref[i * PAIR : (i + 1) * PAIR, :] += lax.dot_general(
                jnp.concatenate([left, left], axis=1),
                spread,
                (((1,), (1,)), ((), ())),
                preferred_element_type=jnp.float32,
            )


def observe(field, blocks, earlier=None):
    count = blocks.shape[0]
    per_step, width = 16, 4

    def fixed(shape):
        return pl.BlockSpec(shape, lambda i: (0,) * len(shape))

    def rows(height):
        return pl.BlockSpec((height, 128), lambda i: (i, 0))

    cells = (12 * LEVELS, 256)
    in_specs = [
        fixed((12 * LEVELS, 512)),
        pl.BlockSpec((per_step, ROWS, 128), lambda i: (i, 0, 0)),
    ]
    first = earlier is None
    outs = [jax.ShapeDtypeStruct(cells, jnp.float32)]
    if first:
        body, operands = first_soundings_body, (field, blocks)
        out_specs = [fixed(cells), rows(per_step)]
        outs += [jax.ShapeDtypeStruct((count, 128), jnp.float32)]
    else:
        body, operands = second_soundings_body, (field, blocks) + tuple(earlier)
        in_specs += [fixed(cells), rows(per_step)]
        out_specs = [fixed(cells), rows(2 * per_step)] + [fixed(edge.shape) for edge in EDGES]
        outs += [jax.ShapeDtypeStruct((2 * count, 128), jnp.float32)] + EDGES
    return pl.pallas_call(
        functools.partial(body, per_step, width),
        grid=(count // per_step,),
        in_specs=in_specs,
        out_specs=out_specs,
        out_shape=outs,
        compiler_params=pltpu.CompilerParams(vmem_limit_bytes=VMEM_LIMIT),
        cost_estimate=pl.CostEstimate(
            flops=count * 4 * 864 * 512 * 128, bytes_accessed=count * 40960, transcendentals=0
        ),
        name="first_soundings" if first else "second_soundings",
    )(*operands)


def per_device(
    initial, east_wind, north_wind, mixing, kernel, columns, observed, obs_weight, counts, targets
):
    lat_count = lax.axis_size("lat")
    lon_count = lax.axis_size("lon")
    sounds = kernel.shape[2]
    target_dev = targets[:, 0]
    block_count = target_dev.shape[0]
    device_count = lat_count * lon_count
    block_id = lax.broadcasted_iota(jnp.int32, (block_count, device_count), 0)
    meant = target_dev[:, None] == lax.broadcasted_iota(
        jnp.int32, (block_count, device_count), 1
    )
    source_first = jnp.min(jnp.where(meant, block_id, block_count), axis=0)
    source_last = jnp.max(jnp.where(meant, block_id, -1), axis=0)
    source_first = jnp.where(source_last >= 0, source_first, -1)
    source_second = jnp.where(source_last > source_first, source_last, -1)
    is_second = jnp.max(jnp.where(meant & (block_id != source_first[None, :]), 1, 0), axis=1)
    slot_index = target_dev * CAP + is_second
    live = lax.broadcasted_iota(jnp.int32, (1, sounds), 1) < counts[:, None]
    weight_live = jnp.where(live, obs_weight, jnp.zeros_like(obs_weight))
    zeros = jnp.zeros_like(obs_weight)
    meta = jnp.stack(
        [(columns // 256).astype(jnp.bfloat16), (columns % 256).astype(jnp.bfloat16)]
        + [observed, weight_live, zeros, zeros, zeros, zeros],
        axis=1,
    )

    def exchange(array):
        return lax.all_to_all(array, ("lat", "lon"), split_axis=0, concat_axis=0, tiled=True)

    got_first = exchange(pack_blocks(source_first, kernel, meta))
    got_second = exchange(pack_blocks(source_second, kernel, meta))

    is_last = (lax.axis_index("lat") == lat_count - 1).astype(jnp.int32).reshape(1)
    winds_like = jax.ShapeDtypeStruct((2, LAT_CELLS, LEVELS, LANES), jnp.float32)
    tall_edge = jax.ShapeDtypeStruct((TRACERS + 2, LEVELS, LANES), jnp.float32)
    prepared = whole(
        prepare_body,
        [STATE, winds_like, winds_like, winds_like, tall_edge] + EDGES[1:],
        (is_last, initial, east_wind, north_wind, mixing),
        "prepare",
        scalars=1,
    )
    state, fields, edges = prepared[0], tuple(prepared[1:4]), prepared[4:]
    halos = exchange_edges(edges)
    winds = (halos[0], halos[2])
    middle, *edges = whole(
        forward_first_body, [STATE] + EDGES, (state,) + fields + halos, "forward_first"
    )
    field = whole(
        forward_last_body,
        jax.ShapeDtypeStruct((12 * LEVELS, 512), jnp.bfloat16),
        (middle,) + fields + exchange_edges(edges) + winds,
        "forward_last",
        scratch=[pltpu.VMEM(STATE.shape, jnp.float32)],
    )
    earlier = observe(field, got_first)
    adjoint, misfit, *edges = observe(field, got_second, earlier)
    halos = exchange_edges(edges)
    returned = exchange(misfit)
    middle, *edges = whole(
        adjoint_first_body, [STATE] + EDGES, (adjoint,) + fields + halos + winds, "adjoint_first"
    )
    gradient = whole(
        adjoint_last_body,
        jax.ShapeDtypeStruct(initial.shape, jnp.float32),
        (middle,) + fields + exchange_edges(edges) + winds,
        "adjoint_last",
    )
    innovations = jnp.where(live, returned[slot_index], jnp.float32(0.0))
    return (gradient, innovations)


def solution(mesh):
    return jax.shard_map(
        per_device,
        mesh=mesh,
        in_specs=(
            P(None, None, "lat", "lon"),
            P(None, None, "lat", "lon"),
            P(None, None, "lat", "lon"),
            P(None, None, "lat", "lon"),
            P(("lat", "lon"), None, None),
            P(("lat", "lon"), None),
            P(("lat", "lon"), None),
            P(("lat", "lon"), None),
            P(("lat", "lon")),
            P(("lat", "lon"), None),
        ),
        out_specs=(P(None, None, "lat", "lon"), P(("lat", "lon"), None)),
        check_vma=False,
    )
```

```python
import functools

import jax
import jax.numpy as jnp
from jax import lax
from jax.experimental import pallas as pl
from jax.experimental.pallas import tpu as pltpu
from jax.sharding import PartitionSpec as P

LEVELS = 72
ROWS = 80
PAIR = 2 * LEVELS
TRACERS = 3
PARTS = 12
GROUPS = 6
GROUP_PARTS = PARTS // GROUPS
WIDTH = 2
LAT_CELLS = 8
LANES = 128
VMEM_LIMIT = 48 << 20


def lane_index():
    return lax.broadcasted_iota(jnp.int32, (LEVELS, LANES), 1)


def rolled(array, shift, axis):
    shift = shift % array.shape[axis]
    return pltpu.roll(array, shift, axis) if shift else array


def west_of(slab, halo, place):
    return jnp.where(lane_index() == 0, rolled(halo, -place, 1), rolled(slab, 1, 1))


def east_of(slab, halo, place):
    return jnp.where(
        lane_index() == LANES - 1, rolled(halo, LANES - 1 - place, 1), rolled(slab, -1, 1)
    )


def packed_columns(slabs, lane):
    packed = jnp.zeros((LEVELS, LANES), jnp.float32)
    for place, slab in enumerate(slabs):
        packed = jnp.where(lane_index() == place, rolled(slab, place - lane, 1), packed)
    return packed


def mixed(slab, coeff):
    upward = coeff * (rolled(slab, -1, 0) - slab)
    return upward - rolled(upward, 1, 0)


def write_edges(read, north_edge, south_edge, east_edge, west_edge):
    slabs = [read(t, row) for t in range(TRACERS) for row in range(LAT_CELLS)]
    for t in range(TRACERS):
        north_edge[t] = slabs[t * LAT_CELLS + LAT_CELLS - 1]
        south_edge[t] = slabs[t * LAT_CELLS]
    east_edge[...] = packed_columns(slabs, LANES - 1)
    west_edge[...] = packed_columns(slabs, 0)


def prepare_body(
    last_ref, initial_ref, east_ref, north_ref, mixing_ref,
    state_ref, east_out, north_out, mixing_out, north_edge, south_edge, east_edge, west_edge,
):
    steps = east_ref.shape[0]
    top = lax.broadcasted_iota(jnp.int32, (LEVELS, LANES), 0) == LEVELS - 1
    for t in range(TRACERS):
        for row in range(LAT_CELLS):
            state_ref[t, row] = initial_ref[t, :, row, :]
    for m in range(steps):
        for row in range(LAT_CELLS):
            east_out[m, row] = east_ref[m, :, row, :]
            north = north_ref[m, :, row, :]
            if row == LAT_CELLS - 1:
                north = jnp.where(last_ref[0] > 0, jnp.float32(0.0), north)
            north_out[m, row] = north
            mixing_out[m, row] = jnp.where(top, jnp.float32(0.0), mixing_ref[m, :, row, :])
    for t in range(TRACERS):
        north_edge[t] = state_ref[t, LAT_CELLS - 1]
        south_edge[t] = state_ref[t, 0]
    for m in range(steps):
        north_edge[TRACERS + m] = north_out[m, LAT_CELLS - 1]
    slabs = [state_ref[t, row] for t in range(TRACERS) for row in range(LAT_CELLS)]
    winds = [east_out[m, row] for m in range(steps) for row in range(LAT_CELLS)]
    east_edge[...] = packed_columns(slabs + winds, LANES - 1)
    west_edge[...] = packed_columns(slabs, 0)


def wind_west(east, east_halo, m, row):
    return west_of(east, east_halo, TRACERS * LAT_CELLS + m * LAT_CELLS + row)


def forward_slabs(m, state_ref, east_ref, north_ref, mixing_ref, halos, winds):
    from_south, from_north, from_west, from_east = halos
    wind_south, wind_column = winds
    for row in range(LAT_CELLS):
        east = east_ref[m, row]
        before = wind_west(east, wind_column[...], m, row)
        north = north_ref[m, row]
        south = north_ref[m, row - 1] if row else wind_south[TRACERS + m]
        coeff = mixing_ref[m, row]
        for t in range(TRACERS):
            place = t * LAT_CELLS + row
            slab = state_ref[t, row]
            left = west_of(slab, from_west[...], place)
            right = east_of(slab, from_east[...], place)
            above = state_ref[t, row + 1] if row < LAT_CELLS - 1 else from_north[t]
            below = state_ref[t, row - 1] if row else from_south[t]
            zonal = jnp.maximum(east, 0.0) * slab + jnp.minimum(east, 0.0) * right
            zonal_before = jnp.maximum(before, 0.0) * left + jnp.minimum(before, 0.0) * slab
            merid = jnp.maximum(north, 0.0) * slab + jnp.minimum(north, 0.0) * above
            merid_before = jnp.maximum(south, 0.0) * below + jnp.minimum(south, 0.0) * slab
            yield t, row, slab - (zonal - zonal_before) - (merid - merid_before) + mixed(
                slab, coeff
            )


def adjoint_slabs(m, read, east_ref, north_ref, mixing_ref, halos, winds):
    from_south, from_north, from_west, from_east = halos
    wind_south, wind_column = winds
    for row in range(LAT_CELLS):
        east = jnp.maximum(east_ref[m, row], 0.0)
        before = jnp.minimum(wind_west(east_ref[m, row], wind_column[...], m, row), 0.0)
        north = jnp.maximum(north_ref[m, row], 0.0)
        south = jnp.minimum(north_ref[m, row - 1] if row else wind_south[TRACERS + m], 0.0)
        coeff = mixing_ref[m, row]
        for t in range(TRACERS):
            place = t * LAT_CELLS + row
            slab = read(t, row)
            left = west_of(slab, from_west[...], place)
            right = east_of(slab, from_east[...], place)
            above = read(t, row + 1) if row < LAT_CELLS - 1 else from_north[t]
            below = read(t, row - 1) if row else from_south[t]
            yield t, row, (
                slab
                + (east * (right - slab) + before * (slab - left))
                + (north * (above - slab) + south * (slab - below))
                + mixed(slab, coeff)
            )


def forward_first_body(
    state_ref, east_ref, north_ref, mixing_ref, s, n, w, e, out_ref, *edges
):
    for t, row, slab in forward_slabs(
        0, state_ref, east_ref, north_ref, mixing_ref, (s, n, w, e), (s, w)
    ):
        out_ref[t, row] = slab
    write_edges(lambda t, row: out_ref[t, row], *edges)


def forward_last_body(
    state_ref, east_ref, north_ref, mixing_ref, s, n, w, e, wind_s, wind_w, field_ref, after_ref
):
    for t, row, slab in forward_slabs(
        1, state_ref, east_ref, north_ref, mixing_ref, (s, n, w, e), (wind_s, wind_w)
    ):
        after_ref[t, row] = slab
    for i in range(6):
        for low_row in range(2):
            slabs = []
            for p in (2 * i, 2 * i + 1):
                slabs.append(after_ref[p // 4, (p % 4) * 2 + low_row])
            both = jnp.concatenate(slabs, axis=0)
            high = both.astype(jnp.bfloat16)
            low = (both - high.astype(jnp.float32)).astype(jnp.bfloat16)
            rows = slice(i * PAIR, (i + 1) * PAIR)
            field_ref[rows, low_row * LANES : (low_row + 1) * LANES] = high
            field_ref[rows, (2 + low_row) * LANES : (3 + low_row) * LANES] = low


def cell_slab(ref, t, row):
    first = (t * 4 + row // 2) * LEVELS
    return ref[first : first + LEVELS, (row % 2) * LANES : (row % 2 + 1) * LANES]


def adjoint_first_body(
    adjoint_ref, east_ref, north_ref, mixing_ref, s, n, w, e, wind_s, wind_w, out_ref, *edges
):
    for t, row, slab in adjoint_slabs(
        1,
        lambda t, row: cell_slab(adjoint_ref, t, row),
        east_ref, north_ref, mixing_ref, (s, n, w, e), (wind_s, wind_w),
    ):
        out_ref[t, row] = slab
    write_edges(lambda t, row: out_ref[t, row], *edges)


def adjoint_last_body(
    state_ref, east_ref, north_ref, mixing_ref, s, n, w, e, wind_s, wind_w, out_ref
):
    for t, row, slab in adjoint_slabs(
        0,
        lambda t, row: state_ref[t, row],
        east_ref, north_ref, mixing_ref, (s, n, w, e), (wind_s, wind_w),
    ):
        out_ref[t, :, row, :] = slab


STATE = jax.ShapeDtypeStruct((TRACERS, LAT_CELLS, LEVELS, LANES), jnp.float32)
ROW_EDGE = jax.ShapeDtypeStruct((TRACERS, LEVELS, LANES), jnp.float32)
COLUMN_EDGE = jax.ShapeDtypeStruct((LEVELS, LANES), jnp.float32)
EDGES = [ROW_EDGE, ROW_EDGE, COLUMN_EDGE, COLUMN_EDGE]


def whole(body, outs, operands, name, scratch=(), scalars=0, flops=5000000):
    vmem = pl.BlockSpec(memory_space=pltpu.VMEM)
    smem = pl.BlockSpec(memory_space=pltpu.SMEM)
    return pl.pallas_call(
        body,
        in_specs=[smem if i < scalars else vmem for i in range(len(operands))],
        out_specs=jax.tree.map(lambda _: vmem, outs),
        out_shape=outs,
        scratch_shapes=list(scratch),
        compiler_params=pltpu.CompilerParams(vmem_limit_bytes=VMEM_LIMIT),
        cost_estimate=pl.CostEstimate(flops=flops, bytes_accessed=6000000, transcendentals=0),
        name=name,
    )(*operands)


def exchange_edges(edges):
    north_edge, south_edge, east_edge, west_edge = edges
    lat, lon = lax.axis_size("lat"), lax.axis_size("lon")
    up = [(i, i + 1) for i in range(lat - 1)]
    right = [(i, (i + 1) % lon) for i in range(lon)]
    return (
        lax.ppermute(north_edge, "lat", up),
        lax.ppermute(south_edge, "lat", [(j, i) for i, j in up]),
        lax.ppermute(east_edge, "lon", right),
        lax.ppermute(west_edge, "lon", [(j, i) for i, j in right]),
    )


def pack_body(source_ref, kernel_ref, columns_ref, observed_ref, weight_ref, place_ref, out_ref):
    row_id = lax.broadcasted_iota(jnp.int32, (8, LANES), 0)
    to_place = lax.broadcasted_iota(jnp.int32, (LANES, LANES), 0).astype(jnp.float32)

    def one(slot, carry):
        source = source_ref[slot]
        block = jnp.maximum(source, 0)
        row = pl.ds(block, 1)
        cell = columns_ref[row, :]
        part = lax.shift_right_logical(cell, 8) + 1
        meta = jnp.where(row_id == 0, part.astype(jnp.float32), jnp.float32(0.0))
        meta = jnp.where(row_id == 1, (cell & 255).astype(jnp.float32), meta)
        meta = jnp.where(row_id == 2, observed_ref[row, :], meta)
        meta = jnp.where(row_id == 3, weight_ref[row, :], meta)
        rows = jnp.concatenate([kernel_ref[block].astype(jnp.float32), meta], axis=0)
        place = jnp.where(source >= 0, place_ref[row, :], LANES).astype(jnp.float32)
        moved = jnp.where(to_place == place, 1.0, 0.0).astype(jnp.bfloat16)
        out_ref[slot] = lax.dot_general(
            rows.astype(jnp.bfloat16),
            moved,
            (((1,), (1,)), ((), ())),
            preferred_element_type=jnp.float32,
        ).astype(jnp.bfloat16)
        return carry

    lax.fori_loop(0, out_ref.shape[0], one, 0, unroll=8)


def innovations_body(first_ref, second_ref, returned_ref, place_ref, out_ref, rows_ref):
    def one(device, carry):
        for rank, source_ref in enumerate((first_ref, second_ref)):
            source = source_ref[device]
            block = jnp.where(source >= 0, source, LANES)
            rows_ref[pl.ds(block, 1), :] = returned_ref[pl.ds(2 * device + rank, 1), :]
        return carry

    lax.fori_loop(0, first_ref.shape[0], one, 0, unroll=8)
    place = place_ref[...]
    live = place < LANES
    found = jnp.take_along_axis(
        rows_ref[: place.shape[0], :], jnp.where(live, place, 0), axis=1
    )
    out_ref[...] = jnp.where(live, found, jnp.float32(0.0))


def soundings(count_ref, field_ref, block_ref, adjoint_ref, write_misfit, stream_ref, found_ref, cell_ref):
    n = WIDTH * LANES
    one, nil = jnp.bfloat16(1), jnp.bfloat16(0)
    lane = lax.broadcasted_iota(jnp.int32, (ROWS, LANES), 1)
    cell_ref[...] = (
        lax.broadcasted_iota(jnp.int32, (256, LANES), 0).astype(jnp.float32).astype(jnp.bfloat16)
    )
    empty = jnp.zeros((ROWS, LANES), jnp.bfloat16)

    def merge(block, carry):
        ends, tails = list(carry[0]), list(carry[1])
        values = block_ref[block]
        start = jnp.int32(0)
        for g in range(GROUPS):
            count = count_ref[block * GROUPS + g]
            tile, at = lax.shift_right_logical(ends[g], 7), ends[g] & (LANES - 1)
            turned = pltpu.roll(values, (at - start) & (LANES - 1), 1)
            joined = jnp.where(lane >= at, turned, tails[g])
            stream_ref[g, tile] = joined
            tails[g] = jnp.where(at + count >= LANES, turned, joined)
            ends[g] = ends[g] + count
            start = start + count
        return tuple(ends), tuple(tails)

    ends, tails = lax.fori_loop(
        0,
        block_ref.shape[0],
        merge,
        ((jnp.int32(0),) * GROUPS, (empty,) * GROUPS),
        unroll=2,
    )
    for g in range(GROUPS):
        tile, at = lax.shift_right_logical(ends[g], 7), ends[g] & (LANES - 1)
        stream_ref[g, tile] = jnp.where(lane < at, tails[g], empty)
        for j in range(1, WIDTH):
            stream_ref[g, tile + j] = empty

    def load(g, step):
        tiles = [stream_ref[g, step * WIDTH + i] for i in range(WIDTH)]
        profile = jnp.concatenate([t[:LEVELS] for t in tiles], axis=1)
        meta = jnp.concatenate([t[LEVELS:] for t in tiles], axis=1).astype(jnp.float32)
        part, cell, observed, weight = (meta[j : j + 1] for j in range(4))
        cell = cell.astype(jnp.bfloat16)
        hits = [
            cell_ref[...] == jnp.broadcast_to(cell[:, i * LANES : (i + 1) * LANES], (256, LANES))
            for i in range(WIDTH)
        ]
        return g, step, profile, part - 1.0, observed, weight, hits

    def gather(g, step, profile, part, observed, weight, hits):
        pick = jnp.concatenate([jnp.where(hit, one, nil) for hit in hits], axis=1)
        pick_twice = jnp.concatenate([pick, pick], axis=0)
        column = jnp.zeros((LEVELS, n), jnp.float32)
        for i in range(g * GROUP_PARTS // 2, (g + 1) * GROUP_PARTS // 2):
            found = jnp.dot(
                field_ref[i * PAIR : (i + 1) * PAIR, :],
                pick_twice,
                preferred_element_type=jnp.float32,
            )
            column = jnp.where(part == 2.0 * i, found[:LEVELS], column)
            column = jnp.where(part == 2.0 * i + 1.0, found[LEVELS:], column)
        return column

    def force(column, g, step, profile, part, observed, weight, hits):
        model = jnp.sum(profile.astype(jnp.float32) * column, axis=0, keepdims=True)
        misfit = model - observed
        for i in range(WIDTH):
            found_ref[g, step * WIDTH + i] = jnp.broadcast_to(
                misfit[:, i * LANES : (i + 1) * LANES], (8, LANES)
            )
        forcing = weight * misfit
        high = forcing.astype(jnp.bfloat16)
        low = (forcing - high.astype(jnp.float32)).astype(jnp.bfloat16)
        return jnp.concatenate(
            [
                jnp.where(
                    hits[i], jnp.broadcast_to(term[:, i * LANES : (i + 1) * LANES], (256, LANES)), nil
                )
                for term in (high, low)
                for i in range(WIDTH)
            ],
            axis=1,
        )

    def scatter(spread, g, step, profile, part, observed, weight, hits):
        twice = jnp.concatenate([profile, profile], axis=0)
        second = lax.broadcasted_iota(jnp.int32, (PAIR, n), 0) >= LEVELS
        part_row = (part - jnp.where(second, 1.0, 0.0)).astype(jnp.bfloat16)
        for i in range(g * GROUP_PARTS // 2, (g + 1) * GROUP_PARTS // 2):
            left = jnp.where(part_row == jnp.bfloat16(2 * i), twice, nil)
            adjoint_ref[i * PAIR : (i + 1) * PAIR, :] += lax.dot_general(
                jnp.concatenate([left, left], axis=1),
                spread,
                (((1,), (1,)), ((), ())),
                preferred_element_type=jnp.float32,
            )

    def work(groups, step):
        loaded = [load(g, step) for g in groups]
        columns = [gather(*x) for x in loaded]
        spreads = [force(column, *x) for x, column in zip(loaded, columns)]
        for x, spread in zip(loaded, spreads):
            scatter(spread, *x)
        return 0

    steps = [lax.shift_right_logical(ends[g] + n - 1, n.bit_length() - 1) for g in range(GROUPS)]
    common = functools.reduce(jnp.minimum, steps)
    lax.fori_loop(0, common, lambda step, _: work(range(GROUPS), step), 0)
    for g in range(GROUPS):
        lax.fori_loop(common, steps[g], lambda step, _, g=g: work([g], step), 0)

    lane = lax.broadcasted_iota(jnp.int32, (8, LANES), 1)
    row_id = lax.broadcasted_iota(jnp.int32, (8, LANES), 0)

    def part_ways(eight, ends):
        ends = list(ends)
        rows = jnp.zeros((8, LANES), jnp.float32)
        for j in range(8):
            start = jnp.int32(0)
            row = jnp.zeros((8, LANES), jnp.float32)
            for g in range(GROUPS):
                count = count_ref[(eight * 8 + j) * GROUPS + g]
                tile, at = lax.shift_right_logical(ends[g], 7), ends[g] & (LANES - 1)
                values = jnp.where(lane >= at, found_ref[g, tile], found_ref[g, tile + 1])
                values = pltpu.roll(values, (start - at) & (LANES - 1), 1)
                row = jnp.where(lane >= start, values, row)
                ends[g] = ends[g] + count
                start = start + count
            rows = jnp.where(row_id == j, row, rows)
        write_misfit(eight, rows)
        return tuple(ends)

    lax.fori_loop(0, block_ref.shape[0] // 8, part_ways, (jnp.int32(0),) * GROUPS)


def first_soundings_body(count_ref, field_ref, block_ref, adjoint_ref, misfit_ref, *scratch):
    adjoint_ref[...] = jnp.zeros_like(adjoint_ref)

    def write_misfit(eight, rows):
        misfit_ref[pl.ds(eight * 8, 8), :] = rows

    soundings(count_ref, field_ref, block_ref, adjoint_ref, write_misfit, *scratch)


def second_soundings_body(
    count_ref, field_ref, block_ref, earlier_ref, other_ref, adjoint_ref, misfit_ref, *rest
):
    edges, scratch = rest[:4], rest[4:]
    adjoint_ref[...] = earlier_ref[...]

    def write_misfit(eight, rows):
        misfit_ref[pl.ds(eight * 16, 8, stride=2), :] = other_ref[pl.ds(eight * 8, 8), :]
        misfit_ref[pl.ds(eight * 16 + 1, 8, stride=2), :] = rows

    soundings(count_ref, field_ref, block_ref, adjoint_ref, write_misfit, *scratch)
    write_edges(lambda t, row: cell_slab(adjoint_ref, t, row), *edges)


def observe(field, blocks, earlier=()):
    count = blocks.shape[0]
    part = blocks[:, LEVELS, :].astype(jnp.int32)[:, None, :]
    lowest = 1 + GROUP_PARTS * lax.broadcasted_iota(jnp.int32, (1, GROUPS, 1), 1)
    inside = (part >= lowest) & (part < lowest + GROUP_PARTS)
    counts = jnp.sum(jnp.where(inside, 1, 0), axis=2).reshape(count * GROUPS)
    tiles = count + WIDTH
    outs = [jax.ShapeDtypeStruct((PARTS * LEVELS, 256), jnp.float32)]
    outs += [jax.ShapeDtypeStruct((count * (2 if earlier else 1), LANES), jnp.float32)]
    return whole(
        second_soundings_body if earlier else first_soundings_body,
        outs + (EDGES if earlier else []),
        (counts, field, blocks) + tuple(earlier),
        "second_soundings" if earlier else "first_soundings",
        scratch=[
            pltpu.VMEM((GROUPS, tiles, ROWS, LANES), jnp.bfloat16),
            pltpu.VMEM((GROUPS, tiles, 8, LANES), jnp.float32),
            pltpu.VMEM((256, LANES), jnp.bfloat16),
        ],
        scalars=1,
        flops=15000000000,
    )


def per_device(
    initial, east_wind, north_wind, mixing, kernel, columns, observed, obs_weight, counts, targets
):
    lat_count = lax.axis_size("lat")
    lon_count = lax.axis_size("lon")
    sounds = kernel.shape[2]
    target_dev = targets[:, 0]
    block_count = target_dev.shape[0]
    device_count = lat_count * lon_count
    block_id = lax.broadcasted_iota(jnp.int32, (block_count, device_count), 0)
    meant = target_dev[:, None] == lax.broadcasted_iota(
        jnp.int32, (block_count, device_count), 1
    )
    source_first = jnp.min(jnp.where(meant, block_id, block_count), axis=0)
    source_last = jnp.max(jnp.where(meant, block_id, -1), axis=0)
    source_first = jnp.where(source_last >= 0, source_first, -1)
    source_second = jnp.where(source_last > source_first, source_last, -1)
    live = lax.broadcasted_iota(jnp.int32, (1, sounds), 1) < counts[:, None]
    key = (columns // 256) * sounds + lax.broadcasted_iota(jnp.int32, (1, sounds), 1)
    key = jnp.where(live, key, PARTS * sounds)
    place = jnp.sum(jnp.where(key[:, :, None] < key[:, None, :], 1, 0), axis=1)
    place = jnp.where(live, place, sounds)
    heard = (kernel, columns, observed.astype(jnp.float32), obs_weight.astype(jnp.float32), place)

    def exchange(array):
        return lax.all_to_all(array, ("lat", "lon"), split_axis=0, concat_axis=0, tiled=True)

    packed = jax.ShapeDtypeStruct((device_count, ROWS, sounds), jnp.bfloat16)
    got_first = exchange(
        whole(pack_body, packed, (source_first,) + heard, "pack_first", scalars=1)
    )
    got_second = exchange(
        whole(pack_body, packed, (source_second,) + heard, "pack_second", scalars=1)
    )

    is_last = (lax.axis_index("lat") == lat_count - 1).astype(jnp.int32).reshape(1)
    winds_like = jax.ShapeDtypeStruct((2, LAT_CELLS, LEVELS, LANES), jnp.float32)
    tall_edge = jax.ShapeDtypeStruct((TRACERS + 2, LEVELS, LANES), jnp.float32)
    prepared = whole(
        prepare_body,
        [STATE, winds_like, winds_like, winds_like, tall_edge] + EDGES[1:],
        (is_last, initial, east_wind, north_wind, mixing),
        "prepare",
        scalars=1,
    )
    state, fields, edges = prepared[0], tuple(prepared[1:4]), prepared[4:]
    halos = exchange_edges(edges)
    winds = (halos[0], halos[2])
    middle, *edges = whole(
        forward_first_body, [STATE] + EDGES, (state,) + fields + halos, "forward_first"
    )
    field = whole(
        forward_last_body,
        jax.ShapeDtypeStruct((12 * LEVELS, 512), jnp.bfloat16),
        (middle,) + fields + exchange_edges(edges) + winds,
        "forward_last",
        scratch=[pltpu.VMEM(STATE.shape, jnp.float32)],
    )
    earlier = observe(field, got_first)
    adjoint, misfit, *edges = observe(field, got_second, earlier)
    halos = exchange_edges(edges)
    returned = exchange(misfit)
    middle, *edges = whole(
        adjoint_first_body, [STATE] + EDGES, (adjoint,) + fields + halos + winds, "adjoint_first"
    )
    gradient = whole(
        adjoint_last_body,
        jax.ShapeDtypeStruct(initial.shape, jnp.float32),
        (middle,) + fields + exchange_edges(edges) + winds,
        "adjoint_last",
    )
    innovations = whole(
        innovations_body,
        jax.ShapeDtypeStruct((block_count, sounds), jnp.float32),
        (source_first, source_second, returned, place),
        "innovations",
        scratch=[pltpu.VMEM((block_count + 8, sounds), jnp.float32)],
        scalars=2,
    )
    return (gradient, innovations)


def solution(mesh):
    return jax.shard_map(
        per_device,
        mesh=mesh,
        in_specs=(
            P(None, None, "lat", "lon"),
            P(None, None, "lat", "lon"),
            P(None, None, "lat", "lon"),
            P(None, None, "lat", "lon"),
            P(("lat", "lon"), None, None),
            P(("lat", "lon"), None),
            P(("lat", "lon"), None),
            P(("lat", "lon"), None),
            P(("lat", "lon")),
            P(("lat", "lon"), None),
        ),
        out_specs=(P(None, None, "lat", "lon"), P(("lat", "lon"), None)),
        check_vma=False,
    )
```

```python
import functools

import jax
import jax.numpy as jnp
from jax import lax
from jax.experimental import pallas as pl
from jax.experimental.pallas import tpu as pltpu
from jax.sharding import PartitionSpec as P

LEVELS = 72
ROWS = 80
PAIR = 2 * LEVELS
TRACERS = 3
PARTS = 12
GROUPS = 6
GROUP_PARTS = PARTS // GROUPS
WIDTH = 2
LAT_CELLS = 8
LANES = 128


def lane_index():
    return lax.broadcasted_iota(jnp.int32, (LEVELS, LANES), 1)


def rolled(array, shift, axis):
    shift = shift % array.shape[axis]
    return pltpu.roll(array, shift, axis) if shift else array


def west_of(slab, halo, place):
    return jnp.where(lane_index() == 0, rolled(halo, -place, 1), rolled(slab, 1, 1))


def east_of(slab, halo, place):
    return jnp.where(
        lane_index() == LANES - 1, rolled(halo, LANES - 1 - place, 1), rolled(slab, -1, 1)
    )


SLOT = 32


def place_of(t, row):
    return t * 10 + row + 1


def packed(slabs, lane, base=0):
    out = jnp.zeros((LEVELS, LANES), jnp.float32)
    for i, slab in enumerate(slabs):
        place = base + place_of(i // LAT_CELLS, i % LAT_CELLS)
        out = jnp.where(lane_index() == place, rolled(slab, place - lane, 1), out)
    return out


def packed_wind(slabs, lane, base):
    one = packed(slabs, lane, base)
    return one + rolled(one, 10, 1) + rolled(one, 20, 1)


def slot(array, number):
    return rolled(array, -SLOT * number, 1)


def with_corners(own, south, north, number=0):
    row = (lane_index() & (SLOT - 1)) % 10
    out = jnp.where(row == 0, rolled(south, number - LAT_CELLS, 1), own)
    return jnp.where(row == 9, rolled(north, LAT_CELLS - number, 1), out)


def corners_body(from_west, from_east, up_in, down_in, up_ref, down_ref):
    last = up_in.shape[0]
    for i in range(last):
        up_ref[i] = up_in[i]
    for i in range(down_in.shape[0]):
        down_ref[i] = down_in[i]
    row = (lane_index() & (SLOT - 1)) % 10
    up = jnp.zeros((LEVELS, LANES), jnp.float32)
    down = jnp.zeros((LEVELS, LANES), jnp.float32)
    for i in range(6):
        column = from_west[i] if i < 3 else from_east[i - 3]
        up = up + rolled(jnp.where(row == LAT_CELLS, column, 0.0), -i, 1)
        down = down + rolled(jnp.where(row == 1, column, 0.0), i, 1)
    up_ref[last] = up
    down_ref[down_in.shape[0]] = down


def mixed(slab, coeff):
    upward = coeff * (rolled(slab, -1, 0) - slab)
    return upward - rolled(upward, 1, 0)


def forward(slab, left, right, above, below, east, before, north, south, coeff):
    zonal = jnp.maximum(east, 0.0) * slab + jnp.minimum(east, 0.0) * right
    zonal_before = jnp.maximum(before, 0.0) * left + jnp.minimum(before, 0.0) * slab
    merid = jnp.maximum(north, 0.0) * slab + jnp.minimum(north, 0.0) * above
    merid_before = jnp.maximum(south, 0.0) * below + jnp.minimum(south, 0.0) * slab
    return slab - (zonal - zonal_before) - (merid - merid_before) + mixed(slab, coeff)


def backward(slab, left, right, above, below, east, before, north, south, coeff):
    zonal = jnp.maximum(east, 0.0) * (right - slab) + jnp.minimum(before, 0.0) * (slab - left)
    merid = jnp.maximum(north, 0.0) * (above - slab) + jnp.minimum(south, 0.0) * (slab - below)
    return slab + zonal + merid + mixed(slab, coeff)


def write_edges(read, up_ref, down_ref, east_edge, west_edge):
    slabs = [read(t, row) for t in range(TRACERS) for row in range(LAT_CELLS)]
    for t in range(TRACERS):
        for i in range(2):
            up_ref[2 * t + i] = slabs[t * LAT_CELLS + LAT_CELLS - 2 + i]
            down_ref[2 * t + i] = slabs[t * LAT_CELLS + i]
    east_edge[...] = packed(slabs, LANES - 1) + packed(slabs, LANES - 2, SLOT)
    west_edge[...] = packed(slabs, 0) + packed(slabs, 1, SLOT)


def prepare_body(
    last_ref, initial_ref, east_ref, north_ref, mixing_ref,
    state_ref, east_out, north_out, mixing_out, up_ref, down_ref, east_edge, west_edge,
):
    steps = east_ref.shape[0]
    last = LAT_CELLS - 1
    top = lax.broadcasted_iota(jnp.int32, (LEVELS, LANES), 0) == LEVELS - 1
    for t in range(TRACERS):
        for row in range(LAT_CELLS):
            state_ref[t, row] = initial_ref[t, :, row, :]
    for m in range(steps):
        for row in range(LAT_CELLS):
            east_out[m, row] = east_ref[m, :, row, :]
            north = north_ref[m, :, row, :]
            if row == last:
                north = jnp.where(last_ref[0] > 0, jnp.float32(0.0), north)
            north_out[m, row] = north
            mixing_out[m, row] = jnp.where(top, jnp.float32(0.0), mixing_ref[m, :, row, :])
    write_edges(
        lambda t, row: state_ref[t, row], up_ref, down_ref, east_edge.at[0], west_edge.at[0]
    )
    for m in range(steps):
        ups = (east_out[m, last], mixing_out[m, last], north_out[m, last], north_out[m, last - 1])
        for i, slab in enumerate(ups):
            up_ref[6 + 4 * m + i] = slab
        for i, slab in enumerate((east_out[m, 0], mixing_out[m, 0], north_out[m, 0])):
            down_ref[6 + 3 * m + i] = slab
        east, north, mixing = (
            [ref[m, row] for row in range(LAT_CELLS)] for ref in (east_out, north_out, mixing_out)
        )
        east_edge[1 + m] = (
            packed_wind(east, LANES - 1, 0)
            + packed_wind(mixing, LANES - 1, SLOT)
            + packed_wind(north, LANES - 1, 2 * SLOT)
            + packed_wind(east, LANES - 2, 3 * SLOT)
        )
        west_edge[1 + m] = (
            packed_wind(east, 0, 0)
            + packed_wind(mixing, 0, SLOT)
            + packed_wind(north, 0, 2 * SLOT)
        )


def two_steps(
    step, moments, read, winds, wind_up, wind_down, wind_east, sides,
    up_ref, down_ref, own_east, own_west, from_west, from_east, middle_ref, write,
):
    east_ref, north_ref, mixing_ref = winds

    def state(t, row):
        if row < 0:
            return up_ref[2 * t + row + 2]
        return read(t, row) if row < LAT_CELLS else down_ref[2 * t + row - LAT_CELLS]

    def wind(ref, number, m, row):
        if row < -1:
            return wind_up(4 * m + 3)
        if row < 0:
            return wind_up(4 * m + number)
        return ref[m, row] if row < LAT_CELLS else wind_down(3 * m + number)

    def winds_of(m, row, east_side):
        east = wind(east_ref, 0, m, row)
        return (
            east,
            west_of(east, east_side, place_of(0, row)),
            wind(north_ref, 2, m, row),
            wind(north_ref, 2, m, row - 1),
            wind(mixing_ref, 1, m, row),
        )

    m = moments[0]
    side_west, side_east = sides(m)
    for row in range(-1, LAT_CELLS + 1):
        local = winds_of(m, row, side_west)
        for t in range(TRACERS):
            slab, place = state(t, row), place_of(t, row)
            middle_ref[t, row + 1] = step(
                slab,
                west_of(slab, from_west, place),
                east_of(slab, from_east, place),
                state(t, row + 1),
                state(t, row - 1),
                *local,
            )

    def column(own, left, right, east, before, side):
        north = slot(side, 2)
        around = (rolled(own, -1, 1), rolled(own, 1, 1))
        return step(
            own, left, right, *around, east, before, north, rolled(north, 1, 1), slot(side, 1)
        )

    next_west = column(
        from_west, slot(from_west, 1), own_west, side_west, slot(side_west, 3), side_west
    )
    next_east = column(
        from_east, own_east, slot(from_east, 1), side_east, wind_east(m), side_east
    )
    m = moments[1]
    side_west, _ = sides(m)
    for row in range(LAT_CELLS):
        local = winds_of(m, row, side_west)
        for t in range(TRACERS):
            slab, place = middle_ref[t, row + 1], place_of(t, row)
            write(
                t,
                row,
                step(
                    slab,
                    west_of(slab, next_west, place),
                    east_of(slab, next_east, place),
                    middle_ref[t, row + 2],
                    middle_ref[t, row],
                    *local,
                ),
            )


def forward_body(
    state_ref, east_ref, north_ref, mixing_ref, own_east, own_west,
    up_ref, down_ref, from_west, from_east,
    field_ref, sides_ref, middle_ref, after_ref,
):
    south, north = up_ref.at[14], down_ref.at[12]
    for m in range(2):
        sides_ref[m, 0] = with_corners(from_west[1 + m], south[...], north[...], 1 + m)
        sides_ref[m, 1] = with_corners(from_east[1 + m], south[...], north[...], 4 + m)

    def write(t, row, slab):
        after_ref[t, row] = slab

    two_steps(
        forward,
        (0, 1),
        lambda t, row: state_ref[t, row],
        (east_ref, north_ref, mixing_ref),
        lambda i: up_ref[6 + i],
        lambda i: down_ref[6 + i],
        lambda m: own_east[1 + m],
        lambda m: (sides_ref[m, 0], sides_ref[m, 1]),
        up_ref,
        down_ref,
        own_east[0],
        own_west[0],
        with_corners(from_west[0], south[...], north[...], 0),
        with_corners(from_east[0], south[...], north[...], 3),
        middle_ref,
        write,
    )
    for i in range(6):
        for low_row in range(2):
            slabs = []
            for p in (2 * i, 2 * i + 1):
                slabs.append(after_ref[p // 4, (p % 4) * 2 + low_row])
            both = jnp.concatenate(slabs, axis=0)
            high = both.astype(jnp.bfloat16)
            low = (both - high.astype(jnp.float32)).astype(jnp.bfloat16)
            rows = slice(i * PAIR, (i + 1) * PAIR)
            field_ref[rows, low_row * LANES : (low_row + 1) * LANES] = high
            field_ref[rows, (2 + low_row) * LANES : (3 + low_row) * LANES] = low


def cell_slab(ref, t, row):
    first = (t * 4 + row // 2) * LEVELS
    return ref[first : first + LEVELS, (row % 2) * LANES : (row % 2 + 1) * LANES]


def adjoint_body(
    adjoint_ref, east_ref, north_ref, mixing_ref, wind_up, wind_down, wind_east, sides_ref,
    own_east, own_west, from_west, from_east, up_ref, down_ref, gradient_ref, middle_ref,
):
    def write(t, row, slab):
        gradient_ref[t, :, row, :] = slab

    two_steps(
        backward,
        (1, 0),
        lambda t, row: cell_slab(adjoint_ref, t, row),
        (east_ref, north_ref, mixing_ref),
        lambda i: wind_up[6 + i],
        lambda i: wind_down[6 + i],
        lambda m: wind_east[1 + m],
        lambda m: (sides_ref[m, 0], sides_ref[m, 1]),
        up_ref,
        down_ref,
        own_east[...],
        own_west[...],
        with_corners(from_west[...], up_ref[6], down_ref[6]),
        with_corners(from_east[...], up_ref[7], down_ref[7]),
        middle_ref,
        write,
    )


STATE = jax.ShapeDtypeStruct((TRACERS, LAT_CELLS, LEVELS, LANES), jnp.float32)
ROW_EDGE = jax.ShapeDtypeStruct((2 * TRACERS, LEVELS, LANES), jnp.float32)
COLUMN_EDGE = jax.ShapeDtypeStruct((LEVELS, LANES), jnp.float32)
EDGES = [ROW_EDGE, ROW_EDGE, COLUMN_EDGE, COLUMN_EDGE]
MIDDLE = pltpu.VMEM((TRACERS, LAT_CELLS + 2, LEVELS, LANES), jnp.float32)


def whole(body, outs, operands, name, scratch=(), scalars=0, flops=5000000, scalar_outs=0, vmem_mib=56):
    smem = pl.BlockSpec(memory_space=pltpu.SMEM)

    def vmem(array):
        zeros = (0,) * len(array.shape)
        return pl.BlockSpec(array.shape, lambda i: zeros, pipeline_mode=pl.Buffered(1))

    return pl.pallas_call(
        body,
        grid=(1,),
        in_specs=[smem if i < scalars else vmem(a) for i, a in enumerate(operands)],
        out_specs=[vmem(a) if i < len(outs) - scalar_outs else smem for i, a in enumerate(outs)],
        out_shape=outs,
        scratch_shapes=list(scratch),
        compiler_params=pltpu.CompilerParams(vmem_limit_bytes=vmem_mib << 20),
        cost_estimate=pl.CostEstimate(flops=flops, bytes_accessed=6000000, transcendentals=0),
        name=name,
    )(*operands)


def shifted(array, lat_by, lon_by):
    lat, lon = lax.axis_size("lat"), lax.axis_size("lon")
    if not lat_by:
        return lax.ppermute(array, "lon", [(j, (j + lon_by) % lon) for j in range(lon)])
    rows = [(i, i + lat_by) for i in range(lat) if 0 <= i + lat_by < lat]
    if not lon_by:
        return lax.ppermute(array, "lat", rows)
    pairs = [(i * lon + j, k * lon + (j + lon_by) % lon) for i, k in rows for j in range(lon)]
    return lax.ppermute(array, ("lat", "lon"), pairs)


def plan(targets_ref, counts_ref, columns_ref, place_ref, first_ref, second_ref, tally_ref):
    def clear(device, carry):
        first_ref[device] = -1
        second_ref[device] = -1
        return carry

    lax.fori_loop(0, first_ref.shape[0], clear, 0, unroll=8)

    def name(block, carry):
        target = targets_ref[block]
        known = first_ref[target]
        second_ref[target] = jnp.where(known < 0, -1, block)
        first_ref[target] = jnp.where(known < 0, block, known)
        return carry

    lax.fori_loop(0, targets_ref.shape[0], name, 0, unroll=8)
    part_id = lax.broadcasted_iota(jnp.int32, (16, LANES), 0)
    group = lax.broadcasted_iota(jnp.int32, (16, LANES), 1) * GROUP_PARTS
    of_group = (part_id >= group) & (part_id < group + GROUP_PARTS)
    lane = lax.broadcasted_iota(jnp.int32, (1, LANES), 1)
    row_id = lax.broadcasted_iota(jnp.int32, (8, LANES), 0)
    square = (LANES, 2 * LANES)
    earlier = lax.broadcasted_iota(jnp.int32, square, 0) < lax.broadcasted_iota(
        jnp.int32, square, 1
    )
    earlier = jnp.where(earlier, 1.0, 0.0).astype(jnp.bfloat16)

    def rank(eight, carry):
        parts = lax.shift_right_logical(columns_ref[pl.ds(eight * 8, 8), :], 8)
        rows = [parts[j : j + 1] for j in range(8)]
        lives = [lane < counts_ref[eight * 8 + j] for j in range(8)]
        members = [
            jnp.where((part_id == row) & live, 1.0, 0.0) for row, live in zip(rows, lives)
        ]
        sums = jnp.dot(
            jnp.concatenate(members, axis=0).astype(jnp.bfloat16),
            earlier,
            preferred_element_type=jnp.float32,
        )
        places = jnp.zeros((8, LANES), jnp.float32)
        tallies = jnp.zeros((8, LANES), jnp.float32)
        for j in range(8):
            own = sums[16 * j : 16 * j + 16]
            before = jnp.where(
                part_id == rows[j],
                own[:, :LANES],
                jnp.where(part_id < rows[j], own[:, LANES:], jnp.float32(0.0)),
            )
            place = jnp.sum(before, axis=0, keepdims=True)
            place = jnp.where(lives[j], place, jnp.float32(LANES))
            places = jnp.where(row_id == j, place, places)
            tally = jnp.sum(jnp.where(of_group, own[:, LANES:], 0.0), axis=0, keepdims=True)
            tallies = jnp.where(row_id == j, tally, tallies)
        place_ref[pl.ds(eight * 8, 8), :] = places
        tally_ref[pl.ds(eight * 8, 8), :] = tallies
        return carry

    lax.fori_loop(0, targets_ref.shape[0] // 8, rank, 0, unroll=2)


def pack(
    source_ref, kernel_ref, columns_ref, observed_ref, weight_ref, place_ref, tally_ref, out_ref,
    observed_wide, weight_wide, order_ref,
):
    observed_wide[...] = observed_ref[...].astype(jnp.float32)
    weight_wide[...] = weight_ref[...].astype(jnp.float32)
    order_ref[...] = (
        lax.broadcasted_iota(jnp.int32, (LANES, LANES), 0).astype(jnp.float32).astype(jnp.bfloat16)
    )
    row_id = lax.broadcasted_iota(jnp.int32, (8, LANES), 0)
    one, nil = jnp.bfloat16(1), jnp.bfloat16(0)

    def sorted_block(slot):
        source = source_ref[slot]
        block = jnp.maximum(source, 0)
        row = pl.ds(block, 1)
        cell = columns_ref[row, :]
        part = lax.shift_right_logical(cell, 8) + 1
        meta = jnp.where(row_id == 0, part.astype(jnp.float32), jnp.float32(0.0))
        meta = jnp.where(row_id == 1, (cell & 255).astype(jnp.float32), meta)
        meta = jnp.where(row_id == 2, observed_wide[row, :], meta)
        meta = jnp.where(row_id == 3, weight_wide[row, :], meta)
        rows = jnp.concatenate([kernel_ref[block].astype(jnp.float32), meta], axis=0)
        place = jnp.where(source >= 0, place_ref[row, :], jnp.float32(LANES)).astype(jnp.bfloat16)
        moved = jnp.where(order_ref[...] == jnp.broadcast_to(place, (LANES, LANES)), one, nil)
        result = lax.dot_general(
            rows.astype(jnp.bfloat16),
            moved,
            (((1,), (1,)), ((), ())),
            preferred_element_type=jnp.float32,
        )
        tally = jnp.where(source >= 0, tally_ref[row, :], jnp.float32(0.0))
        meta = jnp.where(row_id == 4, tally, result[LEVELS:])
        return jnp.concatenate([result[:LEVELS], meta], axis=0).astype(jnp.bfloat16)

    together = 16

    def several(step, carry):
        blocks = [sorted_block(step * together + j) for j in range(together)]
        for j in range(together):
            out_ref[step * together + j] = blocks[j]
        return carry

    lax.fori_loop(0, out_ref.shape[0] // together, several, 0)


def pack_first_body(
    targets_ref, counts_ref, kernel_ref, columns_ref, observed_ref, weight_ref,
    out_ref, place_ref, tally_ref, first_ref, second_ref, *scratch,
):
    plan(targets_ref, counts_ref, columns_ref, place_ref, first_ref, second_ref, tally_ref)
    pack(
        first_ref, kernel_ref, columns_ref, observed_ref, weight_ref, place_ref, tally_ref, out_ref,
        *scratch,
    )


def innovations_body(first_ref, second_ref, returned_ref, place_ref, out_ref, rows_ref):
    def one(device, carry):
        for rank, source_ref in enumerate((first_ref, second_ref)):
            source = source_ref[device]
            block = jnp.where(source >= 0, source, LANES)
            rows_ref[pl.ds(block, 1), :] = returned_ref[pl.ds(2 * device + rank, 1), :]
        return carry

    lax.fori_loop(0, first_ref.shape[0], one, 0, unroll=8)
    place = place_ref[...].astype(jnp.int32)
    live = place < LANES
    found = jnp.take_along_axis(
        rows_ref[: place.shape[0], :], jnp.where(live, place, 0), axis=1
    )
    out_ref[...] = jnp.where(live, found, jnp.float32(0.0))


def soundings(
    field_ref, block_ref, adjoint_ref, write_misfit,
    stream_ref, found_ref, cell_ref, tally_ref, count_ref, sem,
):
    n = WIDTH * LANES
    one, nil = jnp.bfloat16(1), jnp.bfloat16(0)
    lane = lax.broadcasted_iota(jnp.int32, (ROWS, LANES), 1)
    cell_ref[...] = (
        lax.broadcasted_iota(jnp.int32, (256, LANES), 0).astype(jnp.float32).astype(jnp.bfloat16)
    )
    empty = jnp.zeros((ROWS, LANES), jnp.bfloat16)
    eighth = lax.broadcasted_iota(jnp.int32, (8, LANES), 0)

    def tally(eight, carry):
        rows = jnp.zeros((8, LANES), jnp.float32)
        for j in range(8):
            meta = block_ref[eight * 8 + j][LEVELS:].astype(jnp.float32)
            rows = jnp.where(eighth == j, meta[4:5], rows)
        tally_ref[pl.ds(eight * 8, 8), :] = rows.astype(jnp.int32)
        return carry

    lax.fori_loop(0, block_ref.shape[0] // 8, tally, 0, unroll=2)
    copy = pltpu.make_async_copy(tally_ref, count_ref, sem)
    copy.start()
    copy.wait()

    def merge(block, carry):
        ends, tails = list(carry[0]), list(carry[1])
        values = block_ref[block]
        start = jnp.int32(0)
        for g in range(GROUPS):
            count = count_ref[block, g]
            tile, at = lax.shift_right_logical(ends[g], 7), ends[g] & (LANES - 1)
            turned = pltpu.roll(values, (at - start) & (LANES - 1), 1)
            joined = jnp.where(lane >= at, turned, tails[g])
            stream_ref[g, tile] = joined
            tails[g] = jnp.where(at + count >= LANES, turned, joined)
            ends[g] = ends[g] + count
            start = start + count
        return tuple(ends), tuple(tails)

    ends, tails = lax.fori_loop(
        0,
        block_ref.shape[0],
        merge,
        ((jnp.int32(0),) * GROUPS, (empty,) * GROUPS),
        unroll=2,
    )
    for g in range(GROUPS):
        tile, at = lax.shift_right_logical(ends[g], 7), ends[g] & (LANES - 1)
        stream_ref[g, tile] = jnp.where(lane < at, tails[g], empty)
        for j in range(1, WIDTH):
            stream_ref[g, tile + j] = empty

    def load(g, step):
        tiles = [stream_ref[g, step * WIDTH + i] for i in range(WIDTH)]
        profile = jnp.concatenate([t[:LEVELS] for t in tiles], axis=1)
        meta = jnp.concatenate([t[LEVELS:] for t in tiles], axis=1).astype(jnp.float32)
        part, cell, observed, weight = (meta[j : j + 1] for j in range(4))
        cell = cell.astype(jnp.bfloat16)
        hits = [
            cell_ref[...] == jnp.broadcast_to(cell[:, i * LANES : (i + 1) * LANES], (256, LANES))
            for i in range(WIDTH)
        ]
        return g, step, profile, part - 1.0, observed, weight, hits

    def gather(g, step, profile, part, observed, weight, hits):
        pick = jnp.concatenate([jnp.where(hit, one, nil) for hit in hits], axis=1)
        pick_twice = jnp.concatenate([pick, pick], axis=0)
        column = jnp.zeros((LEVELS, n), jnp.float32)
        for i in range(g * GROUP_PARTS // 2, (g + 1) * GROUP_PARTS // 2):
            found = jnp.dot(
                field_ref[i * PAIR : (i + 1) * PAIR, :],
                pick_twice,
                preferred_element_type=jnp.float32,
            )
            column = jnp.where(part == 2.0 * i, found[:LEVELS], column)
            column = jnp.where(part == 2.0 * i + 1.0, found[LEVELS:], column)
        return column

    def force(column, g, step, profile, part, observed, weight, hits):
        model = jnp.sum(profile.astype(jnp.float32) * column, axis=0, keepdims=True)
        misfit = model - observed
        for i in range(WIDTH):
            found_ref[g, step * WIDTH + i] = jnp.broadcast_to(
                misfit[:, i * LANES : (i + 1) * LANES], (8, LANES)
            )
        forcing = weight * misfit
        high = forcing.astype(jnp.bfloat16)
        low = (forcing - high.astype(jnp.float32)).astype(jnp.bfloat16)
        return jnp.concatenate(
            [
                jnp.where(
                    hits[i], jnp.broadcast_to(term[:, i * LANES : (i + 1) * LANES], (256, LANES)), nil
                )
                for term in (high, low)
                for i in range(WIDTH)
            ],
            axis=1,
        )

    def scatter(spread, g, step, profile, part, observed, weight, hits):
        twice = jnp.concatenate([profile, profile], axis=0)
        second = lax.broadcasted_iota(jnp.int32, (PAIR, n), 0) >= LEVELS
        part_row = (part - jnp.where(second, 1.0, 0.0)).astype(jnp.bfloat16)
        for i in range(g * GROUP_PARTS // 2, (g + 1) * GROUP_PARTS // 2):
            left = jnp.where(part_row == jnp.bfloat16(2 * i), twice, nil)
            adjoint_ref[i * PAIR : (i + 1) * PAIR, :] += lax.dot_general(
                jnp.concatenate([left, left], axis=1),
                spread,
                (((1,), (1,)), ((), ())),
                preferred_element_type=jnp.float32,
            )

    def work(groups, step):
        loaded = [load(g, step) for g in groups]
        columns = [gather(*x) for x in loaded]
        spreads = [force(column, *x) for x, column in zip(loaded, columns)]
        for x, spread in zip(loaded, spreads):
            scatter(spread, *x)
        return 0

    steps = [lax.shift_right_logical(ends[g] + n - 1, n.bit_length() - 1) for g in range(GROUPS)]
    common = functools.reduce(jnp.minimum, steps)
    lax.fori_loop(0, common, lambda step, _: work(range(GROUPS), step), 0)
    for g in range(GROUPS):
        lax.fori_loop(common, steps[g], lambda step, _, g=g: work([g], step), 0)

    lane = lax.broadcasted_iota(jnp.int32, (8, LANES), 1)
    row_id = lax.broadcasted_iota(jnp.int32, (8, LANES), 0)

    def part_ways(eight, ends):
        ends = list(ends)
        rows = jnp.zeros((8, LANES), jnp.float32)
        for j in range(8):
            start = jnp.int32(0)
            row = jnp.zeros((8, LANES), jnp.float32)
            for g in range(GROUPS):
                count = count_ref[eight * 8 + j, g]
                tile, at = lax.shift_right_logical(ends[g], 7), ends[g] & (LANES - 1)
                values = jnp.where(lane >= at, found_ref[g, tile], found_ref[g, tile + 1])
                values = pltpu.roll(values, (start - at) & (LANES - 1), 1)
                row = jnp.where(lane >= start, values, row)
                ends[g] = ends[g] + count
                start = start + count
            rows = jnp.where(row_id == j, row, rows)
        write_misfit(eight, rows)
        return tuple(ends)

    lax.fori_loop(0, block_ref.shape[0] // 8, part_ways, (jnp.int32(0),) * GROUPS)


def first_soundings_body(field_ref, block_ref, adjoint_ref, misfit_ref, *scratch):
    adjoint_ref[...] = jnp.zeros_like(adjoint_ref)

    def write_misfit(eight, rows):
        misfit_ref[pl.ds(eight * 8, 8), :] = rows

    soundings(field_ref, block_ref, adjoint_ref, write_misfit, *scratch)


def second_soundings_body(
    field_ref, block_ref, earlier_ref, other_ref, adjoint_ref, misfit_ref, *rest
):
    edges, scratch = rest[:4], rest[4:]
    adjoint_ref[...] = earlier_ref[...]

    def write_misfit(eight, rows):
        misfit_ref[pl.ds(eight * 16, 8, stride=2), :] = other_ref[pl.ds(eight * 8, 8), :]
        misfit_ref[pl.ds(eight * 16 + 1, 8, stride=2), :] = rows

    soundings(field_ref, block_ref, adjoint_ref, write_misfit, *scratch)
    write_edges(lambda t, row: cell_slab(adjoint_ref, t, row), *edges)


def observe(field, blocks, earlier=()):
    count = blocks.shape[0]
    tiles = count + WIDTH
    outs = [jax.ShapeDtypeStruct((PARTS * LEVELS, 256), jnp.float32)]
    outs += [jax.ShapeDtypeStruct((count * (2 if earlier else 1), LANES), jnp.float32)]
    return whole(
        second_soundings_body if earlier else first_soundings_body,
        outs + (EDGES if earlier else []),
        (field, blocks) + tuple(earlier),
        "second_soundings" if earlier else "first_soundings",
        scratch=[
            pltpu.VMEM((GROUPS, tiles, ROWS, LANES), jnp.bfloat16),
            pltpu.VMEM((GROUPS, tiles, 8, LANES), jnp.float32),
            pltpu.VMEM((256, LANES), jnp.bfloat16),
            pltpu.VMEM((count, LANES), jnp.int32),
            pltpu.SMEM((count, LANES), jnp.int32),
            pltpu.SemaphoreType.DMA(()),
        ],
        flops=15000000000,
    )


def per_device(
    initial, east_wind, north_wind, mixing, kernel, columns, observed, obs_weight, counts, targets
):
    lat_count = lax.axis_size("lat")
    lon_count = lax.axis_size("lon")
    sounds = kernel.shape[2]
    block_count = kernel.shape[0]
    device_count = lat_count * lon_count

    def exchange(array):
        return lax.all_to_all(array, ("lat", "lon"), split_axis=0, concat_axis=0, tiled=True)

    is_last = (lax.axis_index("lat") == lat_count - 1).astype(jnp.int32).reshape(1)
    winds_like = jax.ShapeDtypeStruct((2, LAT_CELLS, LEVELS, LANES), jnp.float32)

    def slabs_like(number):
        return jax.ShapeDtypeStruct((number, LEVELS, LANES), jnp.float32)

    prepared = whole(
        prepare_body,
        [STATE, winds_like, winds_like, winds_like]
        + [slabs_like(14), slabs_like(12), slabs_like(3), slabs_like(3)],
        (is_last, initial, east_wind, north_wind, mixing),
        "prepare",
        scalars=1,
    )
    state, fields, (up, down, east, west) = prepared[0], tuple(prepared[1:4]), prepared[4:]
    counts, east, west = lax.optimization_barrier((counts, east, west))
    slots = jax.ShapeDtypeStruct((device_count, ROWS, sounds), jnp.bfloat16)
    by_device = jax.ShapeDtypeStruct((device_count,), jnp.int32)
    heard = (kernel, columns, observed, obs_weight)
    scratch = [pltpu.VMEM((block_count, sounds), jnp.float32)] * 2
    scratch += [pltpu.VMEM((LANES, LANES), jnp.bfloat16)]
    by_block = jax.ShapeDtypeStruct((block_count, sounds), jnp.float32)
    out_first, place, tally, source_first, source_second = whole(
        pack_first_body,
        [slots, by_block, by_block, by_device, by_device],
        (targets[:, 0], counts) + heard,
        "pack_first",
        scratch=scratch,
        scalars=2,
        scalar_outs=2,
    )
    (out_second,) = whole(
        pack, [slots], (source_second,) + heard + (place, tally), "pack_second", scratch=scratch,
        scalars=1,
    )
    sides = (shifted(east, 0, 1), shifted(west, 0, -1))
    out_first, *sides = lax.optimization_barrier((out_first, *sides))
    up, down = whole(
        corners_body, [slabs_like(15), slabs_like(13)], tuple(sides) + (up, down), "corners"
    )
    out_first, up, down = lax.optimization_barrier((out_first, up, down))
    got_first = exchange(out_first)
    from_south, from_north = shifted(up, 1, 0), shifted(down, -1, 0)
    out_second, from_south, from_north = lax.optimization_barrier(
        (out_second, from_south, from_north)
    )
    got_second = exchange(out_second)
    field, wind_sides = whole(
        forward_body,
        [
            jax.ShapeDtypeStruct((12 * LEVELS, 512), jnp.bfloat16),
            jax.ShapeDtypeStruct((2, 2, LEVELS, LANES), jnp.float32),
        ],
        (state,) + fields + (east, west, from_south, from_north) + tuple(sides),
        "forward",
        scratch=[MIDDLE, pltpu.VMEM(STATE.shape, jnp.float32)],
    )
    earlier = observe(field, got_first)
    adjoint, misfit, up, down, own_east, own_west = observe(field, got_second, earlier)
    from_west, from_east = shifted(own_east, 0, 1), shifted(own_west, 0, -1)
    ends = jnp.stack([from_west, from_east])
    returned = exchange(misfit)
    (gradient,) = whole(
        adjoint_body,
        [jax.ShapeDtypeStruct(initial.shape, jnp.float32)],
        (adjoint,) + fields + (from_south, from_north, east, wind_sides)
        + (own_east, own_west, from_west, from_east)
        + (shifted(jnp.concatenate([up, ends]), 1, 0), shifted(jnp.concatenate([down, ends]), -1, 0)),
        "adjoint",
        scratch=[MIDDLE],
    )
    returned, gradient = lax.optimization_barrier((returned, gradient))
    (innovations,) = whole(
        innovations_body,
        [jax.ShapeDtypeStruct((block_count, sounds), jnp.float32)],
        (source_first, source_second, returned, place),
        "innovations",
        scratch=[pltpu.VMEM((block_count + 8, sounds), jnp.float32)],
        scalars=2,
    )
    return (gradient, innovations)


def solution(mesh):
    return jax.shard_map(
        per_device,
        mesh=mesh,
        in_specs=(
            P(None, None, "lat", "lon"),
            P(None, None, "lat", "lon"),
            P(None, None, "lat", "lon"),
            P(None, None, "lat", "lon"),
            P(("lat", "lon"), None, None),
            P(("lat", "lon"), None),
            P(("lat", "lon"), None),
            P(("lat", "lon"), None),
            P(("lat", "lon")),
            P(("lat", "lon"), None),
        ),
        out_specs=(P(None, None, "lat", "lon"), P(("lat", "lon"), None)),
        check_vma=False,
    )
```

```python
import functools

import jax
import jax.numpy as jnp
from jax import lax
from jax.experimental import pallas as pl
from jax.experimental.pallas import tpu as pltpu
from jax.sharding import PartitionSpec as P

LEVELS = 72
ROWS = 80
PAIR = 2 * LEVELS
TRACERS = 3
PARTS = 12
GROUPS = 6
GROUP_PARTS = PARTS // GROUPS
WIDTH = 2
LAT_CELLS = 8
LANES = 128


def lane_index():
    return lax.broadcasted_iota(jnp.int32, (LEVELS, LANES), 1)


def rolled(array, shift, axis):
    shift = shift % array.shape[axis]
    return pltpu.roll(array, shift, axis) if shift else array


def west_of(slab, halo, place):
    return jnp.where(lane_index() == 0, rolled(halo, -place, 1), rolled(slab, 1, 1))


def east_of(slab, halo, place):
    return jnp.where(
        lane_index() == LANES - 1, rolled(halo, LANES - 1 - place, 1), rolled(slab, -1, 1)
    )


SLOT = 32


def place_of(t, row):
    return t * 10 + row + 1


def packed(slabs, lane, base=0):
    out = jnp.zeros((LEVELS, LANES), jnp.float32)
    for i, slab in enumerate(slabs):
        place = base + place_of(i // LAT_CELLS, i % LAT_CELLS)
        out = jnp.where(lane_index() == place, rolled(slab, place - lane, 1), out)
    return out


def packed_wind(slabs, lane, base):
    one = packed(slabs, lane, base)
    return one + rolled(one, 10, 1) + rolled(one, 20, 1)


def slot(array, number):
    return rolled(array, -SLOT * number, 1)


def with_corners(own, south, north, number=0):
    row = (lane_index() & (SLOT - 1)) % 10
    out = jnp.where(row == 0, rolled(south, number - LAT_CELLS, 1), own)
    return jnp.where(row == 9, rolled(north, LAT_CELLS - number, 1), out)


def corners_body(from_west, from_east, up_ref, down_ref):
    row = (lane_index() & (SLOT - 1)) % 10
    up = jnp.zeros((LEVELS, LANES), jnp.float32)
    down = jnp.zeros((LEVELS, LANES), jnp.float32)
    for i in range(6):
        column = from_west[i] if i < 3 else from_east[i - 3]
        up = up + rolled(jnp.where(row == LAT_CELLS, column, 0.0), -i, 1)
        down = down + rolled(jnp.where(row == 1, column, 0.0), i, 1)
    up_ref[...] = up
    down_ref[...] = down


def mixed(slab, coeff):
    upward = coeff * (rolled(slab, -1, 0) - slab)
    return upward - rolled(upward, 1, 0)


def forward(slab, left, right, above, below, east, before, north, south, coeff):
    zonal = jnp.maximum(east, 0.0) * slab + jnp.minimum(east, 0.0) * right
    zonal_before = jnp.maximum(before, 0.0) * left + jnp.minimum(before, 0.0) * slab
    merid = jnp.maximum(north, 0.0) * slab + jnp.minimum(north, 0.0) * above
    merid_before = jnp.maximum(south, 0.0) * below + jnp.minimum(south, 0.0) * slab
    return slab - (zonal - zonal_before) - (merid - merid_before) + mixed(slab, coeff)


def backward(slab, left, right, above, below, east, before, north, south, coeff):
    zonal = jnp.maximum(east, 0.0) * (right - slab) + jnp.minimum(before, 0.0) * (slab - left)
    merid = jnp.maximum(north, 0.0) * (above - slab) + jnp.minimum(south, 0.0) * (slab - below)
    return slab + zonal + merid + mixed(slab, coeff)


def write_edges(read, up_ref, down_ref, east_edge, west_edge):
    slabs = [read(t, row) for t in range(TRACERS) for row in range(LAT_CELLS)]
    for t in range(TRACERS):
        for i in range(2):
            up_ref[2 * t + i] = slabs[t * LAT_CELLS + LAT_CELLS - 2 + i]
            down_ref[2 * t + i] = slabs[t * LAT_CELLS + i]
    east_edge[...] = packed(slabs, LANES - 1) + packed(slabs, LANES - 2, SLOT)
    west_edge[...] = packed(slabs, 0) + packed(slabs, 1, SLOT)


def arrange_body(
    last_ref, initial_ref, east_ref, north_ref, mixing_ref, state_ref, east_out, north_out, mixing_out
):
    for t in range(TRACERS):
        for row in range(LAT_CELLS):
            state_ref[t, row] = initial_ref[t, :, row, :]
    for m in range(east_ref.shape[0]):
        for row in range(LAT_CELLS):
            east_out[m, row] = east_ref[m, :, row, :]
            north_out[m, row] = masked_north(last_ref, north_ref, m, row)
            mixing_out[m, row] = masked_mixing(mixing_ref, m, row)


def masked_north(last_ref, north_ref, m, row):
    north = north_ref[m, :, row, :]
    if row == LAT_CELLS - 1:
        north = jnp.where(last_ref[0] > 0, jnp.float32(0.0), north)
    return north


def masked_mixing(mixing_ref, m, row):
    top = lax.broadcasted_iota(jnp.int32, (LEVELS, LANES), 0) == LEVELS - 1
    return jnp.where(top, jnp.float32(0.0), mixing_ref[m, :, row, :])


def edges_body(
    last_ref, initial_ref, east_ref, north_ref, mixing_ref, up_ref, down_ref, east_edge, west_edge
):
    last = LAT_CELLS - 1
    write_edges(
        lambda t, row: initial_ref[t, :, row, :], up_ref, down_ref, east_edge.at[0], west_edge.at[0]
    )
    for m in range(east_ref.shape[0]):
        east = [east_ref[m, :, row, :] for row in range(LAT_CELLS)]
        north = [masked_north(last_ref, north_ref, m, row) for row in range(LAT_CELLS)]
        mixing = [masked_mixing(mixing_ref, m, row) for row in range(LAT_CELLS)]
        for i, slab in enumerate((east[last], mixing[last], north[last], north[last - 1])):
            up_ref[6 + 4 * m + i] = slab
        for i, slab in enumerate((east[0], mixing[0], north[0])):
            down_ref[6 + 3 * m + i] = slab
        east_edge[1 + m] = (
            packed_wind(east, LANES - 1, 0)
            + packed_wind(mixing, LANES - 1, SLOT)
            + packed_wind(north, LANES - 1, 2 * SLOT)
            + packed_wind(east, LANES - 2, 3 * SLOT)
        )
        west_edge[1 + m] = (
            packed_wind(east, 0, 0)
            + packed_wind(mixing, 0, SLOT)
            + packed_wind(north, 0, 2 * SLOT)
        )


def two_steps(
    step, moments, read, winds, wind_up, wind_down, wind_east, sides,
    up_ref, down_ref, own_east, own_west, from_west, from_east, middle_ref, write,
):
    east_ref, north_ref, mixing_ref = winds

    def state(t, row):
        if row < 0:
            return up_ref[2 * t + row + 2]
        return read(t, row) if row < LAT_CELLS else down_ref[2 * t + row - LAT_CELLS]

    def wind(ref, number, m, row):
        if row < -1:
            return wind_up(4 * m + 3)
        if row < 0:
            return wind_up(4 * m + number)
        return ref[m, row] if row < LAT_CELLS else wind_down(3 * m + number)

    def winds_of(m, row, east_side):
        east = wind(east_ref, 0, m, row)
        return (
            east,
            west_of(east, east_side, place_of(0, row)),
            wind(north_ref, 2, m, row),
            wind(north_ref, 2, m, row - 1),
            wind(mixing_ref, 1, m, row),
        )

    m = moments[0]
    side_west, side_east = sides(m)
    for row in range(-1, LAT_CELLS + 1):
        local = winds_of(m, row, side_west)
        for t in range(TRACERS):
            slab, place = state(t, row), place_of(t, row)
            middle_ref[t, row + 1] = step(
                slab,
                west_of(slab, from_west, place),
                east_of(slab, from_east, place),
                state(t, row + 1),
                state(t, row - 1),
                *local,
            )

    def column(own, left, right, east, before, side):
        north = slot(side, 2)
        around = (rolled(own, -1, 1), rolled(own, 1, 1))
        return step(
            own, left, right, *around, east, before, north, rolled(north, 1, 1), slot(side, 1)
        )

    next_west = column(
        from_west, slot(from_west, 1), own_west, side_west, slot(side_west, 3), side_west
    )
    next_east = column(
        from_east, own_east, slot(from_east, 1), side_east, wind_east(m), side_east
    )
    m = moments[1]
    side_west, _ = sides(m)
    for row in range(LAT_CELLS):
        local = winds_of(m, row, side_west)
        for t in range(TRACERS):
            slab, place = middle_ref[t, row + 1], place_of(t, row)
            write(
                t,
                row,
                step(
                    slab,
                    west_of(slab, next_west, place),
                    east_of(slab, next_east, place),
                    middle_ref[t, row + 2],
                    middle_ref[t, row],
                    *local,
                ),
            )


def forward_body(
    state_ref, east_ref, north_ref, mixing_ref, own_east, own_west,
    up_ref, down_ref, from_west, from_east, south, north,
    field_ref, sides_ref, middle_ref, after_ref,
):
    for m in range(2):
        sides_ref[m, 0] = with_corners(from_west[1 + m], south[...], north[...], 1 + m)
        sides_ref[m, 1] = with_corners(from_east[1 + m], south[...], north[...], 4 + m)

    def write(t, row, slab):
        after_ref[t, row] = slab

    two_steps(
        forward,
        (0, 1),
        lambda t, row: state_ref[t, row],
        (east_ref, north_ref, mixing_ref),
        lambda i: up_ref[6 + i],
        lambda i: down_ref[6 + i],
        lambda m: own_east[1 + m],
        lambda m: (sides_ref[m, 0], sides_ref[m, 1]),
        up_ref,
        down_ref,
        own_east[0],
        own_west[0],
        with_corners(from_west[0], south[...], north[...], 0),
        with_corners(from_east[0], south[...], north[...], 3),
        middle_ref,
        write,
    )
    for i in range(6):
        for low_row in range(2):
            slabs = []
            for p in (2 * i, 2 * i + 1):
                slabs.append(after_ref[p // 4, (p % 4) * 2 + low_row])
            both = jnp.concatenate(slabs, axis=0)
            high = both.astype(jnp.bfloat16)
            low = (both - high.astype(jnp.float32)).astype(jnp.bfloat16)
            rows = slice(i * PAIR, (i + 1) * PAIR)
            field_ref[rows, low_row * LANES : (low_row + 1) * LANES] = high
            field_ref[rows, (2 + low_row) * LANES : (3 + low_row) * LANES] = low


def cell_slab(ref, t, row):
    first = (t * 4 + row // 2) * LEVELS
    return ref[first : first + LEVELS, (row % 2) * LANES : (row % 2 + 1) * LANES]


def adjoint_body(
    adjoint_ref, east_ref, north_ref, mixing_ref, wind_up, wind_down, wind_east, sides_ref,
    own_east, own_west, from_west, from_east, up_ref, down_ref, gradient_ref, middle_ref,
):
    def write(t, row, slab):
        gradient_ref[t, :, row, :] = slab

    two_steps(
        backward,
        (1, 0),
        lambda t, row: cell_slab(adjoint_ref, t, row),
        (east_ref, north_ref, mixing_ref),
        lambda i: wind_up[6 + i],
        lambda i: wind_down[6 + i],
        lambda m: wind_east[1 + m],
        lambda m: (sides_ref[m, 0], sides_ref[m, 1]),
        up_ref,
        down_ref,
        own_east[...],
        own_west[...],
        with_corners(from_west[...], up_ref[6], down_ref[6]),
        with_corners(from_east[...], up_ref[7], down_ref[7]),
        middle_ref,
        write,
    )


STATE = jax.ShapeDtypeStruct((TRACERS, LAT_CELLS, LEVELS, LANES), jnp.float32)
ROW_EDGE = jax.ShapeDtypeStruct((2 * TRACERS, LEVELS, LANES), jnp.float32)
COLUMN_EDGE = jax.ShapeDtypeStruct((LEVELS, LANES), jnp.float32)
EDGES = [ROW_EDGE, ROW_EDGE, COLUMN_EDGE, COLUMN_EDGE]
MIDDLE = pltpu.VMEM((TRACERS, LAT_CELLS + 2, LEVELS, LANES), jnp.float32)


def whole(body, outs, operands, name, scratch=(), scalars=0, flops=5000000, scalar_outs=0, vmem_mib=56):
    smem = pl.BlockSpec(memory_space=pltpu.SMEM)

    def vmem(array):
        zeros = (0,) * len(array.shape)
        return pl.BlockSpec(array.shape, lambda i: zeros, pipeline_mode=pl.Buffered(1))

    return pl.pallas_call(
        body,
        grid=(1,),
        in_specs=[smem if i < scalars else vmem(a) for i, a in enumerate(operands)],
        out_specs=[vmem(a) if i < len(outs) - scalar_outs else smem for i, a in enumerate(outs)],
        out_shape=outs,
        scratch_shapes=list(scratch),
        compiler_params=pltpu.CompilerParams(vmem_limit_bytes=vmem_mib << 20),
        cost_estimate=pl.CostEstimate(flops=flops, bytes_accessed=6000000, transcendentals=0),
        name=name,
    )(*operands)


def shifted(array, lat_by, lon_by):
    lat, lon = lax.axis_size("lat"), lax.axis_size("lon")
    if not lat_by:
        return lax.ppermute(array, "lon", [(j, (j + lon_by) % lon) for j in range(lon)])
    rows = [(i, i + lat_by) for i in range(lat) if 0 <= i + lat_by < lat]
    if not lon_by:
        return lax.ppermute(array, "lat", rows)
    pairs = [(i * lon + j, k * lon + (j + lon_by) % lon) for i, k in rows for j in range(lon)]
    return lax.ppermute(array, ("lat", "lon"), pairs)


def plan(targets_ref, counts_ref, columns_ref, place_ref, first_ref, second_ref, tally_ref):
    def clear(device, carry):
        first_ref[device] = -1
        second_ref[device] = -1
        return carry

    lax.fori_loop(0, first_ref.shape[0], clear, 0, unroll=8)

    def name(block, carry):
        target = targets_ref[block]
        known = first_ref[target]
        second_ref[target] = jnp.where(known < 0, -1, block)
        first_ref[target] = jnp.where(known < 0, block, known)
        return carry

    lax.fori_loop(0, targets_ref.shape[0], name, 0, unroll=8)
    part_id = lax.broadcasted_iota(jnp.int32, (16, LANES), 0)
    group = lax.broadcasted_iota(jnp.int32, (16, LANES), 1) * GROUP_PARTS
    of_group = (part_id >= group) & (part_id < group + GROUP_PARTS)
    lane = lax.broadcasted_iota(jnp.int32, (1, LANES), 1)
    row_id = lax.broadcasted_iota(jnp.int32, (8, LANES), 0)
    square = (LANES, 2 * LANES)
    earlier = lax.broadcasted_iota(jnp.int32, square, 0) < lax.broadcasted_iota(
        jnp.int32, square, 1
    )
    earlier = jnp.where(earlier, 1.0, 0.0).astype(jnp.bfloat16)

    def rank(eight, carry):
        parts = lax.shift_right_logical(columns_ref[pl.ds(eight * 8, 8), :], 8)
        rows = [parts[j : j + 1] for j in range(8)]
        lives = [lane < counts_ref[eight * 8 + j] for j in range(8)]
        members = [
            jnp.where((part_id == row) & live, 1.0, 0.0) for row, live in zip(rows, lives)
        ]
        sums = jnp.dot(
            jnp.concatenate(members, axis=0).astype(jnp.bfloat16),
            earlier,
            preferred_element_type=jnp.float32,
        )
        places = jnp.zeros((8, LANES), jnp.float32)
        tallies = jnp.zeros((8, LANES), jnp.float32)
        for j in range(8):
            own = sums[16 * j : 16 * j + 16]
            before = jnp.where(
                part_id == rows[j],
                own[:, :LANES],
                jnp.where(part_id < rows[j], own[:, LANES:], jnp.float32(0.0)),
            )
            place = jnp.sum(before, axis=0, keepdims=True)
            place = jnp.where(lives[j], place, jnp.float32(LANES))
            places = jnp.where(row_id == j, place, places)
            tally = jnp.sum(jnp.where(of_group, own[:, LANES:], 0.0), axis=0, keepdims=True)
            tallies = jnp.where(row_id == j, tally, tallies)
        place_ref[pl.ds(eight * 8, 8), :] = places
        tally_ref[pl.ds(eight * 8, 8), :] = tallies
        return carry

    lax.fori_loop(0, targets_ref.shape[0] // 8, rank, 0, unroll=2)


def pack(
    source_ref, kernel_ref, columns_ref, observed_ref, weight_ref, place_ref, tally_ref, out_ref,
    observed_wide, weight_wide, order_ref,
):
    observed_wide[...] = observed_ref[...].astype(jnp.float32)
    weight_wide[...] = weight_ref[...].astype(jnp.float32)
    order_ref[...] = (
        lax.broadcasted_iota(jnp.int32, (LANES, LANES), 0).astype(jnp.float32).astype(jnp.bfloat16)
    )
    row_id = lax.broadcasted_iota(jnp.int32, (8, LANES), 0)
    one, nil = jnp.bfloat16(1), jnp.bfloat16(0)

    def sorted_block(slot):
        source = source_ref[slot]
        block = jnp.maximum(source, 0)
        row = pl.ds(block, 1)
        cell = columns_ref[row, :]
        part = lax.shift_right_logical(cell, 8) + 1
        meta = jnp.where(row_id == 0, part.astype(jnp.float32), jnp.float32(0.0))
        meta = jnp.where(row_id == 1, (cell & 255).astype(jnp.float32), meta)
        meta = jnp.where(row_id == 2, observed_wide[row, :], meta)
        meta = jnp.where(row_id == 3, weight_wide[row, :], meta)
        rows = jnp.concatenate([kernel_ref[block].astype(jnp.float32), meta], axis=0)
        place = jnp.where(source >= 0, place_ref[row, :], jnp.float32(LANES)).astype(jnp.bfloat16)
        moved = jnp.where(order_ref[...] == jnp.broadcast_to(place, (LANES, LANES)), one, nil)
        result = lax.dot_general(
            rows.astype(jnp.bfloat16),
            moved,
            (((1,), (1,)), ((), ())),
            preferred_element_type=jnp.float32,
        )
        tally = jnp.where(source >= 0, tally_ref[row, :], jnp.float32(0.0))
        meta = jnp.where(row_id == 4, tally, result[LEVELS:])
        return jnp.concatenate([result[:LEVELS], meta], axis=0).astype(jnp.bfloat16)

    together = 16

    def several(step, carry):
        blocks = [sorted_block(step * together + j) for j in range(together)]
        for j in range(together):
            out_ref[step * together + j] = blocks[j]
        return carry

    lax.fori_loop(0, out_ref.shape[0] // together, several, 0)


def pack_first_body(
    targets_ref, counts_ref, kernel_ref, columns_ref, observed_ref, weight_ref,
    out_ref, place_ref, tally_ref, first_ref, second_ref, *scratch,
):
    plan(targets_ref, counts_ref, columns_ref, place_ref, first_ref, second_ref, tally_ref)
    pack(
        first_ref, kernel_ref, columns_ref, observed_ref, weight_ref, place_ref, tally_ref, out_ref,
        *scratch,
    )


def innovations_body(first_ref, second_ref, returned_ref, place_ref, out_ref, rows_ref):
    def one(device, carry):
        for rank, source_ref in enumerate((first_ref, second_ref)):
            source = source_ref[device]
            block = jnp.where(source >= 0, source, LANES)
            rows_ref[pl.ds(block, 1), :] = returned_ref[pl.ds(2 * device + rank, 1), :]
        return carry

    lax.fori_loop(0, first_ref.shape[0], one, 0, unroll=8)
    place = place_ref[...].astype(jnp.int32)
    live = place < LANES
    found = jnp.take_along_axis(
        rows_ref[: place.shape[0], :], jnp.where(live, place, 0), axis=1
    )
    out_ref[...] = jnp.where(live, found, jnp.float32(0.0))


def soundings(
    field_ref, block_ref, adjoint_ref, write_misfit,
    stream_ref, found_ref, cell_ref, tally_ref, count_ref, sem,
):
    n = WIDTH * LANES
    one, nil = jnp.bfloat16(1), jnp.bfloat16(0)
    lane = lax.broadcasted_iota(jnp.int32, (ROWS, LANES), 1)
    cell_ref[...] = (
        lax.broadcasted_iota(jnp.int32, (256, LANES), 0).astype(jnp.float32).astype(jnp.bfloat16)
    )
    empty = jnp.zeros((ROWS, LANES), jnp.bfloat16)
    eighth = lax.broadcasted_iota(jnp.int32, (8, LANES), 0)

    def tally(eight, carry):
        rows = jnp.zeros((8, LANES), jnp.float32)
        for j in range(8):
            meta = block_ref[eight * 8 + j][LEVELS:].astype(jnp.float32)
            rows = jnp.where(eighth == j, meta[4:5], rows)
        tally_ref[pl.ds(eight * 8, 8), :] = rows.astype(jnp.int32)
        return carry

    lax.fori_loop(0, block_ref.shape[0] // 8, tally, 0, unroll=2)
    copy = pltpu.make_async_copy(tally_ref, count_ref, sem)
    copy.start()
    copy.wait()

    def merge(block, carry):
        ends, tails = list(carry[0]), list(carry[1])
        values = block_ref[block]
        start = jnp.int32(0)
        for g in range(GROUPS):
            count = count_ref[block, g]
            tile, at = lax.shift_right_logical(ends[g], 7), ends[g] & (LANES - 1)
            turned = pltpu.roll(values, (at - start) & (LANES - 1), 1)
            joined = jnp.where(lane >= at, turned, tails[g])
            stream_ref[g, tile] = joined
            tails[g] = jnp.where(at + count >= LANES, turned, joined)
            ends[g] = ends[g] + count
            start = start + count
        return tuple(ends), tuple(tails)

    ends, tails = lax.fori_loop(
        0,
        block_ref.shape[0],
        merge,
        ((jnp.int32(0),) * GROUPS, (empty,) * GROUPS),
        unroll=4,
    )
    for g in range(GROUPS):
        tile, at = lax.shift_right_logical(ends[g], 7), ends[g] & (LANES - 1)
        stream_ref[g, tile] = jnp.where(lane < at, tails[g], empty)
        for j in range(1, WIDTH):
            stream_ref[g, tile + j] = empty

    def load(g, step):
        tiles = [stream_ref[g, step * WIDTH + i] for i in range(WIDTH)]
        profile = jnp.concatenate([t[:LEVELS] for t in tiles], axis=1)
        meta = jnp.concatenate([t[LEVELS:] for t in tiles], axis=1).astype(jnp.float32)
        part, cell, observed, weight = (meta[j : j + 1] for j in range(4))
        cell = cell.astype(jnp.bfloat16)
        hits = [
            cell_ref[...] == jnp.broadcast_to(cell[:, i * LANES : (i + 1) * LANES], (256, LANES))
            for i in range(WIDTH)
        ]
        return g, step, profile, part - 1.0, observed, weight, hits

    def gather(g, step, profile, part, observed, weight, hits):
        pick = jnp.concatenate([jnp.where(hit, one, nil) for hit in hits], axis=1)
        pick_twice = jnp.concatenate([pick, pick], axis=0)
        column = jnp.zeros((LEVELS, n), jnp.float32)
        for i in range(g * GROUP_PARTS // 2, (g + 1) * GROUP_PARTS // 2):
            found = jnp.dot(
                field_ref[i * PAIR : (i + 1) * PAIR, :],
                pick_twice,
                preferred_element_type=jnp.float32,
            )
            column = jnp.where(part == 2.0 * i, found[:LEVELS], column)
            column = jnp.where(part == 2.0 * i + 1.0, found[LEVELS:], column)
        return column

    def force(column, g, step, profile, part, observed, weight, hits):
        model = jnp.sum(profile.astype(jnp.float32) * column, axis=0, keepdims=True)
        misfit = model - observed
        for i in range(WIDTH):
            found_ref[g, step * WIDTH + i] = jnp.broadcast_to(
                misfit[:, i * LANES : (i + 1) * LANES], (8, LANES)
            )
        forcing = weight * misfit
        high = forcing.astype(jnp.bfloat16)
        low = (forcing - high.astype(jnp.float32)).astype(jnp.bfloat16)
        return jnp.concatenate(
            [
                jnp.where(
                    hits[i], jnp.broadcast_to(term[:, i * LANES : (i + 1) * LANES], (256, LANES)), nil
                )
                for term in (high, low)
                for i in range(WIDTH)
            ],
            axis=1,
        )

    def scatter(spread, g, step, profile, part, observed, weight, hits):
        twice = jnp.concatenate([profile, profile], axis=0)
        second = lax.broadcasted_iota(jnp.int32, (PAIR, n), 0) >= LEVELS
        part_row = (part - jnp.where(second, 1.0, 0.0)).astype(jnp.bfloat16)
        for i in range(g * GROUP_PARTS // 2, (g + 1) * GROUP_PARTS // 2):
            left = jnp.where(part_row == jnp.bfloat16(2 * i), twice, nil)
            adjoint_ref[i * PAIR : (i + 1) * PAIR, :] += lax.dot_general(
                jnp.concatenate([left, left], axis=1),
                spread,
                (((1,), (1,)), ((), ())),
                preferred_element_type=jnp.float32,
            )

    def work(groups, step):
        loaded = [load(g, step) for g in groups]
        columns = [gather(*x) for x in loaded]
        spreads = [force(column, *x) for x, column in zip(loaded, columns)]
        for x, spread in zip(loaded, spreads):
            scatter(spread, *x)
        return 0

    steps = [lax.shift_right_logical(ends[g] + n - 1, n.bit_length() - 1) for g in range(GROUPS)]
    common = functools.reduce(jnp.minimum, steps)
    lax.fori_loop(0, common, lambda step, _: work(range(GROUPS), step), 0)
    for g in range(GROUPS):
        lax.fori_loop(common, steps[g], lambda step, _, g=g: work([g], step), 0)

    lane = lax.broadcasted_iota(jnp.int32, (8, LANES), 1)
    row_id = lax.broadcasted_iota(jnp.int32, (8, LANES), 0)

    def part_ways(eight, ends):
        ends = list(ends)
        rows = jnp.zeros((8, LANES), jnp.float32)
        for j in range(8):
            start = jnp.int32(0)
            row = jnp.zeros((8, LANES), jnp.float32)
            for g in range(GROUPS):
                count = count_ref[eight * 8 + j, g]
                tile, at = lax.shift_right_logical(ends[g], 7), ends[g] & (LANES - 1)
                values = jnp.where(lane >= at, found_ref[g, tile], found_ref[g, tile + 1])
                values = pltpu.roll(values, (start - at) & (LANES - 1), 1)
                row = jnp.where(lane >= start, values, row)
                ends[g] = ends[g] + count
                start = start + count
            rows = jnp.where(row_id == j, row, rows)
        write_misfit(eight, rows)
        return tuple(ends)

    lax.fori_loop(0, block_ref.shape[0] // 8, part_ways, (jnp.int32(0),) * GROUPS)


def first_soundings_body(field_ref, block_ref, adjoint_ref, misfit_ref, *scratch):
    adjoint_ref[...] = jnp.zeros_like(adjoint_ref)

    def write_misfit(eight, rows):
        misfit_ref[pl.ds(eight * 8, 8), :] = rows

    soundings(field_ref, block_ref, adjoint_ref, write_misfit, *scratch)


def second_soundings_body(
    field_ref, block_ref, earlier_ref, other_ref, adjoint_ref, misfit_ref, *rest
):
    edges, scratch = rest[:4], rest[4:]
    adjoint_ref[...] = earlier_ref[...]

    def write_misfit(eight, rows):
        misfit_ref[pl.ds(eight * 16, 8, stride=2), :] = other_ref[pl.ds(eight * 8, 8), :]
        misfit_ref[pl.ds(eight * 16 + 1, 8, stride=2), :] = rows

    soundings(field_ref, block_ref, adjoint_ref, write_misfit, *scratch)
    write_edges(lambda t, row: cell_slab(adjoint_ref, t, row), *edges)


def observe(field, blocks, earlier=()):
    count = blocks.shape[0]
    tiles = count + WIDTH
    outs = [jax.ShapeDtypeStruct((PARTS * LEVELS, 256), jnp.float32)]
    outs += [jax.ShapeDtypeStruct((count * (2 if earlier else 1), LANES), jnp.float32)]
    return whole(
        second_soundings_body if earlier else first_soundings_body,
        outs + (EDGES if earlier else []),
        (field, blocks) + tuple(earlier),
        "second_soundings" if earlier else "first_soundings",
        scratch=[
            pltpu.VMEM((GROUPS, tiles, ROWS, LANES), jnp.bfloat16),
            pltpu.VMEM((GROUPS, tiles, 8, LANES), jnp.float32),
            pltpu.VMEM((256, LANES), jnp.bfloat16),
            pltpu.VMEM((count, LANES), jnp.int32),
            pltpu.SMEM((count, LANES), jnp.int32),
            pltpu.SemaphoreType.DMA(()),
        ],
        flops=15000000000,
    )


def per_device(
    initial, east_wind, north_wind, mixing, kernel, columns, observed, obs_weight, counts, targets
):
    lat_count = lax.axis_size("lat")
    lon_count = lax.axis_size("lon")
    sounds = kernel.shape[2]
    block_count = kernel.shape[0]
    device_count = lat_count * lon_count

    def exchange(array):
        return lax.all_to_all(array, ("lat", "lon"), split_axis=0, concat_axis=0, tiled=True)

    is_last = (lax.axis_index("lat") == lat_count - 1).astype(jnp.int32).reshape(1)
    winds_like = jax.ShapeDtypeStruct((2, LAT_CELLS, LEVELS, LANES), jnp.float32)

    def slabs_like(number):
        return jax.ShapeDtypeStruct((number, LEVELS, LANES), jnp.float32)

    grid = (is_last, initial, east_wind, north_wind, mixing)
    up, down, east, west = whole(
        edges_body,
        [slabs_like(14), slabs_like(12), slabs_like(3), slabs_like(3)],
        grid,
        "edges",
        scalars=1,
    )
    counts, up, down, east, west = lax.optimization_barrier((counts, up, down, east, west))
    from_south, from_north = shifted(up, 1, 0), shifted(down, -1, 0)
    slots = jax.ShapeDtypeStruct((device_count, ROWS, sounds), jnp.bfloat16)
    by_device = jax.ShapeDtypeStruct((device_count,), jnp.int32)
    heard = (kernel, columns, observed, obs_weight)
    scratch = [pltpu.VMEM((block_count, sounds), jnp.float32)] * 2
    scratch += [pltpu.VMEM((LANES, LANES), jnp.bfloat16)]
    by_block = jax.ShapeDtypeStruct((block_count, sounds), jnp.float32)
    out_first, place, tally, source_first, source_second = whole(
        pack_first_body,
        [slots, by_block, by_block, by_device, by_device],
        (targets[:, 0], counts) + heard,
        "pack_first",
        scratch=scratch,
        scalars=2,
        scalar_outs=2,
    )
    (out_second,) = whole(
        pack, [slots], (source_second,) + heard + (place, tally), "pack_second", scratch=scratch,
        scalars=1,
    )
    sides = (shifted(east, 0, 1), shifted(west, 0, -1))
    out_first, from_south, from_north, *sides = lax.optimization_barrier(
        (out_first, from_south, from_north, *sides)
    )
    got_first = exchange(out_first)
    corner_up, corner_down = whole(corners_body, [COLUMN_EDGE] * 2, tuple(sides), "corners")
    sides += [shifted(corner_up, 1, 0), shifted(corner_down, -1, 0)]
    grid = lax.optimization_barrier((corner_up,) + grid)[1:]
    arranged = whole(
        arrange_body, [STATE, winds_like, winds_like, winds_like], grid, "arrange", scalars=1
    )
    out_second, *rest = lax.optimization_barrier((out_second, *sides, *arranged))
    got_second = exchange(out_second)
    sides, state, fields = rest[:4], rest[4], tuple(rest[5:])
    field, wind_sides = whole(
        forward_body,
        [
            jax.ShapeDtypeStruct((12 * LEVELS, 512), jnp.bfloat16),
            jax.ShapeDtypeStruct((2, 2, LEVELS, LANES), jnp.float32),
        ],
        (state,) + fields + (east, west, from_south, from_north) + tuple(sides),
        "forward",
        scratch=[MIDDLE, pltpu.VMEM(STATE.shape, jnp.float32)],
    )
    earlier = observe(field, got_first)
    adjoint, misfit, up, down, own_east, own_west = observe(field, got_second, earlier)
    from_west, from_east = shifted(own_east, 0, 1), shifted(own_west, 0, -1)
    ends = jnp.stack([from_west, from_east])
    returned = exchange(misfit)
    (gradient,) = whole(
        adjoint_body,
        [jax.ShapeDtypeStruct(initial.shape, jnp.float32)],
        (adjoint,) + fields + (from_south, from_north, east, wind_sides)
        + (own_east, own_west, from_west, from_east)
        + (shifted(jnp.concatenate([up, ends]), 1, 0), shifted(jnp.concatenate([down, ends]), -1, 0)),
        "adjoint",
        scratch=[MIDDLE],
    )
    returned, gradient = lax.optimization_barrier((returned, gradient))
    (innovations,) = whole(
        innovations_body,
        [jax.ShapeDtypeStruct((block_count, sounds), jnp.float32)],
        (source_first, source_second, returned, place),
        "innovations",
        scratch=[pltpu.VMEM((block_count + 8, sounds), jnp.float32)],
        scalars=2,
    )
    return (gradient, innovations)


def solution(mesh):
    return jax.shard_map(
        per_device,
        mesh=mesh,
        in_specs=(
            P(None, None, "lat", "lon"),
            P(None, None, "lat", "lon"),
            P(None, None, "lat", "lon"),
            P(None, None, "lat", "lon"),
            P(("lat", "lon"), None, None),
            P(("lat", "lon"), None),
            P(("lat", "lon"), None),
            P(("lat", "lon"), None),
            P(("lat", "lon")),
            P(("lat", "lon"), None),
        ),
        out_specs=(P(None, None, "lat", "lon"), P(("lat", "lon"), None)),
        check_vma=False,
    )
```

```python
import functools

import jax
import jax.numpy as jnp
from jax import lax
from jax.experimental import pallas as pl
from jax.experimental.pallas import tpu as pltpu
from jax.sharding import PartitionSpec as P

LEVELS = 72
ROWS = 80
PAIR = 2 * LEVELS
TRACERS = 3
PARTS = 12
GROUPS = 6
GROUP_PARTS = PARTS // GROUPS
WIDTH = 2
LAT_CELLS = 8
LANES = 128


def lane_index():
    return lax.broadcasted_iota(jnp.int32, (LEVELS, LANES), 1)


def rolled(array, shift, axis):
    shift = shift % array.shape[axis]
    return pltpu.roll(array, shift, axis) if shift else array


def west_of(slab, halo, place):
    return jnp.where(lane_index() == 0, rolled(halo, -place, 1), rolled(slab, 1, 1))


def east_of(slab, halo, place):
    return jnp.where(
        lane_index() == LANES - 1, rolled(halo, LANES - 1 - place, 1), rolled(slab, -1, 1)
    )


SLOT = 32


def place_of(t, row):
    return t * 10 + row + 1


def packed(slabs, lane, base=0):
    out = jnp.zeros((LEVELS, LANES), jnp.float32)
    for i, slab in enumerate(slabs):
        place = base + place_of(i // LAT_CELLS, i % LAT_CELLS)
        out = jnp.where(lane_index() == place, rolled(slab, place - lane, 1), out)
    return out


def packed_wind(slabs, lane, base):
    one = packed(slabs, lane, base)
    return one + rolled(one, 10, 1) + rolled(one, 20, 1)


def slot(array, number):
    return rolled(array, -SLOT * number, 1)


def with_corners(own, south, north, number=0):
    row = (lane_index() & (SLOT - 1)) % 10
    out = jnp.where(row == 0, rolled(south, number - LAT_CELLS, 1), own)
    return jnp.where(row == 9, rolled(north, LAT_CELLS - number, 1), out)


def corners_body(from_west, from_east, up_ref, down_ref):
    row = (lane_index() & (SLOT - 1)) % 10
    up = jnp.zeros((LEVELS, LANES), jnp.float32)
    down = jnp.zeros((LEVELS, LANES), jnp.float32)
    for i in range(6):
        column = from_west[i] if i < 3 else from_east[i - 3]
        up = up + rolled(jnp.where(row == LAT_CELLS, column, 0.0), -i, 1)
        down = down + rolled(jnp.where(row == 1, column, 0.0), i, 1)
    up_ref[...] = up
    down_ref[...] = down


def mixed(slab, coeff):
    upward = coeff * (rolled(slab, -1, 0) - slab)
    return upward - rolled(upward, 1, 0)


def forward(slab, left, right, above, below, east, before, north, south, coeff):
    zonal = jnp.maximum(east, 0.0) * slab + jnp.minimum(east, 0.0) * right
    zonal_before = jnp.maximum(before, 0.0) * left + jnp.minimum(before, 0.0) * slab
    merid = jnp.maximum(north, 0.0) * slab + jnp.minimum(north, 0.0) * above
    merid_before = jnp.maximum(south, 0.0) * below + jnp.minimum(south, 0.0) * slab
    return slab - (zonal - zonal_before) - (merid - merid_before) + mixed(slab, coeff)


def backward(slab, left, right, above, below, east, before, north, south, coeff):
    zonal = jnp.maximum(east, 0.0) * (right - slab) + jnp.minimum(before, 0.0) * (slab - left)
    merid = jnp.maximum(north, 0.0) * (above - slab) + jnp.minimum(south, 0.0) * (slab - below)
    return slab + zonal + merid + mixed(slab, coeff)


def write_edges(read, up_ref, down_ref, east_edge, west_edge):
    slabs = [read(t, row) for t in range(TRACERS) for row in range(LAT_CELLS)]
    for t in range(TRACERS):
        for i in range(2):
            up_ref[2 * t + i] = slabs[t * LAT_CELLS + LAT_CELLS - 2 + i]
            down_ref[2 * t + i] = slabs[t * LAT_CELLS + i]
    east_edge[...] = packed(slabs, LANES - 1) + packed(slabs, LANES - 2, SLOT)
    west_edge[...] = packed(slabs, 0) + packed(slabs, 1, SLOT)


def arrange_body(
    last_ref, initial_ref, east_ref, north_ref, mixing_ref, state_ref, east_out, north_out, mixing_out
):
    for t in range(TRACERS):
        for row in range(LAT_CELLS):
            state_ref[t, row] = initial_ref[t, :, row, :]
    for m in range(east_ref.shape[0]):
        for row in range(LAT_CELLS):
            east_out[m, row] = east_ref[m, :, row, :]
            north_out[m, row] = masked_north(last_ref, north_ref, m, row)
            mixing_out[m, row] = masked_mixing(mixing_ref, m, row)


def masked_north(last_ref, north_ref, m, row):
    north = north_ref[m, :, row, :]
    if row == LAT_CELLS - 1:
        north = jnp.where(last_ref[0] > 0, jnp.float32(0.0), north)
    return north


def masked_mixing(mixing_ref, m, row):
    top = lax.broadcasted_iota(jnp.int32, (LEVELS, LANES), 0) == LEVELS - 1
    return jnp.where(top, jnp.float32(0.0), mixing_ref[m, :, row, :])


def edges_body(
    last_ref, initial_ref, east_ref, north_ref, mixing_ref, up_ref, down_ref, east_edge, west_edge
):
    last = LAT_CELLS - 1
    write_edges(
        lambda t, row: initial_ref[t, :, row, :], up_ref, down_ref, east_edge.at[0], west_edge.at[0]
    )
    for m in range(east_ref.shape[0]):
        east = [east_ref[m, :, row, :] for row in range(LAT_CELLS)]
        north = [masked_north(last_ref, north_ref, m, row) for row in range(LAT_CELLS)]
        mixing = [masked_mixing(mixing_ref, m, row) for row in range(LAT_CELLS)]
        for i, slab in enumerate((east[last], mixing[last], north[last], north[last - 1])):
            up_ref[6 + 4 * m + i] = slab
        for i, slab in enumerate((east[0], mixing[0], north[0])):
            down_ref[6 + 3 * m + i] = slab
        east_edge[1 + m] = (
            packed_wind(east, LANES - 1, 0)
            + packed_wind(mixing, LANES - 1, SLOT)
            + packed_wind(north, LANES - 1, 2 * SLOT)
            + packed_wind(east, LANES - 2, 3 * SLOT)
        )
        west_edge[1 + m] = (
            packed_wind(east, 0, 0)
            + packed_wind(mixing, 0, SLOT)
            + packed_wind(north, 0, 2 * SLOT)
        )


def two_steps(
    step, moments, read, winds, wind_up, wind_down, wind_east, sides,
    up_ref, down_ref, own_east, own_west, from_west, from_east, middle_ref, write,
):
    east_ref, north_ref, mixing_ref = winds

    def state(t, row):
        if row < 0:
            return up_ref[2 * t + row + 2]
        return read(t, row) if row < LAT_CELLS else down_ref[2 * t + row - LAT_CELLS]

    def wind(ref, number, m, row):
        if row < -1:
            return wind_up(4 * m + 3)
        if row < 0:
            return wind_up(4 * m + number)
        return ref[m, row] if row < LAT_CELLS else wind_down(3 * m + number)

    def winds_of(m, row, east_side):
        east = wind(east_ref, 0, m, row)
        return (
            east,
            west_of(east, east_side, place_of(0, row)),
            wind(north_ref, 2, m, row),
            wind(north_ref, 2, m, row - 1),
            wind(mixing_ref, 1, m, row),
        )

    m = moments[0]
    side_west, side_east = sides(m)
    for row in range(-1, LAT_CELLS + 1):
        local = winds_of(m, row, side_west)
        for t in range(TRACERS):
            slab, place = state(t, row), place_of(t, row)
            middle_ref[t, row + 1] = step(
                slab,
                west_of(slab, from_west, place),
                east_of(slab, from_east, place),
                state(t, row + 1),
                state(t, row - 1),
                *local,
            )

    def column(own, left, right, east, before, side):
        north = slot(side, 2)
        around = (rolled(own, -1, 1), rolled(own, 1, 1))
        return step(
            own, left, right, *around, east, before, north, rolled(north, 1, 1), slot(side, 1)
        )

    next_west = column(
        from_west, slot(from_west, 1), own_west, side_west, slot(side_west, 3), side_west
    )
    next_east = column(
        from_east, own_east, slot(from_east, 1), side_east, wind_east(m), side_east
    )
    m = moments[1]
    side_west, _ = sides(m)
    for row in range(LAT_CELLS):
        local = winds_of(m, row, side_west)
        for t in range(TRACERS):
            slab, place = middle_ref[t, row + 1], place_of(t, row)
            write(
                t,
                row,
                step(
                    slab,
                    west_of(slab, next_west, place),
                    east_of(slab, next_east, place),
                    middle_ref[t, row + 2],
                    middle_ref[t, row],
                    *local,
                ),
            )


def forward_body(
    state_ref, east_ref, north_ref, mixing_ref, own_east, own_west,
    up_ref, down_ref, from_west, from_east, south, north,
    field_ref, sides_ref, middle_ref, after_ref,
):
    for m in range(2):
        sides_ref[m, 0] = with_corners(from_west[1 + m], south[...], north[...], 1 + m)
        sides_ref[m, 1] = with_corners(from_east[1 + m], south[...], north[...], 4 + m)

    def write(t, row, slab):
        after_ref[t, row] = slab

    two_steps(
        forward,
        (0, 1),
        lambda t, row: state_ref[t, row],
        (east_ref, north_ref, mixing_ref),
        lambda i: up_ref[6 + i],
        lambda i: down_ref[6 + i],
        lambda m: own_east[1 + m],
        lambda m: (sides_ref[m, 0], sides_ref[m, 1]),
        up_ref,
        down_ref,
        own_east[0],
        own_west[0],
        with_corners(from_west[0], south[...], north[...], 0),
        with_corners(from_east[0], south[...], north[...], 3),
        middle_ref,
        write,
    )
    for i in range(6):
        for low_row in range(2):
            slabs = []
            for p in (2 * i, 2 * i + 1):
                slabs.append(after_ref[p // 4, (p % 4) * 2 + low_row])
            both = jnp.concatenate(slabs, axis=0)
            high = both.astype(jnp.bfloat16)
            low = (both - high.astype(jnp.float32)).astype(jnp.bfloat16)
            lanes = slice(low_row * LANES, (low_row + 1) * LANES)
            field_ref[2 * i * PAIR : (2 * i + 1) * PAIR, lanes] = high
            field_ref[(2 * i + 1) * PAIR : (2 * i + 2) * PAIR, lanes] = low


def cell_slab(ref, t, row):
    first = (t * 4 + row // 2) * LEVELS
    return ref[first : first + LEVELS, (row % 2) * LANES : (row % 2 + 1) * LANES]


def adjoint_body(
    adjoint_ref, east_ref, north_ref, mixing_ref, wind_up, wind_down, wind_east, sides_ref,
    own_east, own_west, from_west, from_east, up_ref, down_ref, gradient_ref, middle_ref,
):
    def write(t, row, slab):
        gradient_ref[t, :, row, :] = slab

    two_steps(
        backward,
        (1, 0),
        lambda t, row: cell_slab(adjoint_ref, t, row),
        (east_ref, north_ref, mixing_ref),
        lambda i: wind_up[6 + i],
        lambda i: wind_down[6 + i],
        lambda m: wind_east[1 + m],
        lambda m: (sides_ref[m, 0], sides_ref[m, 1]),
        up_ref,
        down_ref,
        own_east[...],
        own_west[...],
        with_corners(from_west[...], up_ref[6], down_ref[6]),
        with_corners(from_east[...], up_ref[7], down_ref[7]),
        middle_ref,
        write,
    )


STATE = jax.ShapeDtypeStruct((TRACERS, LAT_CELLS, LEVELS, LANES), jnp.float32)
ROW_EDGE = jax.ShapeDtypeStruct((2 * TRACERS, LEVELS, LANES), jnp.float32)
COLUMN_EDGE = jax.ShapeDtypeStruct((LEVELS, LANES), jnp.float32)
EDGES = [ROW_EDGE, ROW_EDGE, COLUMN_EDGE, COLUMN_EDGE]
MIDDLE = pltpu.VMEM((TRACERS, LAT_CELLS + 2, LEVELS, LANES), jnp.float32)


def whole(body, outs, operands, name, scratch=(), scalars=0, flops=5000000, scalar_outs=0, vmem_mib=56):
    smem = pl.BlockSpec(memory_space=pltpu.SMEM)

    def vmem(array):
        zeros = (0,) * len(array.shape)
        return pl.BlockSpec(array.shape, lambda i: zeros, pipeline_mode=pl.Buffered(1))

    return pl.pallas_call(
        body,
        grid=(1,),
        in_specs=[smem if i < scalars else vmem(a) for i, a in enumerate(operands)],
        out_specs=[vmem(a) if i < len(outs) - scalar_outs else smem for i, a in enumerate(outs)],
        out_shape=outs,
        scratch_shapes=list(scratch),
        compiler_params=pltpu.CompilerParams(vmem_limit_bytes=vmem_mib << 20),
        cost_estimate=pl.CostEstimate(flops=flops, bytes_accessed=6000000, transcendentals=0),
        name=name,
    )(*operands)


def shifted(array, lat_by, lon_by):
    lat, lon = lax.axis_size("lat"), lax.axis_size("lon")
    if not lat_by:
        return lax.ppermute(array, "lon", [(j, (j + lon_by) % lon) for j in range(lon)])
    rows = [(i, i + lat_by) for i in range(lat) if 0 <= i + lat_by < lat]
    if not lon_by:
        return lax.ppermute(array, "lat", rows)
    pairs = [(i * lon + j, k * lon + (j + lon_by) % lon) for i, k in rows for j in range(lon)]
    return lax.ppermute(array, ("lat", "lon"), pairs)


def plan(targets_ref, counts_ref, columns_ref, place_ref, first_ref, second_ref, tally_ref):
    def clear(device, carry):
        first_ref[device] = -1
        second_ref[device] = -1
        return carry

    lax.fori_loop(0, first_ref.shape[0], clear, 0, unroll=8)

    def name(block, carry):
        target = targets_ref[block]
        known = first_ref[target]
        second_ref[target] = jnp.where(known < 0, -1, block)
        first_ref[target] = jnp.where(known < 0, block, known)
        return carry

    lax.fori_loop(0, targets_ref.shape[0], name, 0, unroll=8)
    part_id = lax.broadcasted_iota(jnp.int32, (16, LANES), 0)
    group = lax.broadcasted_iota(jnp.int32, (16, LANES), 1) * GROUP_PARTS
    of_group = (part_id >= group) & (part_id < group + GROUP_PARTS)
    lane = lax.broadcasted_iota(jnp.int32, (1, LANES), 1)
    row_id = lax.broadcasted_iota(jnp.int32, (8, LANES), 0)
    square = (LANES, 2 * LANES)
    earlier = lax.broadcasted_iota(jnp.int32, square, 0) < lax.broadcasted_iota(
        jnp.int32, square, 1
    )
    earlier = jnp.where(earlier, 1.0, 0.0).astype(jnp.bfloat16)

    def rank(eight, carry):
        parts = lax.shift_right_logical(columns_ref[pl.ds(eight * 8, 8), :], 8)
        rows = [parts[j : j + 1] for j in range(8)]
        lives = [lane < counts_ref[eight * 8 + j] for j in range(8)]
        members = [
            jnp.where((part_id == row) & live, 1.0, 0.0) for row, live in zip(rows, lives)
        ]
        sums = jnp.dot(
            jnp.concatenate(members, axis=0).astype(jnp.bfloat16),
            earlier,
            preferred_element_type=jnp.float32,
        )
        places = jnp.zeros((8, LANES), jnp.float32)
        tallies = jnp.zeros((8, LANES), jnp.float32)
        for j in range(8):
            own = sums[16 * j : 16 * j + 16]
            before = jnp.where(
                part_id == rows[j],
                own[:, :LANES],
                jnp.where(part_id < rows[j], own[:, LANES:], jnp.float32(0.0)),
            )
            place = jnp.sum(before, axis=0, keepdims=True)
            place = jnp.where(lives[j], place, jnp.float32(LANES))
            places = jnp.where(row_id == j, place, places)
            tally = jnp.sum(jnp.where(of_group, own[:, LANES:], 0.0), axis=0, keepdims=True)
            tallies = jnp.where(row_id == j, tally, tallies)
        place_ref[pl.ds(eight * 8, 8), :] = places
        tally_ref[pl.ds(eight * 8, 8), :] = tallies
        return carry

    lax.fori_loop(0, targets_ref.shape[0] // 8, rank, 0, unroll=2)


def pack(
    source_ref, kernel_ref, columns_ref, observed_ref, weight_ref, place_ref, tally_ref, out_ref,
    observed_wide, weight_wide, order_ref,
):
    observed_wide[...] = observed_ref[...].astype(jnp.float32)
    weight_wide[...] = weight_ref[...].astype(jnp.float32)
    order_ref[...] = (
        lax.broadcasted_iota(jnp.int32, (LANES, LANES), 0).astype(jnp.float32).astype(jnp.bfloat16)
    )
    row_id = lax.broadcasted_iota(jnp.int32, (8, LANES), 0)
    one, nil = jnp.bfloat16(1), jnp.bfloat16(0)

    def sorted_block(slot):
        source = source_ref[slot]
        block = jnp.maximum(source, 0)
        row = pl.ds(block, 1)
        cell = columns_ref[row, :]
        part = lax.shift_right_logical(cell, 8) + 1
        meta = jnp.where(row_id == 0, part.astype(jnp.float32), jnp.float32(0.0))
        meta = jnp.where(row_id == 1, (cell & 255).astype(jnp.float32), meta)
        meta = jnp.where(row_id == 2, observed_wide[row, :], meta)
        meta = jnp.where(row_id == 3, weight_wide[row, :], meta)
        rows = jnp.concatenate([kernel_ref[block].astype(jnp.float32), meta], axis=0)
        place = jnp.where(source >= 0, place_ref[row, :], jnp.float32(LANES)).astype(jnp.bfloat16)
        moved = jnp.where(order_ref[...] == jnp.broadcast_to(place, (LANES, LANES)), one, nil)
        result = lax.dot_general(
            rows.astype(jnp.bfloat16),
            moved,
            (((1,), (1,)), ((), ())),
            preferred_element_type=jnp.float32,
        )
        tally = jnp.where(source >= 0, tally_ref[row, :], jnp.float32(0.0))
        meta = jnp.where(row_id == 4, tally, result[LEVELS:])
        return jnp.concatenate([result[:LEVELS], meta], axis=0).astype(jnp.bfloat16)

    together = 16

    def several(step, carry):
        blocks = [sorted_block(step * together + j) for j in range(together)]
        for j in range(together):
            out_ref[step * together + j] = blocks[j]
        return carry

    lax.fori_loop(0, out_ref.shape[0] // together, several, 0)


def pack_first_body(
    targets_ref, counts_ref, kernel_ref, columns_ref, observed_ref, weight_ref,
    out_ref, place_ref, tally_ref, first_ref, second_ref, *scratch,
):
    plan(targets_ref, counts_ref, columns_ref, place_ref, first_ref, second_ref, tally_ref)
    pack(
        first_ref, kernel_ref, columns_ref, observed_ref, weight_ref, place_ref, tally_ref, out_ref,
        *scratch,
    )


def innovations_body(first_ref, second_ref, returned_ref, place_ref, out_ref, rows_ref):
    def one(device, carry):
        for rank, source_ref in enumerate((first_ref, second_ref)):
            source = source_ref[device]
            block = jnp.where(source >= 0, source, LANES)
            rows_ref[pl.ds(block, 1), :] = returned_ref[pl.ds(2 * device + rank, 1), :]
        return carry

    lax.fori_loop(0, first_ref.shape[0], one, 0, unroll=8)
    place = place_ref[...].astype(jnp.int32)
    live = place < LANES
    found = jnp.take_along_axis(
        rows_ref[: place.shape[0], :], jnp.where(live, place, 0), axis=1
    )
    out_ref[...] = jnp.where(live, found, jnp.float32(0.0))


def soundings(
    field_ref, block_ref, adjoint_ref, write_misfit,
    stream_ref, found_ref, cell_ref, tally_ref, count_ref, sem,
):
    n = WIDTH * LANES
    one, nil = jnp.bfloat16(1), jnp.bfloat16(0)
    lane = lax.broadcasted_iota(jnp.int32, (ROWS, LANES), 1)
    cell_ref[...] = (
        lax.broadcasted_iota(jnp.int32, (256, LANES), 0).astype(jnp.float32).astype(jnp.bfloat16)
    )
    empty = jnp.zeros((ROWS, LANES), jnp.bfloat16)
    eighth = lax.broadcasted_iota(jnp.int32, (8, LANES), 0)

    def tally(eight, carry):
        rows = jnp.zeros((8, LANES), jnp.float32)
        for j in range(8):
            meta = block_ref[eight * 8 + j][LEVELS:].astype(jnp.float32)
            rows = jnp.where(eighth == j, meta[4:5], rows)
        tally_ref[pl.ds(eight * 8, 8), :] = rows.astype(jnp.int32)
        return carry

    lax.fori_loop(0, block_ref.shape[0] // 8, tally, 0, unroll=2)
    copy = pltpu.make_async_copy(tally_ref, count_ref, sem)
    copy.start()
    copy.wait()

    def merge(block, carry):
        ends, tails = list(carry[0]), list(carry[1])
        values = block_ref[block]
        start = jnp.int32(0)
        for g in range(GROUPS):
            count = count_ref[block, g]
            tile, at = lax.shift_right_logical(ends[g], 7), ends[g] & (LANES - 1)
            turned = pltpu.roll(values, (at - start) & (LANES - 1), 1)
            joined = jnp.where(lane >= at, turned, tails[g])
            stream_ref[g, tile] = joined
            tails[g] = jnp.where(at + count >= LANES, turned, joined)
            ends[g] = ends[g] + count
            start = start + count
        return tuple(ends), tuple(tails)

    ends, tails = lax.fori_loop(
        0,
        block_ref.shape[0],
        merge,
        ((jnp.int32(0),) * GROUPS, (empty,) * GROUPS),
        unroll=8,
    )
    for g in range(GROUPS):
        tile, at = lax.shift_right_logical(ends[g], 7), ends[g] & (LANES - 1)
        stream_ref[g, tile] = jnp.where(lane < at, tails[g], empty)
        for j in range(1, WIDTH):
            stream_ref[g, tile + j] = empty

    def load(g, step):
        tiles = [stream_ref[g, step * WIDTH + i] for i in range(WIDTH)]
        profile = jnp.concatenate([t[:LEVELS] for t in tiles], axis=1)
        meta = jnp.concatenate([t[LEVELS:] for t in tiles], axis=1).astype(jnp.float32)
        part, cell, observed, weight = (meta[j : j + 1] for j in range(4))
        cell = cell.astype(jnp.bfloat16)
        hits = [
            cell_ref[...] == jnp.broadcast_to(cell[:, i * LANES : (i + 1) * LANES], (256, LANES))
            for i in range(WIDTH)
        ]
        pick = jnp.concatenate([jnp.where(hit, one, nil) for hit in hits], axis=1)
        return g, step, profile, part - 1.0, observed, weight, pick

    def gather(g, step, profile, part, observed, weight, pick):
        column = jnp.zeros((LEVELS, n), jnp.float32)
        for i in range(g * GROUP_PARTS // 2, (g + 1) * GROUP_PARTS // 2):
            found = jnp.dot(
                field_ref[2 * i * PAIR : 2 * (i + 1) * PAIR, :],
                pick,
                preferred_element_type=jnp.float32,
            )
            found = found[:PAIR] + found[PAIR:]
            column = jnp.where(part == 2.0 * i, found[:LEVELS], column)
            column = jnp.where(part == 2.0 * i + 1.0, found[LEVELS:], column)
        return column

    def force(column, g, step, profile, part, observed, weight, pick):
        wide = profile.astype(jnp.float32)
        model = jnp.sum(wide * column, axis=0, keepdims=True)
        misfit = model - observed
        for i in range(WIDTH):
            found_ref[g, step * WIDTH + i] = jnp.broadcast_to(
                misfit[:, i * LANES : (i + 1) * LANES], (8, LANES)
            )
        vector = wide * (weight * misfit)
        high = vector.astype(jnp.bfloat16)
        return high, (vector - high.astype(jnp.float32)).astype(jnp.bfloat16)

    def scatter(vector, g, step, profile, part, observed, weight, pick):
        high, low = (jnp.concatenate([term, term], axis=0) for term in vector)
        second = lax.broadcasted_iota(jnp.int32, (PAIR, n), 0) >= LEVELS
        part_row = (part - jnp.where(second, 1.0, 0.0)).astype(jnp.bfloat16)
        for i in range(g * GROUP_PARTS // 2, (g + 1) * GROUP_PARTS // 2):
            own = part_row == jnp.bfloat16(2 * i)
            sums = lax.dot_general(
                jnp.concatenate([jnp.where(own, high, nil), jnp.where(own, low, nil)], axis=0),
                pick,
                (((1,), (1,)), ((), ())),
                preferred_element_type=jnp.float32,
            )
            adjoint_ref[i * PAIR : (i + 1) * PAIR, :] += sums[:PAIR] + sums[PAIR:]

    def work(groups, step):
        loaded = [load(g, step) for g in groups]
        columns = [gather(*x) for x in loaded]
        vectors = [force(column, *x) for x, column in zip(loaded, columns)]
        for x, vector in zip(loaded, vectors):
            scatter(vector, *x)
        return 0

    steps = [lax.shift_right_logical(ends[g] + n - 1, n.bit_length() - 1) for g in range(GROUPS)]
    common = functools.reduce(jnp.minimum, steps)
    lax.fori_loop(0, common, lambda step, _: work(range(GROUPS), step), 0)
    for g in range(GROUPS):
        lax.fori_loop(common, steps[g], lambda step, _, g=g: work([g], step), 0)

    lane = lax.broadcasted_iota(jnp.int32, (8, LANES), 1)
    row_id = lax.broadcasted_iota(jnp.int32, (8, LANES), 0)

    def part_ways(eight, ends):
        ends = list(ends)
        rows = jnp.zeros((8, LANES), jnp.float32)
        for j in range(8):
            start = jnp.int32(0)
            row = jnp.zeros((8, LANES), jnp.float32)
            for g in range(GROUPS):
                count = count_ref[eight * 8 + j, g]
                tile, at = lax.shift_right_logical(ends[g], 7), ends[g] & (LANES - 1)
                values = jnp.where(lane >= at, found_ref[g, tile], found_ref[g, tile + 1])
                values = pltpu.roll(values, (start - at) & (LANES - 1), 1)
                row = jnp.where(lane >= start, values, row)
                ends[g] = ends[g] + count
                start = start + count
            rows = jnp.where(row_id == j, row, rows)
        write_misfit(eight, rows)
        return tuple(ends)

    lax.fori_loop(0, block_ref.shape[0] // 8, part_ways, (jnp.int32(0),) * GROUPS)


def first_soundings_body(field_ref, block_ref, adjoint_ref, misfit_ref, *scratch):
    adjoint_ref[...] = jnp.zeros_like(adjoint_ref)

    def write_misfit(eight, rows):
        misfit_ref[pl.ds(eight * 8, 8), :] = rows

    soundings(field_ref, block_ref, adjoint_ref, write_misfit, *scratch)


def second_soundings_body(
    field_ref, block_ref, earlier_ref, other_ref, adjoint_ref, misfit_ref, *rest
):
    edges, scratch = rest[:4], rest[4:]
    adjoint_ref[...] = earlier_ref[...]

    def write_misfit(eight, rows):
        misfit_ref[pl.ds(eight * 16, 8, stride=2), :] = other_ref[pl.ds(eight * 8, 8), :]
        misfit_ref[pl.ds(eight * 16 + 1, 8, stride=2), :] = rows

    soundings(field_ref, block_ref, adjoint_ref, write_misfit, *scratch)
    write_edges(lambda t, row: cell_slab(adjoint_ref, t, row), *edges)


def observe(field, blocks, earlier=()):
    count = blocks.shape[0]
    tiles = count + WIDTH
    outs = [jax.ShapeDtypeStruct((PARTS * LEVELS, 256), jnp.float32)]
    outs += [jax.ShapeDtypeStruct((count * (2 if earlier else 1), LANES), jnp.float32)]
    return whole(
        second_soundings_body if earlier else first_soundings_body,
        outs + (EDGES if earlier else []),
        (field, blocks) + tuple(earlier),
        "second_soundings" if earlier else "first_soundings",
        scratch=[
            pltpu.VMEM((GROUPS, tiles, ROWS, LANES), jnp.bfloat16),
            pltpu.VMEM((GROUPS, tiles, 8, LANES), jnp.float32),
            pltpu.VMEM((256, LANES), jnp.bfloat16),
            pltpu.VMEM((count, LANES), jnp.int32),
            pltpu.SMEM((count, LANES), jnp.int32),
            pltpu.SemaphoreType.DMA(()),
        ],
        flops=15000000000,
    )


def per_device(
    initial, east_wind, north_wind, mixing, kernel, columns, observed, obs_weight, counts, targets
):
    lat_count = lax.axis_size("lat")
    lon_count = lax.axis_size("lon")
    sounds = kernel.shape[2]
    block_count = kernel.shape[0]
    device_count = lat_count * lon_count

    def exchange(array):
        return lax.all_to_all(array, ("lat", "lon"), split_axis=0, concat_axis=0, tiled=True)

    is_last = (lax.axis_index("lat") == lat_count - 1).astype(jnp.int32).reshape(1)
    winds_like = jax.ShapeDtypeStruct((2, LAT_CELLS, LEVELS, LANES), jnp.float32)

    def slabs_like(number):
        return jax.ShapeDtypeStruct((number, LEVELS, LANES), jnp.float32)

    grid = (is_last, initial, east_wind, north_wind, mixing)
    up, down, east, west = whole(
        edges_body,
        [slabs_like(14), slabs_like(12), slabs_like(3), slabs_like(3)],
        grid,
        "edges",
        scalars=1,
    )
    counts, up, down, east, west = lax.optimization_barrier((counts, up, down, east, west))
    from_south, from_north = shifted(up, 1, 0), shifted(down, -1, 0)
    slots = jax.ShapeDtypeStruct((device_count, ROWS, sounds), jnp.bfloat16)
    by_device = jax.ShapeDtypeStruct((device_count,), jnp.int32)
    heard = (kernel, columns, observed, obs_weight)
    scratch = [pltpu.VMEM((block_count, sounds), jnp.float32)] * 2
    scratch += [pltpu.VMEM((LANES, LANES), jnp.bfloat16)]
    by_block = jax.ShapeDtypeStruct((block_count, sounds), jnp.float32)
    out_first, place, tally, source_first, source_second = whole(
        pack_first_body,
        [slots, by_block, by_block, by_device, by_device],
        (targets[:, 0], counts) + heard,
        "pack_first",
        scratch=scratch,
        scalars=2,
        scalar_outs=2,
    )
    (out_second,) = whole(
        pack, [slots], (source_second,) + heard + (place, tally), "pack_second", scratch=scratch,
        scalars=1,
    )
    sides = (shifted(east, 0, 1), shifted(west, 0, -1))
    out_first, from_south, from_north, *sides = lax.optimization_barrier(
        (out_first, from_south, from_north, *sides)
    )
    got_first = exchange(out_first)
    corner_up, corner_down = whole(corners_body, [COLUMN_EDGE] * 2, tuple(sides), "corners")
    sides += [shifted(corner_up, 1, 0), shifted(corner_down, -1, 0)]
    grid = lax.optimization_barrier((corner_up,) + grid)[1:]
    arranged = whole(
        arrange_body, [STATE, winds_like, winds_like, winds_like], grid, "arrange", scalars=1
    )
    out_second, *rest = lax.optimization_barrier((out_second, *sides, *arranged))
    got_second = exchange(out_second)
    sides, state, fields = rest[:4], rest[4], tuple(rest[5:])
    field, wind_sides = whole(
        forward_body,
        [
            jax.ShapeDtypeStruct((2 * PARTS * LEVELS, 256), jnp.bfloat16),
            jax.ShapeDtypeStruct((2, 2, LEVELS, LANES), jnp.float32),
        ],
        (state,) + fields + (east, west, from_south, from_north) + tuple(sides),
        "forward",
        scratch=[MIDDLE, pltpu.VMEM(STATE.shape, jnp.float32)],
    )
    earlier = observe(field, got_first)
    adjoint, misfit, up, down, own_east, own_west = observe(field, got_second, earlier)
    from_west, from_east = shifted(own_east, 0, 1), shifted(own_west, 0, -1)
    ends = jnp.stack([from_west, from_east])
    returned = exchange(misfit)
    (gradient,) = whole(
        adjoint_body,
        [jax.ShapeDtypeStruct(initial.shape, jnp.float32)],
        (adjoint,) + fields + (from_south, from_north, east, wind_sides)
        + (own_east, own_west, from_west, from_east)
        + (shifted(jnp.concatenate([up, ends]), 1, 0), shifted(jnp.concatenate([down, ends]), -1, 0)),
        "adjoint",
        scratch=[MIDDLE],
    )
    returned, gradient = lax.optimization_barrier((returned, gradient))
    (innovations,) = whole(
        innovations_body,
        [jax.ShapeDtypeStruct((block_count, sounds), jnp.float32)],
        (source_first, source_second, returned, place),
        "innovations",
        scratch=[pltpu.VMEM((block_count + 8, sounds), jnp.float32)],
        scalars=2,
    )
    return (gradient, innovations)


def solution(mesh):
    return jax.shard_map(
        per_device,
        mesh=mesh,
        in_specs=(
            P(None, None, "lat", "lon"),
            P(None, None, "lat", "lon"),
            P(None, None, "lat", "lon"),
            P(None, None, "lat", "lon"),
            P(("lat", "lon"), None, None),
            P(("lat", "lon"), None),
            P(("lat", "lon"), None),
            P(("lat", "lon"), None),
            P(("lat", "lon")),
            P(("lat", "lon"), None),
        ),
        out_specs=(P(None, None, "lat", "lon"), P(("lat", "lon"), None)),
        check_vma=False,
    )
```

```python
import functools

import jax
import jax.numpy as jnp
from jax import lax
from jax.experimental import pallas as pl
from jax.experimental.pallas import tpu as pltpu
from jax.sharding import PartitionSpec as P

LEVELS = 72
ROWS = 80
PAIR = 2 * LEVELS
TRACERS = 3
PARTS = 12
GROUPS = 6
GROUP_PARTS = PARTS // GROUPS
WIDTH = 2
LAT_CELLS = 8
LANES = 128


def lane_index():
    return lax.broadcasted_iota(jnp.int32, (LEVELS, LANES), 1)


def rolled(array, shift, axis):
    shift = shift % array.shape[axis]
    return pltpu.roll(array, shift, axis) if shift else array


def west_of(slab, halo, place):
    return jnp.where(lane_index() == 0, rolled(halo, -place, 1), rolled(slab, 1, 1))


def east_of(slab, halo, place):
    return jnp.where(
        lane_index() == LANES - 1, rolled(halo, LANES - 1 - place, 1), rolled(slab, -1, 1)
    )


SLOT = 32


def place_of(t, row):
    return t * 10 + row + 1


def packed(slabs, lane, base=0, first_row=0, rows=LAT_CELLS):
    out = jnp.zeros((LEVELS, LANES), jnp.float32)
    for i, slab in enumerate(slabs):
        place = base + place_of(i // rows, first_row + i % rows)
        out = jnp.where(lane_index() == place, rolled(slab, place - lane, 1), out)
    return out


def packed_wind(slabs, lane, base):
    one = packed(slabs, lane, base, -1, LAT_CELLS + 2)
    return one + rolled(one, 10, 1) + rolled(one, 20, 1)


def slot(array, number):
    return rolled(array, -SLOT * number, 1)


def with_corners(own, south, north):
    row = (lane_index() & (SLOT - 1)) % 10
    out = jnp.where(row == 0, rolled(south, -LAT_CELLS, 1), own)
    return jnp.where(row == 9, rolled(north, LAT_CELLS, 1), out)


def mixed(slab, coeff):
    upward = coeff * (rolled(slab, -1, 0) - slab)
    return upward - rolled(upward, 1, 0)


def forward(slab, left, right, above, below, east, before, north, south, coeff):
    zonal = jnp.maximum(east, 0.0) * slab + jnp.minimum(east, 0.0) * right
    zonal_before = jnp.maximum(before, 0.0) * left + jnp.minimum(before, 0.0) * slab
    merid = jnp.maximum(north, 0.0) * slab + jnp.minimum(north, 0.0) * above
    merid_before = jnp.maximum(south, 0.0) * below + jnp.minimum(south, 0.0) * slab
    return slab - (zonal - zonal_before) - (merid - merid_before) + mixed(slab, coeff)


def backward(slab, left, right, above, below, east, before, north, south, coeff):
    zonal = jnp.maximum(east, 0.0) * (right - slab) + jnp.minimum(before, 0.0) * (slab - left)
    merid = jnp.maximum(north, 0.0) * (above - slab) + jnp.minimum(south, 0.0) * (slab - below)
    return slab + zonal + merid + mixed(slab, coeff)


def write_edges(read, up_ref, down_ref, east_edge, west_edge):
    slabs = [read(t, row) for t in range(TRACERS) for row in range(LAT_CELLS)]
    for t in range(TRACERS):
        for i in range(2):
            up_ref[2 * t + i] = slabs[t * LAT_CELLS + LAT_CELLS - 2 + i]
            down_ref[2 * t + i] = slabs[t * LAT_CELLS + i]
    east_edge[...] = packed(slabs, LANES - 1) + packed(slabs, LANES - 2, SLOT)
    west_edge[...] = packed(slabs, 0) + packed(slabs, 1, SLOT)


def arrange_body(
    last_ref, initial_ref, east_ref, north_ref, mixing_ref, up_ref, down_ref,
    state_ref, east_out, north_out, mixing_out, east_edge, west_edge,
):
    slabs = []
    for t in range(TRACERS):
        slabs.append(up_ref[2 * t + 1])
        for row in range(LAT_CELLS):
            state_ref[t, row] = initial_ref[t, :, row, :]
            slabs.append(state_ref[t, row])
        slabs.append(down_ref[2 * t])
    rows = LAT_CELLS + 2
    east_edge[0] = packed(slabs, LANES - 1, 0, -1, rows) + packed(slabs, LANES - 2, SLOT, -1, rows)
    west_edge[0] = packed(slabs, 0, 0, -1, rows) + packed(slabs, 1, SLOT, -1, rows)
    for m in range(east_ref.shape[0]):
        for row in range(LAT_CELLS):
            east_out[m, row] = east_ref[m, :, row, :]
            north_out[m, row] = masked_north(last_ref, north_ref, m, row)
            mixing_out[m, row] = masked_mixing(mixing_ref, m, row)

        def column(ref, number):
            own = [ref[m, row] for row in range(LAT_CELLS)]
            return [up_ref[6 + 4 * m + number]] + own + [down_ref[6 + 3 * m + number]]

        east, mixing, north = column(east_out, 0), column(mixing_out, 1), column(north_out, 2)
        east_edge[1 + m] = (
            packed_wind(east, LANES - 1, 0)
            + packed_wind(mixing, LANES - 1, SLOT)
            + packed_wind(north, LANES - 1, 2 * SLOT)
            + packed_wind(east, LANES - 2, 3 * SLOT)
        )
        west_edge[1 + m] = (
            packed_wind(east, 0, 0)
            + packed_wind(mixing, 0, SLOT)
            + packed_wind(north, 0, 2 * SLOT)
        )


def masked_north(last_ref, north_ref, m, row):
    north = north_ref[m, :, row, :]
    if row == LAT_CELLS - 1:
        north = jnp.where(last_ref[0] > 0, jnp.float32(0.0), north)
    return north


def masked_mixing(mixing_ref, m, row):
    top = lax.broadcasted_iota(jnp.int32, (LEVELS, LANES), 0) == LEVELS - 1
    return jnp.where(top, jnp.float32(0.0), mixing_ref[m, :, row, :])


def rows_body(last_ref, initial_ref, east_ref, north_ref, mixing_ref, up_ref, down_ref):
    last = LAT_CELLS - 1
    for t in range(TRACERS):
        for i in range(2):
            up_ref[2 * t + i] = initial_ref[t, :, LAT_CELLS - 2 + i, :]
            down_ref[2 * t + i] = initial_ref[t, :, i, :]
    for m in range(east_ref.shape[0]):
        up_ref[6 + 4 * m] = east_ref[m, :, last, :]
        up_ref[7 + 4 * m] = masked_mixing(mixing_ref, m, last)
        up_ref[8 + 4 * m] = masked_north(last_ref, north_ref, m, last)
        up_ref[9 + 4 * m] = masked_north(last_ref, north_ref, m, last - 1)
        down_ref[6 + 3 * m] = east_ref[m, :, 0, :]
        down_ref[7 + 3 * m] = masked_mixing(mixing_ref, m, 0)
        down_ref[8 + 3 * m] = masked_north(last_ref, north_ref, m, 0)


def two_steps(
    step, moments, read, winds, wind_up, wind_down, wind_east, sides,
    up_ref, down_ref, own_east, own_west, from_west, from_east, middle_ref, write,
):
    east_ref, north_ref, mixing_ref = winds

    def state(t, row):
        if row < 0:
            return up_ref[2 * t + row + 2]
        return read(t, row) if row < LAT_CELLS else down_ref[2 * t + row - LAT_CELLS]

    def wind(ref, number, m, row):
        if row < -1:
            return wind_up(4 * m + 3)
        if row < 0:
            return wind_up(4 * m + number)
        return ref[m, row] if row < LAT_CELLS else wind_down(3 * m + number)

    def winds_of(m, row, east_side):
        east = wind(east_ref, 0, m, row)
        return (
            east,
            west_of(east, east_side, place_of(0, row)),
            wind(north_ref, 2, m, row),
            wind(north_ref, 2, m, row - 1),
            wind(mixing_ref, 1, m, row),
        )

    m = moments[0]
    side_west, side_east = sides(m)
    for row in range(-1, LAT_CELLS + 1):
        local = winds_of(m, row, side_west)
        for t in range(TRACERS):
            slab, place = state(t, row), place_of(t, row)
            middle_ref[t, row + 1] = step(
                slab,
                west_of(slab, from_west, place),
                east_of(slab, from_east, place),
                state(t, row + 1),
                state(t, row - 1),
                *local,
            )

    def column(own, left, right, east, before, side):
        north = slot(side, 2)
        around = (rolled(own, -1, 1), rolled(own, 1, 1))
        return step(
            own, left, right, *around, east, before, north, rolled(north, 1, 1), slot(side, 1)
        )

    next_west = column(
        from_west, slot(from_west, 1), own_west, side_west, slot(side_west, 3), side_west
    )
    next_east = column(
        from_east, own_east, slot(from_east, 1), side_east, wind_east(m), side_east
    )
    m = moments[1]
    side_west, _ = sides(m)
    for row in range(LAT_CELLS):
        local = winds_of(m, row, side_west)
        for t in range(TRACERS):
            slab, place = middle_ref[t, row + 1], place_of(t, row)
            write(
                t,
                row,
                step(
                    slab,
                    west_of(slab, next_west, place),
                    east_of(slab, next_east, place),
                    middle_ref[t, row + 2],
                    middle_ref[t, row],
                    *local,
                ),
            )


def forward_body(
    state_ref, east_ref, north_ref, mixing_ref, own_east, own_west,
    up_ref, down_ref, from_west, from_east, field_ref, middle_ref, after_ref,
):
    def write(t, row, slab):
        after_ref[t, row] = slab

    two_steps(
        forward,
        (0, 1),
        lambda t, row: state_ref[t, row],
        (east_ref, north_ref, mixing_ref),
        lambda i: up_ref[6 + i],
        lambda i: down_ref[6 + i],
        lambda m: own_east[1 + m],
        lambda m: (from_west[1 + m], from_east[1 + m]),
        up_ref,
        down_ref,
        own_east[0],
        own_west[0],
        from_west[0],
        from_east[0],
        middle_ref,
        write,
    )
    for i in range(6):
        for low_row in range(2):
            slabs = []
            for p in (2 * i, 2 * i + 1):
                slabs.append(after_ref[p // 4, (p % 4) * 2 + low_row])
            both = jnp.concatenate(slabs, axis=0)
            high = both.astype(jnp.bfloat16)
            low = (both - high.astype(jnp.float32)).astype(jnp.bfloat16)
            lanes = slice(low_row * LANES, (low_row + 1) * LANES)
            field_ref[2 * i * PAIR : (2 * i + 1) * PAIR, lanes] = high
            field_ref[(2 * i + 1) * PAIR : (2 * i + 2) * PAIR, lanes] = low


def cell_slab(ref, t, row):
    first = (t * 4 + row // 2) * LEVELS
    return ref[first : first + LEVELS, (row % 2) * LANES : (row % 2 + 1) * LANES]


def adjoint_body(
    adjoint_ref, east_ref, north_ref, mixing_ref, wind_up, wind_down, wind_east, side_west, side_east,
    own_east, own_west, from_west, from_east, up_ref, down_ref, gradient_ref, middle_ref,
):
    def write(t, row, slab):
        gradient_ref[t, :, row, :] = slab

    two_steps(
        backward,
        (1, 0),
        lambda t, row: cell_slab(adjoint_ref, t, row),
        (east_ref, north_ref, mixing_ref),
        lambda i: wind_up[6 + i],
        lambda i: wind_down[6 + i],
        lambda m: wind_east[1 + m],
        lambda m: (side_west[1 + m], side_east[1 + m]),
        up_ref,
        down_ref,
        own_east[...],
        own_west[...],
        with_corners(from_west[...], up_ref[6], down_ref[6]),
        with_corners(from_east[...], up_ref[7], down_ref[7]),
        middle_ref,
        write,
    )


STATE = jax.ShapeDtypeStruct((TRACERS, LAT_CELLS, LEVELS, LANES), jnp.float32)
ROW_EDGE = jax.ShapeDtypeStruct((2 * TRACERS, LEVELS, LANES), jnp.float32)
COLUMN_EDGE = jax.ShapeDtypeStruct((LEVELS, LANES), jnp.float32)
EDGES = [ROW_EDGE, ROW_EDGE, COLUMN_EDGE, COLUMN_EDGE]
MIDDLE = pltpu.VMEM((TRACERS, LAT_CELLS + 2, LEVELS, LANES), jnp.float32)


def whole(body, outs, operands, name, scratch=(), scalars=0, flops=5000000, scalar_outs=0, vmem_mib=63):
    smem = pl.BlockSpec(memory_space=pltpu.SMEM)

    def vmem(array):
        zeros = (0,) * len(array.shape)
        return pl.BlockSpec(array.shape, lambda i: zeros, pipeline_mode=pl.Buffered(1))

    return pl.pallas_call(
        body,
        grid=(1,),
        in_specs=[smem if i < scalars else vmem(a) for i, a in enumerate(operands)],
        out_specs=[vmem(a) if i < len(outs) - scalar_outs else smem for i, a in enumerate(outs)],
        out_shape=outs,
        scratch_shapes=list(scratch),
        compiler_params=pltpu.CompilerParams(vmem_limit_bytes=vmem_mib << 20),
        cost_estimate=pl.CostEstimate(flops=flops, bytes_accessed=6000000, transcendentals=0),
        name=name,
    )(*operands)


def shifted(array, lat_by, lon_by):
    lat, lon = lax.axis_size("lat"), lax.axis_size("lon")
    if not lat_by:
        return lax.ppermute(array, "lon", [(j, (j + lon_by) % lon) for j in range(lon)])
    rows = [(i, i + lat_by) for i in range(lat) if 0 <= i + lat_by < lat]
    if not lon_by:
        return lax.ppermute(array, "lat", rows)
    pairs = [(i * lon + j, k * lon + (j + lon_by) % lon) for i, k in rows for j in range(lon)]
    return lax.ppermute(array, ("lat", "lon"), pairs)


def plan(targets_ref, counts_ref, columns_ref, place_ref, first_ref, second_ref, tally_ref):
    def clear(device, carry):
        first_ref[device] = -1
        second_ref[device] = -1
        return carry

    lax.fori_loop(0, first_ref.shape[0], clear, 0, unroll=8)

    def name(block, carry):
        target = targets_ref[block]
        known = first_ref[target]
        second_ref[target] = jnp.where(known < 0, -1, block)
        first_ref[target] = jnp.where(known < 0, block, known)
        return carry

    lax.fori_loop(0, targets_ref.shape[0], name, 0, unroll=8)
    part_id = lax.broadcasted_iota(jnp.int32, (16, LANES), 0)
    group = lax.broadcasted_iota(jnp.int32, (16, LANES), 1) * GROUP_PARTS
    of_group = (part_id >= group) & (part_id < group + GROUP_PARTS)
    lane = lax.broadcasted_iota(jnp.int32, (1, LANES), 1)
    row_id = lax.broadcasted_iota(jnp.int32, (8, LANES), 0)
    square = (LANES, 2 * LANES)
    earlier = lax.broadcasted_iota(jnp.int32, square, 0) < lax.broadcasted_iota(
        jnp.int32, square, 1
    )
    earlier = jnp.where(earlier, 1.0, 0.0).astype(jnp.bfloat16)

    def rank(eight, carry):
        parts = lax.shift_right_logical(columns_ref[pl.ds(eight * 8, 8), :], 8)
        rows = [parts[j : j + 1] for j in range(8)]
        lives = [lane < counts_ref[eight * 8 + j] for j in range(8)]
        members = [
            jnp.where((part_id == row) & live, 1.0, 0.0) for row, live in zip(rows, lives)
        ]
        sums = jnp.dot(
            jnp.concatenate(members, axis=0).astype(jnp.bfloat16),
            earlier,
            preferred_element_type=jnp.float32,
        )
        places = jnp.zeros((8, LANES), jnp.float32)
        tallies = jnp.zeros((8, LANES), jnp.float32)
        for j in range(8):
            own = sums[16 * j : 16 * j + 16]
            before = jnp.where(
                part_id == rows[j],
                own[:, :LANES],
                jnp.where(part_id < rows[j], own[:, LANES:], jnp.float32(0.0)),
            )
            place = jnp.sum(before, axis=0, keepdims=True)
            place = jnp.where(lives[j], place, jnp.float32(LANES))
            places = jnp.where(row_id == j, place, places)
            tally = jnp.sum(jnp.where(of_group, own[:, LANES:], 0.0), axis=0, keepdims=True)
            tallies = jnp.where(row_id == j, tally, tallies)
        place_ref[pl.ds(eight * 8, 8), :] = places
        tally_ref[pl.ds(eight * 8, 8), :] = tallies
        return carry

    lax.fori_loop(0, targets_ref.shape[0] // 8, rank, 0, unroll=2)


def pack(
    source_ref, kernel_ref, columns_ref, observed_ref, weight_ref, place_ref, tally_ref, out_ref,
    observed_wide, weight_wide, order_ref,
):
    observed_wide[...] = observed_ref[...].astype(jnp.float32)
    weight_wide[...] = weight_ref[...].astype(jnp.float32)
    order_ref[...] = (
        lax.broadcasted_iota(jnp.int32, (LANES, LANES), 0).astype(jnp.float32).astype(jnp.bfloat16)
    )
    row_id = lax.broadcasted_iota(jnp.int32, (8, LANES), 0)
    one, nil = jnp.bfloat16(1), jnp.bfloat16(0)

    def sorted_block(slot):
        source = source_ref[slot]
        block = jnp.maximum(source, 0)
        row = pl.ds(block, 1)
        cell = columns_ref[row, :]
        part = lax.shift_right_logical(cell, 8) + 1
        meta = jnp.where(row_id == 0, part.astype(jnp.float32), jnp.float32(0.0))
        meta = jnp.where(row_id == 1, (cell & 255).astype(jnp.float32), meta)
        meta = jnp.where(row_id == 2, observed_wide[row, :], meta)
        meta = jnp.where(row_id == 3, weight_wide[row, :], meta)
        rows = jnp.concatenate([kernel_ref[block].astype(jnp.float32), meta], axis=0)
        place = jnp.where(source >= 0, place_ref[row, :], jnp.float32(LANES)).astype(jnp.bfloat16)
        moved = jnp.where(order_ref[...] == jnp.broadcast_to(place, (LANES, LANES)), one, nil)
        result = lax.dot_general(
            rows.astype(jnp.bfloat16),
            moved,
            (((1,), (1,)), ((), ())),
            preferred_element_type=jnp.float32,
        )
        tally = jnp.where(source >= 0, tally_ref[row, :], jnp.float32(0.0))
        meta = jnp.where(row_id == 4, tally, result[LEVELS:])
        return jnp.concatenate([result[:LEVELS], meta], axis=0).astype(jnp.bfloat16)

    together = 16

    def several(step, carry):
        blocks = [sorted_block(step * together + j) for j in range(together)]
        for j in range(together):
            out_ref[step * together + j] = blocks[j]
        return carry

    lax.fori_loop(0, out_ref.shape[0] // together, several, 0)


def pack_first_body(
    targets_ref, counts_ref, kernel_ref, columns_ref, observed_ref, weight_ref,
    out_ref, place_ref, tally_ref, first_ref, second_ref, *scratch,
):
    plan(targets_ref, counts_ref, columns_ref, place_ref, first_ref, second_ref, tally_ref)
    pack(
        first_ref, kernel_ref, columns_ref, observed_ref, weight_ref, place_ref, tally_ref, out_ref,
        *scratch,
    )


def innovations_body(first_ref, second_ref, returned_ref, place_ref, out_ref, rows_ref):
    def one(device, carry):
        for rank, source_ref in enumerate((first_ref, second_ref)):
            source = source_ref[device]
            block = jnp.where(source >= 0, source, LANES)
            rows_ref[pl.ds(block, 1), :] = returned_ref[pl.ds(2 * device + rank, 1), :]
        return carry

    lax.fori_loop(0, first_ref.shape[0], one, 0, unroll=8)
    place = place_ref[...].astype(jnp.int32)
    live = place < LANES
    found = jnp.take_along_axis(
        rows_ref[: place.shape[0], :], jnp.where(live, place, 0), axis=1
    )
    out_ref[...] = jnp.where(live, found, jnp.float32(0.0))


def soundings(
    field_ref, block_ref, adjoint_ref, write_misfit,
    stream_ref, found_ref, cell_ref, tally_ref, count_ref, sem,
):
    n = WIDTH * LANES
    one, nil = jnp.bfloat16(1), jnp.bfloat16(0)
    lane = lax.broadcasted_iota(jnp.int32, (ROWS, LANES), 1)
    cell_ref[...] = (
        lax.broadcasted_iota(jnp.int32, (256, LANES), 0).astype(jnp.float32).astype(jnp.bfloat16)
    )
    empty = jnp.zeros((ROWS, LANES), jnp.bfloat16)
    eighth = lax.broadcasted_iota(jnp.int32, (8, LANES), 0)

    def tally(eight, carry):
        rows = jnp.zeros((8, LANES), jnp.float32)
        for j in range(8):
            meta = block_ref[eight * 8 + j][LEVELS:].astype(jnp.float32)
            rows = jnp.where(eighth == j, meta[4:5], rows)
        tally_ref[pl.ds(eight * 8, 8), :] = rows.astype(jnp.int32)
        return carry

    lax.fori_loop(0, block_ref.shape[0] // 8, tally, 0, unroll=2)
    copy = pltpu.make_async_copy(tally_ref, count_ref, sem)
    copy.start()
    copy.wait()

    def merge(block, carry):
        ends, tails = list(carry[0]), list(carry[1])
        values = block_ref[block]
        start = jnp.int32(0)
        for g in range(GROUPS):
            count = count_ref[block, g]
            tile, at = lax.shift_right_logical(ends[g], 7), ends[g] & (LANES - 1)
            turned = pltpu.roll(values, (at - start) & (LANES - 1), 1)
            joined = jnp.where(lane >= at, turned, tails[g])
            stream_ref[g, tile] = joined
            tails[g] = jnp.where(at + count >= LANES, turned, joined)
            ends[g] = ends[g] + count
            start = start + count
        return tuple(ends), tuple(tails)

    ends, tails = lax.fori_loop(
        0,
        block_ref.shape[0],
        merge,
        ((jnp.int32(0),) * GROUPS, (empty,) * GROUPS),
        unroll=8,
    )
    for g in range(GROUPS):
        tile, at = lax.shift_right_logical(ends[g], 7), ends[g] & (LANES - 1)
        stream_ref[g, tile] = jnp.where(lane < at, tails[g], empty)
        for j in range(1, WIDTH):
            stream_ref[g, tile + j] = empty

    def load(g, step):
        tiles = [stream_ref[g, step * WIDTH + i] for i in range(WIDTH)]
        profile = jnp.concatenate([t[:LEVELS] for t in tiles], axis=1)
        meta = jnp.concatenate([t[LEVELS:] for t in tiles], axis=1).astype(jnp.float32)
        part, cell, observed, weight = (meta[j : j + 1] for j in range(4))
        cell = cell.astype(jnp.bfloat16)
        hits = [
            cell_ref[...] == jnp.broadcast_to(cell[:, i * LANES : (i + 1) * LANES], (256, LANES))
            for i in range(WIDTH)
        ]
        pick = jnp.concatenate([jnp.where(hit, one, nil) for hit in hits], axis=1)
        return g, step, profile, part - 1.0, observed, weight, pick

    def gather(g, step, profile, part, observed, weight, pick):
        column = jnp.zeros((LEVELS, n), jnp.float32)
        for i in range(g * GROUP_PARTS // 2, (g + 1) * GROUP_PARTS // 2):
            found = jnp.dot(
                field_ref[2 * i * PAIR : 2 * (i + 1) * PAIR, :],
                pick,
                preferred_element_type=jnp.float32,
            )
            found = found[:PAIR] + found[PAIR:]
            column = jnp.where(part == 2.0 * i, found[:LEVELS], column)
            column = jnp.where(part == 2.0 * i + 1.0, found[LEVELS:], column)
        return column

    def force(column, g, step, profile, part, observed, weight, pick):
        wide = profile.astype(jnp.float32)
        model = jnp.sum(wide * column, axis=0, keepdims=True)
        misfit = model - observed
        for i in range(WIDTH):
            found_ref[g, step * WIDTH + i] = jnp.broadcast_to(
                misfit[:, i * LANES : (i + 1) * LANES], (8, LANES)
            )
        vector = wide * (weight * misfit)
        high = vector.astype(jnp.bfloat16)
        return high, (vector - high.astype(jnp.float32)).astype(jnp.bfloat16)

    def scatter(vector, g, step, profile, part, observed, weight, pick):
        high, low = (jnp.concatenate([term, term], axis=0) for term in vector)
        second = lax.broadcasted_iota(jnp.int32, (PAIR, n), 0) >= LEVELS
        part_row = (part - jnp.where(second, 1.0, 0.0)).astype(jnp.bfloat16)
        for i in range(g * GROUP_PARTS // 2, (g + 1) * GROUP_PARTS // 2):
            own = part_row == jnp.bfloat16(2 * i)
            sums = lax.dot_general(
                jnp.concatenate([jnp.where(own, high, nil), jnp.where(own, low, nil)], axis=0),
                pick,
                (((1,), (1,)), ((), ())),
                preferred_element_type=jnp.float32,
            )
            adjoint_ref[i * PAIR : (i + 1) * PAIR, :] += sums[:PAIR] + sums[PAIR:]

    def work(groups, step):
        loaded = [load(g, step) for g in groups]
        columns = [gather(*x) for x in loaded]
        vectors = [force(column, *x) for x, column in zip(loaded, columns)]
        for x, vector in zip(loaded, vectors):
            scatter(vector, *x)
        return 0

    steps = [lax.shift_right_logical(ends[g] + n - 1, n.bit_length() - 1) for g in range(GROUPS)]
    common = functools.reduce(jnp.minimum, steps)
    lax.fori_loop(0, common, lambda step, _: work(range(GROUPS), step), 0)
    for g in range(GROUPS):
        lax.fori_loop(common, steps[g], lambda step, _, g=g: work([g], step), 0)

    lane = lax.broadcasted_iota(jnp.int32, (8, LANES), 1)
    row_id = lax.broadcasted_iota(jnp.int32, (8, LANES), 0)

    def part_ways(eight, ends):
        ends = list(ends)
        rows = jnp.zeros((8, LANES), jnp.float32)
        for j in range(8):
            start = jnp.int32(0)
            row = jnp.zeros((8, LANES), jnp.float32)
            for g in range(GROUPS):
                count = count_ref[eight * 8 + j, g]
                tile, at = lax.shift_right_logical(ends[g], 7), ends[g] & (LANES - 1)
                values = jnp.where(lane >= at, found_ref[g, tile], found_ref[g, tile + 1])
                values = pltpu.roll(values, (start - at) & (LANES - 1), 1)
                row = jnp.where(lane >= start, values, row)
                ends[g] = ends[g] + count
                start = start + count
            rows = jnp.where(row_id == j, row, rows)
        write_misfit(eight, rows)
        return tuple(ends)

    lax.fori_loop(0, block_ref.shape[0] // 8, part_ways, (jnp.int32(0),) * GROUPS)


def first_soundings_body(field_ref, block_ref, adjoint_ref, misfit_ref, *scratch):
    adjoint_ref[...] = jnp.zeros_like(adjoint_ref)

    def write_misfit(eight, rows):
        misfit_ref[pl.ds(eight * 8, 8), :] = rows

    soundings(field_ref, block_ref, adjoint_ref, write_misfit, *scratch)


def second_soundings_body(
    field_ref, block_ref, earlier_ref, other_ref, adjoint_ref, misfit_ref, *rest
):
    edges, scratch = rest[:4], rest[4:]
    adjoint_ref[...] = earlier_ref[...]

    def write_misfit(eight, rows):
        misfit_ref[pl.ds(eight * 16, 8, stride=2), :] = other_ref[pl.ds(eight * 8, 8), :]
        misfit_ref[pl.ds(eight * 16 + 1, 8, stride=2), :] = rows

    soundings(field_ref, block_ref, adjoint_ref, write_misfit, *scratch)
    write_edges(lambda t, row: cell_slab(adjoint_ref, t, row), *edges)


def observe(field, blocks, earlier=()):
    count = blocks.shape[0]
    tiles = count + WIDTH
    outs = [jax.ShapeDtypeStruct((PARTS * LEVELS, 256), jnp.float32)]
    outs += [jax.ShapeDtypeStruct((count * (2 if earlier else 1), LANES), jnp.float32)]
    return whole(
        second_soundings_body if earlier else first_soundings_body,
        outs + (EDGES if earlier else []),
        (field, blocks) + tuple(earlier),
        "second_soundings" if earlier else "first_soundings",
        scratch=[
            pltpu.VMEM((GROUPS, tiles, ROWS, LANES), jnp.bfloat16),
            pltpu.VMEM((GROUPS, tiles, 8, LANES), jnp.float32),
            pltpu.VMEM((256, LANES), jnp.bfloat16),
            pltpu.VMEM((count, LANES), jnp.int32),
            pltpu.SMEM((count, LANES), jnp.int32),
            pltpu.SemaphoreType.DMA(()),
        ],
        flops=15000000000,
    )


def per_device(
    initial, east_wind, north_wind, mixing, kernel, columns, observed, obs_weight, counts, targets
):
    lat_count = lax.axis_size("lat")
    lon_count = lax.axis_size("lon")
    sounds = kernel.shape[2]
    block_count = kernel.shape[0]
    device_count = lat_count * lon_count

    def exchange(array):
        return lax.all_to_all(array, ("lat", "lon"), split_axis=0, concat_axis=0, tiled=True)

    is_last = (lax.axis_index("lat") == lat_count - 1).astype(jnp.int32).reshape(1)
    winds_like = jax.ShapeDtypeStruct((2, LAT_CELLS, LEVELS, LANES), jnp.float32)

    def slabs_like(number):
        return jax.ShapeDtypeStruct((number, LEVELS, LANES), jnp.float32)

    grid = (is_last, initial, east_wind, north_wind, mixing)
    up, down = whole(rows_body, [slabs_like(14), slabs_like(12)], grid, "rows", scalars=1)
    counts, up, down = lax.optimization_barrier((counts, up, down))
    from_south, from_north = shifted(up, 1, 0), shifted(down, -1, 0)
    slots = jax.ShapeDtypeStruct((device_count, ROWS, sounds), jnp.bfloat16)
    by_device = jax.ShapeDtypeStruct((device_count,), jnp.int32)
    heard = (kernel, columns, observed, obs_weight)
    scratch = [pltpu.VMEM((block_count, sounds), jnp.float32)] * 2
    scratch += [pltpu.VMEM((LANES, LANES), jnp.bfloat16)]
    by_block = jax.ShapeDtypeStruct((block_count, sounds), jnp.float32)
    out_first, place, tally, source_first, source_second = whole(
        pack_first_body,
        [slots, by_block, by_block, by_device, by_device],
        (targets[:, 0], counts) + heard,
        "pack_first",
        scratch=scratch,
        scalars=2,
        scalar_outs=2,
    )
    (out_second,) = whole(
        pack, [slots], (source_second,) + heard + (place, tally), "pack_second", scratch=scratch,
        scalars=1,
    )
    out_first, from_south, from_north = lax.optimization_barrier(
        (out_first, from_south, from_north)
    )
    got_first = exchange(out_first)
    state, *rest = whole(
        arrange_body,
        [STATE, winds_like, winds_like, winds_like, slabs_like(3), slabs_like(3)],
        grid + (from_south, from_north),
        "arrange",
        scalars=1,
    )
    fields, (east, west) = tuple(rest[:3]), rest[3:]
    side_west, side_east = shifted(east, 0, 1), shifted(west, 0, -1)
    out_second, side_west, side_east = lax.optimization_barrier((out_second, side_west, side_east))
    got_second = exchange(out_second)
    (field,) = whole(
        forward_body,
        [jax.ShapeDtypeStruct((2 * PARTS * LEVELS, 256), jnp.bfloat16)],
        (state,) + fields + (east, west, from_south, from_north, side_west, side_east),
        "forward",
        scratch=[MIDDLE, pltpu.VMEM(STATE.shape, jnp.float32)],
    )
    earlier = observe(field, got_first)
    adjoint, misfit, up, down, own_east, own_west = observe(field, got_second, earlier)
    from_west, from_east = shifted(own_east, 0, 1), shifted(own_west, 0, -1)
    ends = jnp.stack([from_west, from_east])
    returned = exchange(misfit)
    (gradient,) = whole(
        adjoint_body,
        [jax.ShapeDtypeStruct(initial.shape, jnp.float32)],
        (adjoint,) + fields + (from_south, from_north, east, side_west, side_east)
        + (own_east, own_west, from_west, from_east)
        + (shifted(jnp.concatenate([up, ends]), 1, 0), shifted(jnp.concatenate([down, ends]), -1, 0)),
        "adjoint",
        scratch=[MIDDLE],
    )
    returned, gradient = lax.optimization_barrier((returned, gradient))
    (innovations,) = whole(
        innovations_body,
        [jax.ShapeDtypeStruct((block_count, sounds), jnp.float32)],
        (source_first, source_second, returned, place),
        "innovations",
        scratch=[pltpu.VMEM((block_count + 8, sounds), jnp.float32)],
        scalars=2,
    )
    return (gradient, innovations)


def solution(mesh):
    return jax.shard_map(
        per_device,
        mesh=mesh,
        in_specs=(
            P(None, None, "lat", "lon"),
            P(None, None, "lat", "lon"),
            P(None, None, "lat", "lon"),
            P(None, None, "lat", "lon"),
            P(("lat", "lon"), None, None),
            P(("lat", "lon"), None),
            P(("lat", "lon"), None),
            P(("lat", "lon"), None),
            P(("lat", "lon")),
            P(("lat", "lon"), None),
        ),
        out_specs=(P(None, None, "lat", "lon"), P(("lat", "lon"), None)),
        check_vma=False,
    )
```

```python
import functools

import jax
import jax.numpy as jnp
from jax import lax
from jax.experimental import pallas as pl
from jax.experimental.pallas import tpu as pltpu
from jax.sharding import PartitionSpec as P

LEVELS = 72
ROWS = 80
PAIR = 2 * LEVELS
TRACERS = 3
PARTS = 12
GROUPS = 6
GROUP_PARTS = PARTS // GROUPS
WIDTH = 2
LAT_CELLS = 8
LANES = 128


def lane_index():
    return lax.broadcasted_iota(jnp.int32, (LEVELS, LANES), 1)


def rolled(array, shift, axis):
    shift = shift % array.shape[axis]
    return pltpu.roll(array, shift, axis) if shift else array


def west_of(slab, halo, place):
    return jnp.where(lane_index() == 0, rolled(halo, -place, 1), rolled(slab, 1, 1))


def east_of(slab, halo, place):
    return jnp.where(
        lane_index() == LANES - 1, rolled(halo, LANES - 1 - place, 1), rolled(slab, -1, 1)
    )


SLOT = 32


def place_of(t, row):
    return t * 10 + row + 1


def packed(slabs, lane, base=0, first_row=0, rows=LAT_CELLS):
    out = jnp.zeros((LEVELS, LANES), jnp.float32)
    for i, slab in enumerate(slabs):
        place = base + place_of(i // rows, first_row + i % rows)
        out = jnp.where(lane_index() == place, rolled(slab, place - lane, 1), out)
    return out


def packed_wind(slabs, lane, base):
    one = packed(slabs, lane, base, -1, LAT_CELLS + 2)
    return one + rolled(one, 10, 1) + rolled(one, 20, 1)


def slot(array, number):
    return rolled(array, -SLOT * number, 1)


def with_corners(own, south, north):
    row = (lane_index() & (SLOT - 1)) % 10
    out = jnp.where(row == 0, rolled(south, -LAT_CELLS, 1), own)
    return jnp.where(row == 9, rolled(north, LAT_CELLS, 1), out)


def mixed(slab, coeff):
    upward = coeff * (rolled(slab, -1, 0) - slab)
    return upward - rolled(upward, 1, 0)


def forward(slab, left, right, above, below, east, before, north, south, coeff):
    zonal = jnp.maximum(east, 0.0) * slab + jnp.minimum(east, 0.0) * right
    zonal_before = jnp.maximum(before, 0.0) * left + jnp.minimum(before, 0.0) * slab
    merid = jnp.maximum(north, 0.0) * slab + jnp.minimum(north, 0.0) * above
    merid_before = jnp.maximum(south, 0.0) * below + jnp.minimum(south, 0.0) * slab
    return slab - (zonal - zonal_before) - (merid - merid_before) + mixed(slab, coeff)


def backward(slab, left, right, above, below, east, before, north, south, coeff):
    zonal = jnp.maximum(east, 0.0) * (right - slab) + jnp.minimum(before, 0.0) * (slab - left)
    merid = jnp.maximum(north, 0.0) * (above - slab) + jnp.minimum(south, 0.0) * (slab - below)
    return slab + zonal + merid + mixed(slab, coeff)


def write_edges(read, up_ref, down_ref, east_edge, west_edge):
    slabs = [read(t, row) for t in range(TRACERS) for row in range(LAT_CELLS)]
    for t in range(TRACERS):
        for i in range(2):
            up_ref[2 * t + i] = slabs[t * LAT_CELLS + LAT_CELLS - 2 + i]
            down_ref[2 * t + i] = slabs[t * LAT_CELLS + i]
    east_edge[...] = packed(slabs, LANES - 1) + packed(slabs, LANES - 2, SLOT)
    west_edge[...] = packed(slabs, 0) + packed(slabs, 1, SLOT)


def arrange_body(
    last_ref, initial_ref, east_ref, north_ref, mixing_ref, up_terms, down_terms,
    state_ref, east_out, north_out, mixing_out, east_edge, west_edge, up_ref, down_ref,
):
    joined_terms(up_terms, UP_LOW, up_ref)
    joined_terms(down_terms, DOWN_LOW, down_ref)
    slabs = []
    for t in range(TRACERS):
        slabs.append(up_ref[2 * t + 1])
        for row in range(LAT_CELLS):
            state_ref[t, row] = initial_ref[t, :, row, :]
            slabs.append(state_ref[t, row])
        slabs.append(down_ref[2 * t])
    rows = LAT_CELLS + 2
    east_edge[0] = packed(slabs, LANES - 1, 0, -1, rows) + packed(slabs, LANES - 2, SLOT, -1, rows)
    west_edge[0] = packed(slabs, 0, 0, -1, rows) + packed(slabs, 1, SLOT, -1, rows)
    for m in range(east_ref.shape[0]):
        for row in range(LAT_CELLS):
            east_out[m, row] = east_ref[m, :, row, :]
            north_out[m, row] = masked_north(last_ref, north_ref, m, row)
            mixing_out[m, row] = masked_mixing(mixing_ref, m, row)

        def column(ref, number):
            own = [ref[m, row] for row in range(LAT_CELLS)]
            return [up_ref[6 + 4 * m + number]] + own + [down_ref[6 + 3 * m + number]]

        east, mixing, north = column(east_out, 0), column(mixing_out, 1), column(north_out, 2)
        east_edge[1 + m] = (
            packed_wind(east, LANES - 1, 0)
            + packed_wind(mixing, LANES - 1, SLOT)
            + packed_wind(north, LANES - 1, 2 * SLOT)
            + packed_wind(east, LANES - 2, 3 * SLOT)
        )
        west_edge[1 + m] = (
            packed_wind(east, 0, 0)
            + packed_wind(mixing, 0, SLOT)
            + packed_wind(north, 0, 2 * SLOT)
        )


def masked_north(last_ref, north_ref, m, row):
    north = north_ref[m, :, row, :]
    if row == LAT_CELLS - 1:
        north = jnp.where(last_ref[0] > 0, jnp.float32(0.0), north)
    return north


def masked_mixing(mixing_ref, m, row):
    top = lax.broadcasted_iota(jnp.int32, (LEVELS, LANES), 0) == LEVELS - 1
    return jnp.where(top, jnp.float32(0.0), mixing_ref[m, :, row, :])


UP_LOW = (1, 3, 5, 8, 12)
DOWN_LOW = (0, 2, 4)


def rows_body(last_ref, initial_ref, east_ref, north_ref, mixing_ref, up_ref, down_ref):
    last = LAT_CELLS - 1
    up, down = [], []
    for t in range(TRACERS):
        for i in range(2):
            up.append(initial_ref[t, :, LAT_CELLS - 2 + i, :])
            down.append(initial_ref[t, :, i, :])
    for m in range(east_ref.shape[0]):
        for slabs, row in ((up, last), (down, 0)):
            slabs.append(east_ref[m, :, row, :])
            slabs.append(masked_mixing(mixing_ref, m, row))
            slabs.append(masked_north(last_ref, north_ref, m, row))
        up.append(masked_north(last_ref, north_ref, m, last - 1))
    for ref, slabs, lows in ((up_ref, up, UP_LOW), (down_ref, down, DOWN_LOW)):
        for i, slab in enumerate(slabs):
            high = slab.astype(jnp.bfloat16)
            ref[i] = high
            if i in lows:
                rest = slab - high.astype(jnp.float32)
                ref[len(slabs) + lows.index(i)] = rest.astype(jnp.bfloat16)


def joined_terms(terms_ref, lows, out_ref):
    count = out_ref.shape[0]
    for i in range(count):
        slab = terms_ref[i].astype(jnp.float32)
        if i in lows:
            slab = slab + terms_ref[count + lows.index(i)].astype(jnp.float32)
        out_ref[i] = slab


def two_steps(
    step, moments, read, winds, wind_up, wind_down, wind_east, sides,
    up_ref, down_ref, own_east, own_west, from_west, from_east, middle_ref, write,
):
    east_ref, north_ref, mixing_ref = winds

    def state(t, row):
        if row < 0:
            return up_ref[2 * t + row + 2]
        return read(t, row) if row < LAT_CELLS else down_ref[2 * t + row - LAT_CELLS]

    def wind(ref, number, m, row):
        if row < -1:
            return wind_up(4 * m + 3)
        if row < 0:
            return wind_up(4 * m + number)
        return ref[m, row] if row < LAT_CELLS else wind_down(3 * m + number)

    def winds_of(m, row, east_side):
        east = wind(east_ref, 0, m, row)
        return (
            east,
            west_of(east, east_side, place_of(0, row)),
            wind(north_ref, 2, m, row),
            wind(north_ref, 2, m, row - 1),
            wind(mixing_ref, 1, m, row),
        )

    m = moments[0]
    side_west, side_east = sides(m)
    for row in range(-1, LAT_CELLS + 1):
        local = winds_of(m, row, side_west)
        for t in range(TRACERS):
            slab, place = state(t, row), place_of(t, row)
            middle_ref[t, row + 1] = step(
                slab,
                west_of(slab, from_west, place),
                east_of(slab, from_east, place),
                state(t, row + 1),
                state(t, row - 1),
                *local,
            )

    def column(own, left, right, east, before, side):
        north = slot(side, 2)
        around = (rolled(own, -1, 1), rolled(own, 1, 1))
        return step(
            own, left, right, *around, east, before, north, rolled(north, 1, 1), slot(side, 1)
        )

    next_west = column(
        from_west, slot(from_west, 1), own_west, side_west, slot(side_west, 3), side_west
    )
    next_east = column(
        from_east, own_east, slot(from_east, 1), side_east, wind_east(m), side_east
    )
    m = moments[1]
    side_west, _ = sides(m)
    for row in range(LAT_CELLS):
        local = winds_of(m, row, side_west)
        for t in range(TRACERS):
            slab, place = middle_ref[t, row + 1], place_of(t, row)
            write(
                t,
                row,
                step(
                    slab,
                    west_of(slab, next_west, place),
                    east_of(slab, next_east, place),
                    middle_ref[t, row + 2],
                    middle_ref[t, row],
                    *local,
                ),
            )


def forward_body(
    state_ref, east_ref, north_ref, mixing_ref, own_east, own_west,
    up_ref, down_ref, from_west, from_east, field_ref, middle_ref, after_ref,
):
    def write(t, row, slab):
        after_ref[t, row] = slab

    two_steps(
        forward,
        (0, 1),
        lambda t, row: state_ref[t, row],
        (east_ref, north_ref, mixing_ref),
        lambda i: up_ref[6 + i],
        lambda i: down_ref[6 + i],
        lambda m: own_east[1 + m],
        lambda m: (from_west[1 + m], from_east[1 + m]),
        up_ref,
        down_ref,
        own_east[0],
        own_west[0],
        from_west[0],
        from_east[0],
        middle_ref,
        write,
    )
    for i in range(6):
        for low_row in range(2):
            slabs = []
            for p in (2 * i, 2 * i + 1):
                slabs.append(after_ref[p // 4, (p % 4) * 2 + low_row])
            both = jnp.concatenate(slabs, axis=0)
            high = both.astype(jnp.bfloat16)
            low = (both - high.astype(jnp.float32)).astype(jnp.bfloat16)
            lanes = slice(low_row * LANES, (low_row + 1) * LANES)
            field_ref[2 * i * PAIR : (2 * i + 1) * PAIR, lanes] = high
            field_ref[(2 * i + 1) * PAIR : (2 * i + 2) * PAIR, lanes] = low


def cell_slab(ref, t, row):
    first = (t * 4 + row // 2) * LEVELS
    return ref[first : first + LEVELS, (row % 2) * LANES : (row % 2 + 1) * LANES]


def adjoint_body(
    adjoint_ref, east_ref, north_ref, mixing_ref, wind_up, wind_down, wind_east, side_west, side_east,
    own_east, own_west, from_west, from_east, up_ref, down_ref, gradient_ref, middle_ref,
):
    def write(t, row, slab):
        gradient_ref[t, :, row, :] = slab

    two_steps(
        backward,
        (1, 0),
        lambda t, row: cell_slab(adjoint_ref, t, row),
        (east_ref, north_ref, mixing_ref),
        lambda i: wind_up[6 + i],
        lambda i: wind_down[6 + i],
        lambda m: wind_east[1 + m],
        lambda m: (side_west[1 + m], side_east[1 + m]),
        up_ref,
        down_ref,
        own_east[...],
        own_west[...],
        with_corners(from_west[...], up_ref[6], down_ref[6]),
        with_corners(from_east[...], up_ref[7], down_ref[7]),
        middle_ref,
        write,
    )


STATE = jax.ShapeDtypeStruct((TRACERS, LAT_CELLS, LEVELS, LANES), jnp.float32)
ROW_EDGE = jax.ShapeDtypeStruct((2 * TRACERS, LEVELS, LANES), jnp.float32)
COLUMN_EDGE = jax.ShapeDtypeStruct((LEVELS, LANES), jnp.float32)
EDGES = [ROW_EDGE, ROW_EDGE, COLUMN_EDGE, COLUMN_EDGE]
MIDDLE = pltpu.VMEM((TRACERS, LAT_CELLS + 2, LEVELS, LANES), jnp.float32)


def whole(body, outs, operands, name, scratch=(), scalars=0, flops=5000000, scalar_outs=0, in_hbm=(), steps=1, vmem_mib=63):
    smem = pl.BlockSpec(memory_space=pltpu.SMEM)

    def vmem(array):
        zeros = (0,) * len(array.shape)
        return pl.BlockSpec(array.shape, lambda i: zeros, pipeline_mode=pl.Buffered(1))

    def spec(i, array):
        if i < scalars:
            return smem
        return pl.BlockSpec(memory_space=pl.ANY) if i in in_hbm else vmem(array)

    def out_spec(i, array):
        if i >= len(outs) - scalar_outs:
            return smem
        if i or steps == 1:
            return vmem(array)
        rest = array.shape[1:]
        return pl.BlockSpec(
            (array.shape[0] // steps,) + rest, lambda j: (j,) + (0,) * len(rest)
        )

    return pl.pallas_call(
        body,
        grid=(steps,),
        in_specs=[spec(i, array) for i, array in enumerate(operands)],
        out_specs=[out_spec(i, array) for i, array in enumerate(outs)],
        out_shape=outs,
        scratch_shapes=list(scratch),
        compiler_params=pltpu.CompilerParams(vmem_limit_bytes=vmem_mib << 20),
        cost_estimate=pl.CostEstimate(flops=flops, bytes_accessed=6000000, transcendentals=0),
        name=name,
    )(*operands)


def shifted(array, lat_by, lon_by):
    lat, lon = lax.axis_size("lat"), lax.axis_size("lon")
    if not lat_by:
        return lax.ppermute(array, "lon", [(j, (j + lon_by) % lon) for j in range(lon)])
    rows = [(i, i + lat_by) for i in range(lat) if 0 <= i + lat_by < lat]
    if not lon_by:
        return lax.ppermute(array, "lat", rows)
    pairs = [(i * lon + j, k * lon + (j + lon_by) % lon) for i, k in rows for j in range(lon)]
    return lax.ppermute(array, ("lat", "lon"), pairs)


def plan(targets_ref, counts_ref, columns_ref, place_ref, first_ref, second_ref, tally_ref):
    def clear(device, carry):
        first_ref[device] = -1
        second_ref[device] = -1
        return carry

    lax.fori_loop(0, first_ref.shape[0], clear, 0, unroll=8)

    def name(block, carry):
        target = targets_ref[block]
        known = first_ref[target]
        second_ref[target] = jnp.where(known < 0, -1, block)
        first_ref[target] = jnp.where(known < 0, block, known)
        return carry

    lax.fori_loop(0, targets_ref.shape[0], name, 0, unroll=8)
    part_id = lax.broadcasted_iota(jnp.int32, (16, LANES), 0)
    group = lax.broadcasted_iota(jnp.int32, (16, LANES), 1) * GROUP_PARTS
    of_group = (part_id >= group) & (part_id < group + GROUP_PARTS)
    lane = lax.broadcasted_iota(jnp.int32, (1, LANES), 1)
    row_id = lax.broadcasted_iota(jnp.int32, (8, LANES), 0)
    square = (LANES, 2 * LANES)
    earlier = lax.broadcasted_iota(jnp.int32, square, 0) < lax.broadcasted_iota(
        jnp.int32, square, 1
    )
    earlier = jnp.where(earlier, 1.0, 0.0).astype(jnp.bfloat16)

    def rank(eight, carry):
        parts = lax.shift_right_logical(columns_ref[pl.ds(eight * 8, 8), :], 8)
        rows = [parts[j : j + 1] for j in range(8)]
        lives = [lane < counts_ref[eight * 8 + j] for j in range(8)]
        members = [
            jnp.where((part_id == row) & live, 1.0, 0.0) for row, live in zip(rows, lives)
        ]
        sums = jnp.dot(
            jnp.concatenate(members, axis=0).astype(jnp.bfloat16),
            earlier,
            preferred_element_type=jnp.float32,
        )
        places = jnp.zeros((8, LANES), jnp.float32)
        tallies = jnp.zeros((8, LANES), jnp.float32)
        for j in range(8):
            own = sums[16 * j : 16 * j + 16]
            before = jnp.where(
                part_id == rows[j],
                own[:, :LANES],
                jnp.where(part_id < rows[j], own[:, LANES:], jnp.float32(0.0)),
            )
            place = jnp.sum(before, axis=0, keepdims=True)
            place = jnp.where(lives[j], place, jnp.float32(LANES))
            places = jnp.where(row_id == j, place, places)
            tally = jnp.sum(jnp.where(of_group, own[:, LANES:], 0.0), axis=0, keepdims=True)
            tallies = jnp.where(row_id == j, tally, tallies)
        place_ref[pl.ds(eight * 8, 8), :] = places
        tally_ref[pl.ds(eight * 8, 8), :] = tallies
        return carry

    lax.fori_loop(0, targets_ref.shape[0] // 8, rank, 0, unroll=2)


TOGETHER = 16


def widen(observed_ref, weight_ref, observed_wide, weight_wide, order_ref):
    observed_wide[...] = observed_ref[...].astype(jnp.float32)
    weight_wide[...] = weight_ref[...].astype(jnp.float32)
    order_ref[...] = (
        lax.broadcasted_iota(jnp.int32, (LANES, LANES), 0).astype(jnp.float32).astype(jnp.bfloat16)
    )


def pack(
    first, source_ref, kernel_ref, columns_ref, place_ref, tally_ref, out_ref, at,
    observed_wide, weight_wide, order_ref,
):
    row_id = lax.broadcasted_iota(jnp.int32, (8, LANES), 0)
    one, nil = jnp.bfloat16(1), jnp.bfloat16(0)

    def sorted_block(slot):
        source = source_ref[slot]
        block = jnp.maximum(source, 0)
        row = pl.ds(block, 1)
        cell = columns_ref[row, :]
        part = lax.shift_right_logical(cell, 8) + 1
        meta = jnp.where(row_id == 0, part.astype(jnp.float32), jnp.float32(0.0))
        meta = jnp.where(row_id == 1, (cell & 255).astype(jnp.float32), meta)
        meta = jnp.where(row_id == 2, observed_wide[row, :], meta)
        meta = jnp.where(row_id == 3, weight_wide[row, :], meta)
        rows = jnp.concatenate([kernel_ref[block].astype(jnp.float32), meta], axis=0)
        place = jnp.where(source >= 0, place_ref[row, :], jnp.float32(LANES)).astype(jnp.bfloat16)
        moved = jnp.where(order_ref[...] == jnp.broadcast_to(place, (LANES, LANES)), one, nil)
        result = lax.dot_general(
            rows.astype(jnp.bfloat16),
            moved,
            (((1,), (1,)), ((), ())),
            preferred_element_type=jnp.float32,
        )
        tally = jnp.where(source >= 0, tally_ref[row, :], jnp.float32(0.0))
        meta = jnp.where(row_id == 4, tally, result[LEVELS:])
        return jnp.concatenate([result[:LEVELS], meta], axis=0).astype(jnp.bfloat16)

    blocks = [sorted_block(first + j) for j in range(TOGETHER)]
    for j in range(TOGETHER):
        out_ref[at + j] = blocks[j]


def pack_second_body(
    source_ref, kernel_ref, columns_ref, observed_ref, weight_ref, place_ref, tally_ref, out_ref,
    *scratch,
):
    widen(observed_ref, weight_ref, *scratch)

    def step(i, carry):
        at = i * TOGETHER
        pack(
            at, source_ref, kernel_ref, columns_ref, place_ref, tally_ref, out_ref, at, *scratch
        )
        return carry

    lax.fori_loop(0, out_ref.shape[0] // TOGETHER, step, 0)


def pack_first_body(
    targets_ref, counts_ref, kernel_hbm, columns_ref, observed_ref, weight_ref,
    out_ref, place_ref, tally_ref, first_ref, second_ref,
    observed_wide, weight_wide, order_ref, kernel_ref, sem,
):
    scratch = (observed_wide, weight_wide, order_ref)

    @pl.when(pl.program_id(0) == 0)
    def _():
        copy = pltpu.make_async_copy(kernel_hbm, kernel_ref, sem)
        copy.start()
        widen(observed_ref, weight_ref, *scratch)
        plan(targets_ref, counts_ref, columns_ref, place_ref, first_ref, second_ref, tally_ref)
        copy.wait()

    pack(
        pl.program_id(0) * TOGETHER, first_ref, kernel_ref, columns_ref, place_ref, tally_ref,
        out_ref, 0, *scratch,
    )


def innovations_body(first_ref, second_ref, returned_ref, place_ref, out_ref, rows_ref):
    def one(device, carry):
        for rank, source_ref in enumerate((first_ref, second_ref)):
            source = source_ref[device]
            block = jnp.where(source >= 0, source, LANES)
            rows_ref[pl.ds(block, 1), :] = returned_ref[pl.ds(2 * device + rank, 1), :]
        return carry

    lax.fori_loop(0, first_ref.shape[0], one, 0, unroll=8)
    place = place_ref[...].astype(jnp.int32)
    live = place < LANES
    found = jnp.take_along_axis(
        rows_ref[: place.shape[0], :], jnp.where(live, place, 0), axis=1
    )
    out_ref[...] = jnp.where(live, found, jnp.float32(0.0))


def soundings(
    field_ref, block_ref, adjoint_ref, write_misfit, arrive,
    stream_ref, found_ref, cell_ref, tally_ref, count_ref, sem,
):
    n = WIDTH * LANES
    one, nil = jnp.bfloat16(1), jnp.bfloat16(0)
    lane = lax.broadcasted_iota(jnp.int32, (ROWS, LANES), 1)
    cell_ref[...] = (
        lax.broadcasted_iota(jnp.int32, (256, LANES), 0).astype(jnp.float32).astype(jnp.bfloat16)
    )
    empty = jnp.zeros((ROWS, LANES), jnp.bfloat16)
    eighth = lax.broadcasted_iota(jnp.int32, (8, LANES), 0)

    def tally(eight, carry):
        rows = jnp.zeros((8, LANES), jnp.float32)
        for j in range(8):
            meta = block_ref[eight * 8 + j][LEVELS:].astype(jnp.float32)
            rows = jnp.where(eighth == j, meta[4:5], rows)
        tally_ref[pl.ds(eight * 8, 8), :] = rows.astype(jnp.int32)
        return carry

    lax.fori_loop(0, block_ref.shape[0] // 8, tally, 0, unroll=2)
    copy = pltpu.make_async_copy(tally_ref, count_ref, sem)
    copy.start()
    copy.wait()

    def merge(block, carry):
        ends, tails = list(carry[0]), list(carry[1])
        values = block_ref[block]
        start = jnp.int32(0)
        for g in range(GROUPS):
            count = count_ref[block, g]
            tile, at = lax.shift_right_logical(ends[g], 7), ends[g] & (LANES - 1)
            turned = pltpu.roll(values, (at - start) & (LANES - 1), 1)
            joined = jnp.where(lane >= at, turned, tails[g])
            stream_ref[g, tile] = joined
            tails[g] = jnp.where(at + count >= LANES, turned, joined)
            ends[g] = ends[g] + count
            start = start + count
        return tuple(ends), tuple(tails)

    ends, tails = lax.fori_loop(
        0,
        block_ref.shape[0],
        merge,
        ((jnp.int32(0),) * GROUPS, (empty,) * GROUPS),
        unroll=8,
    )
    for g in range(GROUPS):
        tile, at = lax.shift_right_logical(ends[g], 7), ends[g] & (LANES - 1)
        stream_ref[g, tile] = jnp.where(lane < at, tails[g], empty)
        for j in range(1, WIDTH):
            stream_ref[g, tile + j] = empty

    arrive()

    def load(g, step):
        tiles = [stream_ref[g, step * WIDTH + i] for i in range(WIDTH)]
        profile = jnp.concatenate([t[:LEVELS] for t in tiles], axis=1)
        meta = jnp.concatenate([t[LEVELS:] for t in tiles], axis=1).astype(jnp.float32)
        part, cell, observed, weight = (meta[j : j + 1] for j in range(4))
        cell = cell.astype(jnp.bfloat16)
        hits = [
            cell_ref[...] == jnp.broadcast_to(cell[:, i * LANES : (i + 1) * LANES], (256, LANES))
            for i in range(WIDTH)
        ]
        pick = jnp.concatenate([jnp.where(hit, one, nil) for hit in hits], axis=1)
        return g, step, profile, part - 1.0, observed, weight, pick

    def gather(g, step, profile, part, observed, weight, pick):
        column = jnp.zeros((LEVELS, n), jnp.float32)
        for i in range(g * GROUP_PARTS // 2, (g + 1) * GROUP_PARTS // 2):
            found = jnp.dot(
                field_ref[2 * i * PAIR : 2 * (i + 1) * PAIR, :],
                pick,
                preferred_element_type=jnp.float32,
            )
            found = found[:PAIR] + found[PAIR:]
            column = jnp.where(part == 2.0 * i, found[:LEVELS], column)
            column = jnp.where(part == 2.0 * i + 1.0, found[LEVELS:], column)
        return column

    def force(column, g, step, profile, part, observed, weight, pick):
        wide = profile.astype(jnp.float32)
        model = jnp.sum(wide * column, axis=0, keepdims=True)
        misfit = model - observed
        for i in range(WIDTH):
            found_ref[g, step * WIDTH + i] = jnp.broadcast_to(
                misfit[:, i * LANES : (i + 1) * LANES], (8, LANES)
            )
        vector = wide * (weight * misfit)
        high = vector.astype(jnp.bfloat16)
        return high, (vector - high.astype(jnp.float32)).astype(jnp.bfloat16)

    def scatter(vector, g, step, profile, part, observed, weight, pick):
        high, low = (jnp.concatenate([term, term], axis=0) for term in vector)
        second = lax.broadcasted_iota(jnp.int32, (PAIR, n), 0) >= LEVELS
        part_row = (part - jnp.where(second, 1.0, 0.0)).astype(jnp.bfloat16)
        for i in range(g * GROUP_PARTS // 2, (g + 1) * GROUP_PARTS // 2):
            own = part_row == jnp.bfloat16(2 * i)
            sums = lax.dot_general(
                jnp.concatenate([jnp.where(own, high, nil), jnp.where(own, low, nil)], axis=0),
                pick,
                (((1,), (1,)), ((), ())),
                preferred_element_type=jnp.float32,
            )
            adjoint_ref[i * PAIR : (i + 1) * PAIR, :] += sums[:PAIR] + sums[PAIR:]

    def work(groups, step):
        loaded = [load(g, step) for g in groups]
        columns = [gather(*x) for x in loaded]
        vectors = [force(column, *x) for x, column in zip(loaded, columns)]
        for x, vector in zip(loaded, vectors):
            scatter(vector, *x)
        return 0

    steps = [lax.shift_right_logical(ends[g] + n - 1, n.bit_length() - 1) for g in range(GROUPS)]
    common = functools.reduce(jnp.minimum, steps)
    lax.fori_loop(0, common, lambda step, _: work(range(GROUPS), step), 0)
    for g in range(GROUPS):
        lax.fori_loop(common, steps[g], lambda step, _, g=g: work([g], step), 0)

    lane = lax.broadcasted_iota(jnp.int32, (8, LANES), 1)
    row_id = lax.broadcasted_iota(jnp.int32, (8, LANES), 0)

    def part_ways(eight, ends):
        ends = list(ends)
        rows = jnp.zeros((8, LANES), jnp.float32)
        for j in range(8):
            start = jnp.int32(0)
            row = jnp.zeros((8, LANES), jnp.float32)
            for g in range(GROUPS):
                count = count_ref[eight * 8 + j, g]
                tile, at = lax.shift_right_logical(ends[g], 7), ends[g] & (LANES - 1)
                values = jnp.where(lane >= at, found_ref[g, tile], found_ref[g, tile + 1])
                values = pltpu.roll(values, (start - at) & (LANES - 1), 1)
                row = jnp.where(lane >= start, values, row)
                ends[g] = ends[g] + count
                start = start + count
            rows = jnp.where(row_id == j, row, rows)
        write_misfit(eight, rows)
        return tuple(ends)

    lax.fori_loop(0, block_ref.shape[0] // 8, part_ways, (jnp.int32(0),) * GROUPS)


def first_soundings_body(
    field_hbm, block_ref, adjoint_ref, misfit_ref, field_ref, field_sem, *scratch
):
    copy = pltpu.make_async_copy(field_hbm, field_ref, field_sem)
    copy.start()
    adjoint_ref[...] = jnp.zeros_like(adjoint_ref)

    def write_misfit(eight, rows):
        misfit_ref[pl.ds(eight * 8, 8), :] = rows

    soundings(field_ref, block_ref, adjoint_ref, write_misfit, copy.wait, *scratch)


def second_soundings_body(
    field_hbm, block_ref, earlier_hbm, other_ref, adjoint_ref, misfit_ref, *rest
):
    edges, (field_ref, field_sem), scratch = rest[:4], rest[4:6], rest[6:-1]
    copies = [
        pltpu.make_async_copy(field_hbm, field_ref, field_sem),
        pltpu.make_async_copy(earlier_hbm, adjoint_ref, rest[-1]),
    ]
    for copy in copies:
        copy.start()

    def arrive():
        for copy in copies:
            copy.wait()

    def write_misfit(eight, rows):
        misfit_ref[pl.ds(eight * 16, 8, stride=2), :] = other_ref[pl.ds(eight * 8, 8), :]
        misfit_ref[pl.ds(eight * 16 + 1, 8, stride=2), :] = rows

    soundings(field_ref, block_ref, adjoint_ref, write_misfit, arrive, *scratch)
    write_edges(lambda t, row: cell_slab(adjoint_ref, t, row), *edges)


def observe(field, blocks, earlier=()):
    count = blocks.shape[0]
    tiles = count + WIDTH
    outs = [jax.ShapeDtypeStruct((PARTS * LEVELS, 256), jnp.float32)]
    outs += [jax.ShapeDtypeStruct((count * (2 if earlier else 1), LANES), jnp.float32)]
    return whole(
        second_soundings_body if earlier else first_soundings_body,
        outs + (EDGES if earlier else []),
        (field, blocks) + tuple(earlier),
        "second_soundings" if earlier else "first_soundings",
        in_hbm=(0, 2) if earlier else (0,),
        scratch=[
            pltpu.VMEM(field.shape, jnp.bfloat16),
            pltpu.SemaphoreType.DMA(()),
            pltpu.VMEM((GROUPS, tiles, ROWS, LANES), jnp.bfloat16),
            pltpu.VMEM((GROUPS, tiles, 8, LANES), jnp.float32),
            pltpu.VMEM((256, LANES), jnp.bfloat16),
            pltpu.VMEM((count, LANES), jnp.int32),
            pltpu.SMEM((count, LANES), jnp.int32),
            pltpu.SemaphoreType.DMA(()),
        ]
        + ([pltpu.SemaphoreType.DMA(())] if earlier else []),
        flops=15000000000,
    )


def per_device(
    initial, east_wind, north_wind, mixing, kernel, columns, observed, obs_weight, counts, targets
):
    lat_count = lax.axis_size("lat")
    lon_count = lax.axis_size("lon")
    sounds = kernel.shape[2]
    block_count = kernel.shape[0]
    device_count = lat_count * lon_count

    def exchange(array):
        return lax.all_to_all(array, ("lat", "lon"), split_axis=0, concat_axis=0, tiled=True)

    is_last = (lax.axis_index("lat") == lat_count - 1).astype(jnp.int32).reshape(1)
    winds_like = jax.ShapeDtypeStruct((2, LAT_CELLS, LEVELS, LANES), jnp.float32)

    def slabs_like(number):
        return jax.ShapeDtypeStruct((number, LEVELS, LANES), jnp.float32)

    grid = (is_last, initial, east_wind, north_wind, mixing)
    terms = [
        jax.ShapeDtypeStruct((14 + len(UP_LOW), LEVELS, LANES), jnp.bfloat16),
        jax.ShapeDtypeStruct((12 + len(DOWN_LOW), LEVELS, LANES), jnp.bfloat16),
    ]
    up, down = whole(rows_body, terms, grid, "rows", scalars=1)
    counts, up, down = lax.optimization_barrier((counts, up, down))
    from_south, from_north = shifted(up, 1, 0), shifted(down, -1, 0)
    slots = jax.ShapeDtypeStruct((device_count, ROWS, sounds), jnp.bfloat16)
    by_device = jax.ShapeDtypeStruct((device_count,), jnp.int32)
    heard = (kernel, columns, observed, obs_weight)
    scratch = [pltpu.VMEM((block_count, sounds), jnp.float32)] * 2
    scratch += [pltpu.VMEM((LANES, LANES), jnp.bfloat16)]
    by_block = jax.ShapeDtypeStruct((block_count, sounds), jnp.float32)
    out_first, place, tally, source_first, source_second = whole(
        pack_first_body,
        [slots, by_block, by_block, by_device, by_device],
        (targets[:, 0], counts) + heard,
        "pack_first",
        scratch=scratch
        + [pltpu.VMEM(kernel.shape, jnp.bfloat16), pltpu.SemaphoreType.DMA(())],
        scalars=2,
        scalar_outs=2,
        in_hbm=(2,),
        steps=device_count // TOGETHER,
    )
    (out_second,) = whole(
        pack_second_body,
        [slots],
        (source_second,) + heard + (place, tally),
        "pack_second",
        scratch=scratch,
        scalars=1,
    )
    out_first, from_south, from_north = lax.optimization_barrier(
        (out_first, from_south, from_north)
    )
    got_first = exchange(out_first)
    state, *rest = whole(
        arrange_body,
        [STATE, winds_like, winds_like, winds_like]
        + [slabs_like(3), slabs_like(3), slabs_like(14), slabs_like(12)],
        grid + (from_south, from_north),
        "arrange",
        scalars=1,
    )
    fields, (east, west, from_south, from_north) = tuple(rest[:3]), rest[3:]
    side_west, side_east = shifted(east, 0, 1), shifted(west, 0, -1)
    out_second, side_west, side_east = lax.optimization_barrier((out_second, side_west, side_east))
    got_second = exchange(out_second)
    (field,) = whole(
        forward_body,
        [jax.ShapeDtypeStruct((2 * PARTS * LEVELS, 256), jnp.bfloat16)],
        (state,) + fields + (east, west, from_south, from_north, side_west, side_east),
        "forward",
        scratch=[MIDDLE, pltpu.VMEM(STATE.shape, jnp.float32)],
    )
    earlier = observe(field, got_first)
    adjoint, misfit, up, down, own_east, own_west = observe(field, got_second, earlier)
    from_west, from_east = shifted(own_east, 0, 1), shifted(own_west, 0, -1)
    ends = jnp.stack([from_west, from_east])
    returned = exchange(misfit)
    (gradient,) = whole(
        adjoint_body,
        [jax.ShapeDtypeStruct(initial.shape, jnp.float32)],
        (adjoint,) + fields + (from_south, from_north, east, side_west, side_east)
        + (own_east, own_west, from_west, from_east)
        + (shifted(jnp.concatenate([up, ends]), 1, 0), shifted(jnp.concatenate([down, ends]), -1, 0)),
        "adjoint",
        scratch=[MIDDLE],
    )
    returned, gradient = lax.optimization_barrier((returned, gradient))
    (innovations,) = whole(
        innovations_body,
        [jax.ShapeDtypeStruct((block_count, sounds), jnp.float32)],
        (source_first, source_second, returned, place),
        "innovations",
        scratch=[pltpu.VMEM((block_count + 8, sounds), jnp.float32)],
        scalars=2,
    )
    return (gradient, innovations)


def solution(mesh):
    return jax.shard_map(
        per_device,
        mesh=mesh,
        in_specs=(
            P(None, None, "lat", "lon"),
            P(None, None, "lat", "lon"),
            P(None, None, "lat", "lon"),
            P(None, None, "lat", "lon"),
            P(("lat", "lon"), None, None),
            P(("lat", "lon"), None),
            P(("lat", "lon"), None),
            P(("lat", "lon"), None),
            P(("lat", "lon")),
            P(("lat", "lon"), None),
        ),
        out_specs=(P(None, None, "lat", "lon"), P(("lat", "lon"), None)),
        check_vma=False,
    )
```

```python
import functools

import jax
import jax.numpy as jnp
from jax import lax
from jax.experimental import pallas as pl
from jax.experimental.pallas import tpu as pltpu
from jax.sharding import PartitionSpec as P

LEVELS = 72
ROWS = 80
PAIR = 2 * LEVELS
TRACERS = 3
PARTS = 12
GROUPS = 6
GROUP_PARTS = PARTS // GROUPS
WIDTH = 4
LAT_CELLS = 8
LANES = 128


def lane_index():
    return lax.broadcasted_iota(jnp.int32, (LEVELS, LANES), 1)


def rolled(array, shift, axis):
    shift = shift % array.shape[axis]
    return pltpu.roll(array, shift, axis) if shift else array


def west_of(slab, halo, place):
    return jnp.where(lane_index() == 0, rolled(halo, -place, 1), rolled(slab, 1, 1))


def east_of(slab, halo, place):
    return jnp.where(
        lane_index() == LANES - 1, rolled(halo, LANES - 1 - place, 1), rolled(slab, -1, 1)
    )


SLOT = 32


def place_of(t, row):
    return t * 10 + row + 1


def packed(slabs, lane, base=0, first_row=0, rows=LAT_CELLS):
    out = jnp.zeros((LEVELS, LANES), jnp.float32)
    for i, slab in enumerate(slabs):
        place = base + place_of(i // rows, first_row + i % rows)
        out = jnp.where(lane_index() == place, rolled(slab, place - lane, 1), out)
    return out


def packed_wind(slabs, lane, base):
    one = packed(slabs, lane, base, -1, LAT_CELLS + 2)
    return one + rolled(one, 10, 1) + rolled(one, 20, 1)


def slot(array, number):
    return rolled(array, -SLOT * number, 1)


def with_corners(own, south, north):
    row = (lane_index() & (SLOT - 1)) % 10
    out = jnp.where(row == 0, rolled(south, -LAT_CELLS, 1), own)
    return jnp.where(row == 9, rolled(north, LAT_CELLS, 1), out)


def mixed(slab, coeff):
    upward = coeff * (rolled(slab, -1, 0) - slab)
    return upward - rolled(upward, 1, 0)


def forward(slab, left, right, above, below, east, before, north, south, coeff):
    zonal = jnp.maximum(east, 0.0) * slab + jnp.minimum(east, 0.0) * right
    zonal_before = jnp.maximum(before, 0.0) * left + jnp.minimum(before, 0.0) * slab
    merid = jnp.maximum(north, 0.0) * slab + jnp.minimum(north, 0.0) * above
    merid_before = jnp.maximum(south, 0.0) * below + jnp.minimum(south, 0.0) * slab
    return slab - (zonal - zonal_before) - (merid - merid_before) + mixed(slab, coeff)


def backward(slab, left, right, above, below, east, before, north, south, coeff):
    zonal = jnp.maximum(east, 0.0) * (right - slab) + jnp.minimum(before, 0.0) * (slab - left)
    merid = jnp.maximum(north, 0.0) * (above - slab) + jnp.minimum(south, 0.0) * (slab - below)
    return slab + zonal + merid + mixed(slab, coeff)


def write_edges(read, up_ref, down_ref, east_edge, west_edge):
    slabs = [read(t, row) for t in range(TRACERS) for row in range(LAT_CELLS)]
    for t in range(TRACERS):
        for i in range(2):
            up_ref[2 * t + i] = slabs[t * LAT_CELLS + LAT_CELLS - 2 + i]
            down_ref[2 * t + i] = slabs[t * LAT_CELLS + i]
    east_edge[...] = packed(slabs, LANES - 1) + packed(slabs, LANES - 2, SLOT)
    west_edge[...] = packed(slabs, 0) + packed(slabs, 1, SLOT)


def arrange_body(
    last_ref, initial_ref, east_ref, north_ref, mixing_ref, up_terms, down_terms,
    state_ref, east_out, north_out, mixing_out, east_edge, west_edge, up_ref, down_ref,
):
    joined_terms(up_terms, UP_LOW, up_ref)
    joined_terms(down_terms, DOWN_LOW, down_ref)
    slabs = []
    for t in range(TRACERS):
        slabs.append(up_ref[2 * t + 1])
        for row in range(LAT_CELLS):
            state_ref[t, row] = initial_ref[t, :, row, :]
            slabs.append(state_ref[t, row])
        slabs.append(down_ref[2 * t])
    rows = LAT_CELLS + 2
    east_edge[0] = packed(slabs, LANES - 1, 0, -1, rows) + packed(slabs, LANES - 2, SLOT, -1, rows)
    west_edge[0] = packed(slabs, 0, 0, -1, rows) + packed(slabs, 1, SLOT, -1, rows)
    for m in range(east_ref.shape[0]):
        for row in range(LAT_CELLS):
            east_out[m, row] = east_ref[m, :, row, :]
            north_out[m, row] = masked_north(last_ref, north_ref, m, row)
            mixing_out[m, row] = masked_mixing(mixing_ref, m, row)

        def column(ref, number):
            own = [ref[m, row] for row in range(LAT_CELLS)]
            return [up_ref[6 + 4 * m + number]] + own + [down_ref[6 + 3 * m + number]]

        east, mixing, north = column(east_out, 0), column(mixing_out, 1), column(north_out, 2)
        east_edge[1 + m] = (
            packed_wind(east, LANES - 1, 0)
            + packed_wind(mixing, LANES - 1, SLOT)
            + packed_wind(north, LANES - 1, 2 * SLOT)
            + packed_wind(east, LANES - 2, 3 * SLOT)
        )
        west_edge[1 + m] = (
            packed_wind(east, 0, 0)
            + packed_wind(mixing, 0, SLOT)
            + packed_wind(north, 0, 2 * SLOT)
        )


def masked_north(last_ref, north_ref, m, row):
    north = north_ref[m, :, row, :]
    if row == LAT_CELLS - 1:
        north = jnp.where(last_ref[0] > 0, jnp.float32(0.0), north)
    return north


def masked_mixing(mixing_ref, m, row):
    top = lax.broadcasted_iota(jnp.int32, (LEVELS, LANES), 0) == LEVELS - 1
    return jnp.where(top, jnp.float32(0.0), mixing_ref[m, :, row, :])


UP_LOW = (1, 3, 5, 8, 12)
DOWN_LOW = (0, 2, 4)


def rows_body(last_ref, initial_ref, east_ref, north_ref, mixing_ref, up_ref, down_ref):
    last = LAT_CELLS - 1
    up, down = [], []
    for t in range(TRACERS):
        for i in range(2):
            up.append(initial_ref[t, :, LAT_CELLS - 2 + i, :])
            down.append(initial_ref[t, :, i, :])
    for m in range(east_ref.shape[0]):
        for slabs, row in ((up, last), (down, 0)):
            slabs.append(east_ref[m, :, row, :])
            slabs.append(masked_mixing(mixing_ref, m, row))
            slabs.append(masked_north(last_ref, north_ref, m, row))
        up.append(masked_north(last_ref, north_ref, m, last - 1))
    for ref, slabs, lows in ((up_ref, up, UP_LOW), (down_ref, down, DOWN_LOW)):
        for i, slab in enumerate(slabs):
            high = slab.astype(jnp.bfloat16)
            ref[i] = high
            if i in lows:
                rest = slab - high.astype(jnp.float32)
                ref[len(slabs) + lows.index(i)] = rest.astype(jnp.bfloat16)


def joined_terms(terms_ref, lows, out_ref):
    count = out_ref.shape[0]
    for i in range(count):
        slab = terms_ref[i].astype(jnp.float32)
        if i in lows:
            slab = slab + terms_ref[count + lows.index(i)].astype(jnp.float32)
        out_ref[i] = slab


def two_steps(
    step, moments, read, winds, wind_up, wind_down, wind_east, sides,
    up_ref, down_ref, own_east, own_west, from_west, from_east, middle_ref, write,
):
    east_ref, north_ref, mixing_ref = winds

    def state(t, row):
        if row < 0:
            return up_ref[2 * t + row + 2]
        return read(t, row) if row < LAT_CELLS else down_ref[2 * t + row - LAT_CELLS]

    def wind(ref, number, m, row):
        if row < -1:
            return wind_up(4 * m + 3)
        if row < 0:
            return wind_up(4 * m + number)
        return ref[m, row] if row < LAT_CELLS else wind_down(3 * m + number)

    def winds_of(m, row, east_side):
        east = wind(east_ref, 0, m, row)
        return (
            east,
            west_of(east, east_side, place_of(0, row)),
            wind(north_ref, 2, m, row),
            wind(north_ref, 2, m, row - 1),
            wind(mixing_ref, 1, m, row),
        )

    m = moments[0]
    side_west, side_east = sides(m)
    for row in range(-1, LAT_CELLS + 1):
        local = winds_of(m, row, side_west)
        for t in range(TRACERS):
            slab, place = state(t, row), place_of(t, row)
            middle_ref[t, row + 1] = step(
                slab,
                west_of(slab, from_west, place),
                east_of(slab, from_east, place),
                state(t, row + 1),
                state(t, row - 1),
                *local,
            )

    def column(own, left, right, east, before, side):
        north = slot(side, 2)
        around = (rolled(own, -1, 1), rolled(own, 1, 1))
        return step(
            own, left, right, *around, east, before, north, rolled(north, 1, 1), slot(side, 1)
        )

    next_west = column(
        from_west, slot(from_west, 1), own_west, side_west, slot(side_west, 3), side_west
    )
    next_east = column(
        from_east, own_east, slot(from_east, 1), side_east, wind_east(m), side_east
    )
    m = moments[1]
    side_west, _ = sides(m)
    for row in range(LAT_CELLS):
        local = winds_of(m, row, side_west)
        for t in range(TRACERS):
            slab, place = middle_ref[t, row + 1], place_of(t, row)
            write(
                t,
                row,
                step(
                    slab,
                    west_of(slab, next_west, place),
                    east_of(slab, next_east, place),
                    middle_ref[t, row + 2],
                    middle_ref[t, row],
                    *local,
                ),
            )


def forward_body(
    state_ref, east_ref, north_ref, mixing_ref, own_east, own_west,
    up_ref, down_ref, from_west, from_east, field_ref, middle_ref, after_ref,
):
    def write(t, row, slab):
        after_ref[t, row] = slab

    two_steps(
        forward,
        (0, 1),
        lambda t, row: state_ref[t, row],
        (east_ref, north_ref, mixing_ref),
        lambda i: up_ref[6 + i],
        lambda i: down_ref[6 + i],
        lambda m: own_east[1 + m],
        lambda m: (from_west[1 + m], from_east[1 + m]),
        up_ref,
        down_ref,
        own_east[0],
        own_west[0],
        from_west[0],
        from_east[0],
        middle_ref,
        write,
    )
    for i in range(6):
        for low_row in range(2):
            slabs = []
            for p in (2 * i, 2 * i + 1):
                slabs.append(after_ref[p // 4, (p % 4) * 2 + low_row])
            both = jnp.concatenate(slabs, axis=0)
            high = both.astype(jnp.bfloat16)
            low = (both - high.astype(jnp.float32)).astype(jnp.bfloat16)
            lanes = slice(low_row * LANES, (low_row + 1) * LANES)
            field_ref[2 * i * PAIR : (2 * i + 1) * PAIR, lanes] = high
            field_ref[(2 * i + 1) * PAIR : (2 * i + 2) * PAIR, lanes] = low


def cell_slab(ref, t, row):
    first = (t * 4 + row // 2) * LEVELS
    return ref[first : first + LEVELS, (row % 2) * LANES : (row % 2 + 1) * LANES]


def adjoint_body(
    adjoint_ref, east_ref, north_ref, mixing_ref, wind_up, wind_down, wind_east, side_west, side_east,
    own_east, own_west, from_west, from_east, up_ref, down_ref, gradient_ref, middle_ref,
):
    def write(t, row, slab):
        gradient_ref[t, :, row, :] = slab

    two_steps(
        backward,
        (1, 0),
        lambda t, row: cell_slab(adjoint_ref, t, row),
        (east_ref, north_ref, mixing_ref),
        lambda i: wind_up[6 + i],
        lambda i: wind_down[6 + i],
        lambda m: wind_east[1 + m],
        lambda m: (side_west[1 + m], side_east[1 + m]),
        up_ref,
        down_ref,
        own_east[...],
        own_west[...],
        with_corners(from_west[...], up_ref[6], down_ref[6]),
        with_corners(from_east[...], up_ref[7], down_ref[7]),
        middle_ref,
        write,
    )


STATE = jax.ShapeDtypeStruct((TRACERS, LAT_CELLS, LEVELS, LANES), jnp.float32)
ROW_EDGE = jax.ShapeDtypeStruct((2 * TRACERS, LEVELS, LANES), jnp.float32)
COLUMN_EDGE = jax.ShapeDtypeStruct((LEVELS, LANES), jnp.float32)
EDGES = [ROW_EDGE, ROW_EDGE, COLUMN_EDGE, COLUMN_EDGE]
MIDDLE = pltpu.VMEM((TRACERS, LAT_CELLS + 2, LEVELS, LANES), jnp.float32)


def whole(body, outs, operands, name, scratch=(), scalars=0, flops=5000000, scalar_outs=0, in_hbm=(), steps=1, vmem_kib=65472):
    smem = pl.BlockSpec(memory_space=pltpu.SMEM)

    def vmem(array):
        zeros = (0,) * len(array.shape)
        return pl.BlockSpec(array.shape, lambda i: zeros, pipeline_mode=pl.Buffered(1))

    def spec(i, array):
        if i < scalars:
            return smem
        return pl.BlockSpec(memory_space=pl.ANY) if i in in_hbm else vmem(array)

    def out_spec(i, array):
        if i >= len(outs) - scalar_outs:
            return smem
        if i or steps == 1:
            return vmem(array)
        rest = array.shape[1:]
        return pl.BlockSpec(
            (array.shape[0] // steps,) + rest, lambda j: (j,) + (0,) * len(rest)
        )

    return pl.pallas_call(
        body,
        grid=(steps,),
        in_specs=[spec(i, array) for i, array in enumerate(operands)],
        out_specs=[out_spec(i, array) for i, array in enumerate(outs)],
        out_shape=outs,
        scratch_shapes=list(scratch),
        compiler_params=pltpu.CompilerParams(vmem_limit_bytes=vmem_kib << 10),
        cost_estimate=pl.CostEstimate(flops=flops, bytes_accessed=6000000, transcendentals=0),
        name=name,
    )(*operands)


def shifted(array, lat_by, lon_by):
    lat, lon = lax.axis_size("lat"), lax.axis_size("lon")
    if not lat_by:
        return lax.ppermute(array, "lon", [(j, (j + lon_by) % lon) for j in range(lon)])
    rows = [(i, i + lat_by) for i in range(lat) if 0 <= i + lat_by < lat]
    if not lon_by:
        return lax.ppermute(array, "lat", rows)
    pairs = [(i * lon + j, k * lon + (j + lon_by) % lon) for i, k in rows for j in range(lon)]
    return lax.ppermute(array, ("lat", "lon"), pairs)


def plan(targets_ref, counts_ref, columns_ref, place_ref, first_ref, second_ref, tally_ref):
    def clear(device, carry):
        first_ref[device] = -1
        second_ref[device] = -1
        return carry

    lax.fori_loop(0, first_ref.shape[0], clear, 0, unroll=8)

    def name(block, carry):
        target = targets_ref[block]
        known = first_ref[target]
        second_ref[target] = jnp.where(known < 0, -1, block)
        first_ref[target] = jnp.where(known < 0, block, known)
        return carry

    lax.fori_loop(0, targets_ref.shape[0], name, 0, unroll=8)
    part_id = lax.broadcasted_iota(jnp.int32, (16, LANES), 0)
    group = lax.broadcasted_iota(jnp.int32, (16, LANES), 1) * GROUP_PARTS
    of_group = (part_id >= group) & (part_id < group + GROUP_PARTS)
    lane = lax.broadcasted_iota(jnp.int32, (1, LANES), 1)
    row_id = lax.broadcasted_iota(jnp.int32, (8, LANES), 0)
    square = (LANES, 2 * LANES)
    earlier = lax.broadcasted_iota(jnp.int32, square, 0) < lax.broadcasted_iota(
        jnp.int32, square, 1
    )
    earlier = jnp.where(earlier, 1.0, 0.0).astype(jnp.bfloat16)

    def rank(eight, carry):
        parts = lax.shift_right_logical(columns_ref[pl.ds(eight * 8, 8), :], 8)
        rows = [parts[j : j + 1] for j in range(8)]
        lives = [lane < counts_ref[eight * 8 + j] for j in range(8)]
        members = [
            jnp.where((part_id == row) & live, 1.0, 0.0) for row, live in zip(rows, lives)
        ]
        sums = jnp.dot(
            jnp.concatenate(members, axis=0).astype(jnp.bfloat16),
            earlier,
            preferred_element_type=jnp.float32,
        )
        places = jnp.zeros((8, LANES), jnp.float32)
        tallies = jnp.zeros((8, LANES), jnp.float32)
        for j in range(8):
            own = sums[16 * j : 16 * j + 16]
            before = jnp.where(
                part_id == rows[j],
                own[:, :LANES],
                jnp.where(part_id < rows[j], own[:, LANES:], jnp.float32(0.0)),
            )
            place = jnp.sum(before, axis=0, keepdims=True)
            place = jnp.where(lives[j], place, jnp.float32(LANES))
            places = jnp.where(row_id == j, place, places)
            tally = jnp.sum(jnp.where(of_group, own[:, LANES:], 0.0), axis=0, keepdims=True)
            tallies = jnp.where(row_id == j, tally, tallies)
        place_ref[pl.ds(eight * 8, 8), :] = places
        tally_ref[pl.ds(eight * 8, 8), :] = tallies
        return carry

    lax.fori_loop(0, targets_ref.shape[0] // 8, rank, 0, unroll=2)


TOGETHER = 16


def widen(observed_ref, weight_ref, observed_wide, weight_wide, order_ref):
    observed_wide[...] = observed_ref[...].astype(jnp.float32)
    weight_wide[...] = weight_ref[...].astype(jnp.float32)
    order_ref[...] = (
        lax.broadcasted_iota(jnp.int32, (LANES, LANES), 0).astype(jnp.float32).astype(jnp.bfloat16)
    )


def pack(
    first, source_ref, kernel_ref, columns_ref, place_ref, tally_ref, out_ref, at,
    observed_wide, weight_wide, order_ref,
):
    row_id = lax.broadcasted_iota(jnp.int32, (8, LANES), 0)
    one, nil = jnp.bfloat16(1), jnp.bfloat16(0)

    def sorted_block(slot):
        source = source_ref[slot]
        block = jnp.maximum(source, 0)
        row = pl.ds(block, 1)
        cell = columns_ref[row, :]
        part = lax.shift_right_logical(cell, 8) + 1
        meta = jnp.where(row_id == 0, part.astype(jnp.float32), jnp.float32(0.0))
        meta = jnp.where(row_id == 1, (cell & 255).astype(jnp.float32), meta)
        meta = jnp.where(row_id == 2, observed_wide[row, :], meta)
        meta = jnp.where(row_id == 3, weight_wide[row, :], meta)
        rows = jnp.concatenate([kernel_ref[block].astype(jnp.float32), meta], axis=0)
        place = jnp.where(source >= 0, place_ref[row, :], jnp.float32(LANES)).astype(jnp.bfloat16)
        moved = jnp.where(order_ref[...] == jnp.broadcast_to(place, (LANES, LANES)), one, nil)
        result = lax.dot_general(
            rows.astype(jnp.bfloat16),
            moved,
            (((1,), (1,)), ((), ())),
            preferred_element_type=jnp.float32,
        )
        tally = jnp.where(source >= 0, tally_ref[row, :], jnp.float32(0.0))
        meta = jnp.where(row_id == 4, tally, result[LEVELS:])
        return jnp.concatenate([result[:LEVELS], meta], axis=0).astype(jnp.bfloat16)

    blocks = [sorted_block(first + j) for j in range(TOGETHER)]
    for j in range(TOGETHER):
        out_ref[at + j] = blocks[j]


def pack_second_body(
    source_ref, kernel_ref, columns_ref, observed_ref, weight_ref, place_ref, tally_ref, out_ref,
    *scratch,
):
    widen(observed_ref, weight_ref, *scratch)

    def step(i, carry):
        at = i * TOGETHER
        pack(
            at, source_ref, kernel_ref, columns_ref, place_ref, tally_ref, out_ref, at, *scratch
        )
        return carry

    lax.fori_loop(0, out_ref.shape[0] // TOGETHER, step, 0)


def pack_first_body(
    targets_ref, counts_ref, kernel_hbm, columns_ref, observed_ref, weight_ref,
    out_ref, place_ref, tally_ref, first_ref, second_ref,
    observed_wide, weight_wide, order_ref, kernel_ref, sem,
):
    scratch = (observed_wide, weight_wide, order_ref)

    @pl.when(pl.program_id(0) == 0)
    def _():
        copy = pltpu.make_async_copy(kernel_hbm, kernel_ref, sem)
        copy.start()
        widen(observed_ref, weight_ref, *scratch)
        plan(targets_ref, counts_ref, columns_ref, place_ref, first_ref, second_ref, tally_ref)
        copy.wait()

    pack(
        pl.program_id(0) * TOGETHER, first_ref, kernel_ref, columns_ref, place_ref, tally_ref,
        out_ref, 0, *scratch,
    )


def innovations_body(first_ref, second_ref, returned_ref, place_ref, out_ref, rows_ref):
    def one(device, carry):
        for rank, source_ref in enumerate((first_ref, second_ref)):
            source = source_ref[device]
            block = jnp.where(source >= 0, source, LANES)
            rows_ref[pl.ds(block, 1), :] = returned_ref[pl.ds(2 * device + rank, 1), :]
        return carry

    lax.fori_loop(0, first_ref.shape[0], one, 0, unroll=8)
    place = place_ref[...].astype(jnp.int32)
    live = place < LANES
    found = jnp.take_along_axis(
        rows_ref[: place.shape[0], :], jnp.where(live, place, 0), axis=1
    )
    out_ref[...] = jnp.where(live, found, jnp.float32(0.0))


def soundings(
    field_ref, block_ref, adjoint_ref, write_misfit, arrive,
    stream_ref, found_ref, cell_ref, tally_ref, count_ref, sem,
):
    n = WIDTH * LANES
    one, nil = jnp.bfloat16(1), jnp.bfloat16(0)
    lane = lax.broadcasted_iota(jnp.int32, (ROWS, LANES), 1)
    cell_ref[...] = (
        lax.broadcasted_iota(jnp.int32, (256, LANES), 0).astype(jnp.float32).astype(jnp.bfloat16)
    )
    empty = jnp.zeros((ROWS, LANES), jnp.bfloat16)
    eighth = lax.broadcasted_iota(jnp.int32, (8, LANES), 0)

    def tally(eight, carry):
        rows = jnp.zeros((8, LANES), jnp.float32)
        for j in range(8):
            meta = block_ref[eight * 8 + j][LEVELS:].astype(jnp.float32)
            rows = jnp.where(eighth == j, meta[4:5], rows)
        tally_ref[pl.ds(eight * 8, 8), :] = rows.astype(jnp.int32)
        return carry

    lax.fori_loop(0, block_ref.shape[0] // 8, tally, 0, unroll=2)
    copy = pltpu.make_async_copy(tally_ref, count_ref, sem)
    copy.start()
    copy.wait()

    def merge(block, carry):
        ends, tails = list(carry[0]), list(carry[1])
        values = block_ref[block]
        start = jnp.int32(0)
        for g in range(GROUPS):
            count = count_ref[block, g]
            tile, at = lax.shift_right_logical(ends[g], 7), ends[g] & (LANES - 1)
            turned = pltpu.roll(values, (at - start) & (LANES - 1), 1)
            joined = jnp.where(lane >= at, turned, tails[g])
            stream_ref[g, tile] = joined
            tails[g] = jnp.where(at + count >= LANES, turned, joined)
            ends[g] = ends[g] + count
            start = start + count
        return tuple(ends), tuple(tails)

    ends, tails = lax.fori_loop(
        0,
        block_ref.shape[0],
        merge,
        ((jnp.int32(0),) * GROUPS, (empty,) * GROUPS),
        unroll=8,
    )
    for g in range(GROUPS):
        tile, at = lax.shift_right_logical(ends[g], 7), ends[g] & (LANES - 1)
        stream_ref[g, tile] = jnp.where(lane < at, tails[g], empty)
        for j in range(1, WIDTH):
            stream_ref[g, tile + j] = empty

    arrive()

    def load(g, step):
        tiles = [stream_ref[g, step * WIDTH + i] for i in range(WIDTH)]
        profile = jnp.concatenate([t[:LEVELS] for t in tiles], axis=1)
        meta = jnp.concatenate([t[LEVELS:] for t in tiles], axis=1).astype(jnp.float32)
        part, cell, observed, weight = (meta[j : j + 1] for j in range(4))
        cell = cell.astype(jnp.bfloat16)
        hits = [
            cell_ref[...] == jnp.broadcast_to(cell[:, i * LANES : (i + 1) * LANES], (256, LANES))
            for i in range(WIDTH)
        ]
        pick = jnp.concatenate([jnp.where(hit, one, nil) for hit in hits], axis=1)
        return g, step, profile, part - 1.0, observed, weight, pick

    def gather(g, step, profile, part, observed, weight, pick):
        column = jnp.zeros((LEVELS, n), jnp.float32)
        for i in range(g * GROUP_PARTS // 2, (g + 1) * GROUP_PARTS // 2):
            found = jnp.dot(
                field_ref[2 * i * PAIR : 2 * (i + 1) * PAIR, :],
                pick,
                preferred_element_type=jnp.float32,
            )
            found = found[:PAIR] + found[PAIR:]
            column = jnp.where(part == 2.0 * i, found[:LEVELS], column)
            column = jnp.where(part == 2.0 * i + 1.0, found[LEVELS:], column)
        return column

    def force(column, g, step, profile, part, observed, weight, pick):
        wide = profile.astype(jnp.float32)
        model = jnp.sum(wide * column, axis=0, keepdims=True)
        misfit = model - observed
        for i in range(WIDTH):
            found_ref[g, step * WIDTH + i] = jnp.broadcast_to(
                misfit[:, i * LANES : (i + 1) * LANES], (8, LANES)
            )
        vector = wide * (weight * misfit)
        high = vector.astype(jnp.bfloat16)
        return high, (vector - high.astype(jnp.float32)).astype(jnp.bfloat16)

    def scatter(vector, g, step, profile, part, observed, weight, pick):
        high, low = (jnp.concatenate([term, term], axis=0) for term in vector)
        second = lax.broadcasted_iota(jnp.int32, (PAIR, n), 0) >= LEVELS
        part_row = (part - jnp.where(second, 1.0, 0.0)).astype(jnp.bfloat16)
        for i in range(g * GROUP_PARTS // 2, (g + 1) * GROUP_PARTS // 2):
            own = part_row == jnp.bfloat16(2 * i)
            sums = lax.dot_general(
                jnp.concatenate([jnp.where(own, high, nil), jnp.where(own, low, nil)], axis=0),
                pick,
                (((1,), (1,)), ((), ())),
                preferred_element_type=jnp.float32,
            )
            adjoint_ref[i * PAIR : (i + 1) * PAIR, :] += sums[:PAIR] + sums[PAIR:]

    def work(groups, step):
        loaded = [load(g, step) for g in groups]
        columns = [gather(*x) for x in loaded]
        vectors = [force(column, *x) for x, column in zip(loaded, columns)]
        for x, vector in zip(loaded, vectors):
            scatter(vector, *x)
        return 0

    steps = [lax.shift_right_logical(ends[g] + n - 1, n.bit_length() - 1) for g in range(GROUPS)]
    common = functools.reduce(jnp.minimum, steps)
    lax.fori_loop(0, common, lambda step, _: work(range(GROUPS), step), 0)
    for g in range(GROUPS):
        lax.fori_loop(common, steps[g], lambda step, _, g=g: work([g], step), 0)

    lane = lax.broadcasted_iota(jnp.int32, (8, LANES), 1)
    row_id = lax.broadcasted_iota(jnp.int32, (8, LANES), 0)

    def part_ways(eight, ends):
        ends = list(ends)
        rows = jnp.zeros((8, LANES), jnp.float32)
        for j in range(8):
            start = jnp.int32(0)
            row = jnp.zeros((8, LANES), jnp.float32)
            for g in range(GROUPS):
                count = count_ref[eight * 8 + j, g]
                tile, at = lax.shift_right_logical(ends[g], 7), ends[g] & (LANES - 1)
                values = jnp.where(lane >= at, found_ref[g, tile], found_ref[g, tile + 1])
                values = pltpu.roll(values, (start - at) & (LANES - 1), 1)
                row = jnp.where(lane >= start, values, row)
                ends[g] = ends[g] + count
                start = start + count
            rows = jnp.where(row_id == j, row, rows)
        write_misfit(eight, rows)
        return tuple(ends)

    lax.fori_loop(0, block_ref.shape[0] // 8, part_ways, (jnp.int32(0),) * GROUPS, unroll=2)


def first_soundings_body(
    field_hbm, block_ref, adjoint_ref, misfit_ref, field_ref, field_sem, *scratch
):
    copy = pltpu.make_async_copy(field_hbm, field_ref, field_sem)
    copy.start()
    adjoint_ref[...] = jnp.zeros_like(adjoint_ref)

    def write_misfit(eight, rows):
        misfit_ref[pl.ds(eight * 8, 8), :] = rows

    soundings(field_ref, block_ref, adjoint_ref, write_misfit, copy.wait, *scratch)


def second_soundings_body(
    field_hbm, block_ref, earlier_hbm, other_ref, adjoint_ref, misfit_ref, *rest
):
    edges, (field_ref, field_sem), scratch = rest[:4], rest[4:6], rest[6:-1]
    copies = [
        pltpu.make_async_copy(field_hbm, field_ref, field_sem),
        pltpu.make_async_copy(earlier_hbm, adjoint_ref, rest[-1]),
    ]
    for copy in copies:
        copy.start()

    def arrive():
        for copy in copies:
            copy.wait()

    def write_misfit(eight, rows):
        misfit_ref[pl.ds(eight * 16, 8, stride=2), :] = other_ref[pl.ds(eight * 8, 8), :]
        misfit_ref[pl.ds(eight * 16 + 1, 8, stride=2), :] = rows

    soundings(field_ref, block_ref, adjoint_ref, write_misfit, arrive, *scratch)
    write_edges(lambda t, row: cell_slab(adjoint_ref, t, row), *edges)


def observe(field, blocks, earlier=()):
    count = blocks.shape[0]
    tiles = count + WIDTH
    outs = [jax.ShapeDtypeStruct((PARTS * LEVELS, 256), jnp.float32)]
    outs += [jax.ShapeDtypeStruct((count * (2 if earlier else 1), LANES), jnp.float32)]
    return whole(
        second_soundings_body if earlier else first_soundings_body,
        outs + (EDGES if earlier else []),
        (field, blocks) + tuple(earlier),
        "second_soundings" if earlier else "first_soundings",
        in_hbm=(0, 2) if earlier else (0,),
        scratch=[
            pltpu.VMEM(field.shape, jnp.bfloat16),
            pltpu.SemaphoreType.DMA(()),
            pltpu.VMEM((GROUPS, tiles, ROWS, LANES), jnp.bfloat16),
            pltpu.VMEM((GROUPS, tiles, 8, LANES), jnp.float32),
            pltpu.VMEM((256, LANES), jnp.bfloat16),
            pltpu.VMEM((count, LANES), jnp.int32),
            pltpu.SMEM((count, LANES), jnp.int32),
            pltpu.SemaphoreType.DMA(()),
        ]
        + ([pltpu.SemaphoreType.DMA(())] if earlier else []),
        flops=15000000000,
    )


def per_device(
    initial, east_wind, north_wind, mixing, kernel, columns, observed, obs_weight, counts, targets
):
    lat_count = lax.axis_size("lat")
    lon_count = lax.axis_size("lon")
    sounds = kernel.shape[2]
    block_count = kernel.shape[0]
    device_count = lat_count * lon_count

    def exchange(array):
        return lax.all_to_all(array, ("lat", "lon"), split_axis=0, concat_axis=0, tiled=True)

    is_last = (lax.axis_index("lat") == lat_count - 1).astype(jnp.int32).reshape(1)
    winds_like = jax.ShapeDtypeStruct((2, LAT_CELLS, LEVELS, LANES), jnp.float32)

    def slabs_like(number):
        return jax.ShapeDtypeStruct((number, LEVELS, LANES), jnp.float32)

    grid = (is_last, initial, east_wind, north_wind, mixing)
    terms = [
        jax.ShapeDtypeStruct((14 + len(UP_LOW), LEVELS, LANES), jnp.bfloat16),
        jax.ShapeDtypeStruct((12 + len(DOWN_LOW), LEVELS, LANES), jnp.bfloat16),
    ]
    up, down = whole(rows_body, terms, grid, "rows", scalars=1)
    counts, up, down = lax.optimization_barrier((counts, up, down))
    from_south, from_north = shifted(up, 1, 0), shifted(down, -1, 0)
    slots = jax.ShapeDtypeStruct((device_count, ROWS, sounds), jnp.bfloat16)
    by_device = jax.ShapeDtypeStruct((device_count,), jnp.int32)
    heard = (kernel, columns, observed, obs_weight)
    scratch = [pltpu.VMEM((block_count, sounds), jnp.float32)] * 2
    scratch += [pltpu.VMEM((LANES, LANES), jnp.bfloat16)]
    by_block = jax.ShapeDtypeStruct((block_count, sounds), jnp.float32)
    out_first, place, tally, source_first, source_second = whole(
        pack_first_body,
        [slots, by_block, by_block, by_device, by_device],
        (targets[:, 0], counts) + heard,
        "pack_first",
        scratch=scratch
        + [pltpu.VMEM(kernel.shape, jnp.bfloat16), pltpu.SemaphoreType.DMA(())],
        scalars=2,
        scalar_outs=2,
        in_hbm=(2,),
        steps=device_count // TOGETHER,
    )
    (out_second,) = whole(
        pack_second_body,
        [slots],
        (source_second,) + heard + (place, tally),
        "pack_second",
        scratch=scratch,
        scalars=1,
    )
    out_first, from_south, from_north = lax.optimization_barrier(
        (out_first, from_south, from_north)
    )
    got_first = exchange(out_first)
    state, *rest = whole(
        arrange_body,
        [STATE, winds_like, winds_like, winds_like]
        + [slabs_like(3), slabs_like(3), slabs_like(14), slabs_like(12)],
        grid + (from_south, from_north),
        "arrange",
        scalars=1,
    )
    fields, (east, west, from_south, from_north) = tuple(rest[:3]), rest[3:]
    side_west, side_east = shifted(east, 0, 1), shifted(west, 0, -1)
    out_second, side_west, side_east = lax.optimization_barrier((out_second, side_west, side_east))
    got_second = exchange(out_second)
    (field,) = whole(
        forward_body,
        [jax.ShapeDtypeStruct((2 * PARTS * LEVELS, 256), jnp.bfloat16)],
        (state,) + fields + (east, west, from_south, from_north, side_west, side_east),
        "forward",
        scratch=[MIDDLE, pltpu.VMEM(STATE.shape, jnp.float32)],
    )
    earlier = observe(field, got_first)
    adjoint, misfit, up, down, own_east, own_west = observe(field, got_second, earlier)
    from_west, from_east = shifted(own_east, 0, 1), shifted(own_west, 0, -1)
    ends = jnp.stack([from_west, from_east])
    returned = exchange(misfit)
    (gradient,) = whole(
        adjoint_body,
        [jax.ShapeDtypeStruct(initial.shape, jnp.float32)],
        (adjoint,) + fields + (from_south, from_north, east, side_west, side_east)
        + (own_east, own_west, from_west, from_east)
        + (shifted(jnp.concatenate([up, ends]), 1, 0), shifted(jnp.concatenate([down, ends]), -1, 0)),
        "adjoint",
        scratch=[MIDDLE],
    )
    returned, gradient = lax.optimization_barrier((returned, gradient))
    (innovations,) = whole(
        innovations_body,
        [jax.ShapeDtypeStruct((block_count, sounds), jnp.float32)],
        (source_first, source_second, returned, place),
        "innovations",
        scratch=[pltpu.VMEM((block_count + 8, sounds), jnp.float32)],
        scalars=2,
    )
    return (gradient, innovations)


def solution(mesh):
    return jax.shard_map(
        per_device,
        mesh=mesh,
        in_specs=(
            P(None, None, "lat", "lon"),
            P(None, None, "lat", "lon"),
            P(None, None, "lat", "lon"),
            P(None, None, "lat", "lon"),
            P(("lat", "lon"), None, None),
            P(("lat", "lon"), None),
            P(("lat", "lon"), None),
            P(("lat", "lon"), None),
            P(("lat", "lon")),
            P(("lat", "lon"), None),
        ),
        out_specs=(P(None, None, "lat", "lon"), P(("lat", "lon"), None)),
        check_vma=False,
    )
```

```python
import functools

import jax
import jax.numpy as jnp
from jax import lax
from jax.experimental import pallas as pl
from jax.experimental.pallas import tpu as pltpu
from jax.sharding import PartitionSpec as P

LEVELS = 72
ROWS = 80
PAIR = 2 * LEVELS
TRACERS = 3
PARTS = 12
GROUPS = 6
GROUP_PARTS = PARTS // GROUPS
WIDTH = 4
LAT_CELLS = 8
LANES = 128


def lane_index():
    return lax.broadcasted_iota(jnp.int32, (LEVELS, LANES), 1)


def rolled(array, shift, axis):
    shift = shift % array.shape[axis]
    return pltpu.roll(array, shift, axis) if shift else array


def west_of(slab, halo, place):
    return jnp.where(lane_index() == 0, rolled(halo, -place, 1), rolled(slab, 1, 1))


def east_of(slab, halo, place):
    return jnp.where(
        lane_index() == LANES - 1, rolled(halo, LANES - 1 - place, 1), rolled(slab, -1, 1)
    )


SLOT = 32


def place_of(t, row):
    return t * 10 + row + 1


def packed(slabs, lane, base=0, first_row=0, rows=LAT_CELLS):
    out = jnp.zeros((LEVELS, LANES), jnp.float32)
    for i, slab in enumerate(slabs):
        place = base + place_of(i // rows, first_row + i % rows)
        out = jnp.where(lane_index() == place, rolled(slab, place - lane, 1), out)
    return out


def packed_wind(slabs, lane, base):
    one = packed(slabs, lane, base, -1, LAT_CELLS + 2)
    return one + rolled(one, 10, 1) + rolled(one, 20, 1)


def slot(array, number):
    return rolled(array, -SLOT * number, 1)


def with_corners(own, south, north):
    row = (lane_index() & (SLOT - 1)) % 10
    out = jnp.where(row == 0, rolled(south, -LAT_CELLS, 1), own)
    return jnp.where(row == 9, rolled(north, LAT_CELLS, 1), out)


def mixed(slab, coeff):
    upward = coeff * (rolled(slab, -1, 0) - slab)
    return upward - rolled(upward, 1, 0)


def forward(slab, left, right, above, below, east, before, north, south, coeff):
    zonal = jnp.maximum(east, 0.0) * slab + jnp.minimum(east, 0.0) * right
    zonal_before = jnp.maximum(before, 0.0) * left + jnp.minimum(before, 0.0) * slab
    merid = jnp.maximum(north, 0.0) * slab + jnp.minimum(north, 0.0) * above
    merid_before = jnp.maximum(south, 0.0) * below + jnp.minimum(south, 0.0) * slab
    return slab - (zonal - zonal_before) - (merid - merid_before) + mixed(slab, coeff)


def backward(slab, left, right, above, below, east, before, north, south, coeff):
    zonal = jnp.maximum(east, 0.0) * (right - slab) + jnp.minimum(before, 0.0) * (slab - left)
    merid = jnp.maximum(north, 0.0) * (above - slab) + jnp.minimum(south, 0.0) * (slab - below)
    return slab + zonal + merid + mixed(slab, coeff)


def write_edges(read, up_ref, down_ref, east_edge, west_edge):
    slabs = [read(t, row) for t in range(TRACERS) for row in range(LAT_CELLS)]
    for t in range(TRACERS):
        for i in range(2):
            up_ref[2 * t + i] = slabs[t * LAT_CELLS + LAT_CELLS - 2 + i]
            down_ref[2 * t + i] = slabs[t * LAT_CELLS + i]
    east_edge[...] = packed(slabs, LANES - 1) + packed(slabs, LANES - 2, SLOT)
    west_edge[...] = packed(slabs, 0) + packed(slabs, 1, SLOT)


def arrange_body(
    last_ref, initial_ref, east_ref, north_ref, mixing_ref, up_terms, down_terms,
    state_ref, east_out, north_out, mixing_out, east_edge, west_edge, up_ref, down_ref,
):
    joined_terms(up_terms, UP_LOW, up_ref)
    joined_terms(down_terms, DOWN_LOW, down_ref)
    slabs = []
    for t in range(TRACERS):
        slabs.append(up_ref[2 * t + 1])
        for row in range(LAT_CELLS):
            state_ref[t, row] = initial_ref[t, :, row, :]
            slabs.append(state_ref[t, row])
        slabs.append(down_ref[2 * t])
    rows = LAT_CELLS + 2
    east_edge[0] = packed(slabs, LANES - 1, 0, -1, rows) + packed(slabs, LANES - 2, SLOT, -1, rows)
    west_edge[0] = packed(slabs, 0, 0, -1, rows) + packed(slabs, 1, SLOT, -1, rows)
    for m in range(east_ref.shape[0]):
        for row in range(LAT_CELLS):
            east_out[m, row] = east_ref[m, :, row, :]
            north_out[m, row] = masked_north(last_ref, north_ref, m, row)
            mixing_out[m, row] = masked_mixing(mixing_ref, m, row)

        def column(ref, number):
            own = [ref[m, row] for row in range(LAT_CELLS)]
            return [up_ref[6 + 4 * m + number]] + own + [down_ref[6 + 3 * m + number]]

        east, mixing, north = column(east_out, 0), column(mixing_out, 1), column(north_out, 2)
        east_edge[1 + m] = (
            packed_wind(east, LANES - 1, 0)
            + packed_wind(mixing, LANES - 1, SLOT)
            + packed_wind(north, LANES - 1, 2 * SLOT)
            + packed_wind(east, LANES - 2, 3 * SLOT)
        )
        west_edge[1 + m] = (
            packed_wind(east, 0, 0)
            + packed_wind(mixing, 0, SLOT)
            + packed_wind(north, 0, 2 * SLOT)
        )


def masked_north(last_ref, north_ref, m, row):
    north = north_ref[m, :, row, :]
    if row == LAT_CELLS - 1:
        north = jnp.where(last_ref[0] > 0, jnp.float32(0.0), north)
    return north


def masked_mixing(mixing_ref, m, row):
    top = lax.broadcasted_iota(jnp.int32, (LEVELS, LANES), 0) == LEVELS - 1
    return jnp.where(top, jnp.float32(0.0), mixing_ref[m, :, row, :])


UP_LOW = (1, 3, 5, 8, 12)
DOWN_LOW = (0, 2, 4)


def rows_body(last_ref, initial_ref, east_ref, north_ref, mixing_ref, up_ref, down_ref):
    last = LAT_CELLS - 1
    up, down = [], []
    for t in range(TRACERS):
        for i in range(2):
            up.append(initial_ref[t, :, LAT_CELLS - 2 + i, :])
            down.append(initial_ref[t, :, i, :])
    for m in range(east_ref.shape[0]):
        for slabs, row in ((up, last), (down, 0)):
            slabs.append(east_ref[m, :, row, :])
            slabs.append(masked_mixing(mixing_ref, m, row))
            slabs.append(masked_north(last_ref, north_ref, m, row))
        up.append(masked_north(last_ref, north_ref, m, last - 1))
    for ref, slabs, lows in ((up_ref, up, UP_LOW), (down_ref, down, DOWN_LOW)):
        for i, slab in enumerate(slabs):
            high = slab.astype(jnp.bfloat16)
            ref[i] = high
            if i in lows:
                rest = slab - high.astype(jnp.float32)
                ref[len(slabs) + lows.index(i)] = rest.astype(jnp.bfloat16)


def joined_terms(terms_ref, lows, out_ref):
    count = out_ref.shape[0]
    for i in range(count):
        slab = terms_ref[i].astype(jnp.float32)
        if i in lows:
            slab = slab + terms_ref[count + lows.index(i)].astype(jnp.float32)
        out_ref[i] = slab


def two_steps(
    step, moments, read, winds, wind_up, wind_down, wind_east, sides,
    up_ref, down_ref, own_east, own_west, from_west, from_east, middle_ref, write,
):
    east_ref, north_ref, mixing_ref = winds

    def state(t, row):
        if row < 0:
            return up_ref[2 * t + row + 2]
        return read(t, row) if row < LAT_CELLS else down_ref[2 * t + row - LAT_CELLS]

    def wind(ref, number, m, row):
        if row < -1:
            return wind_up(4 * m + 3)
        if row < 0:
            return wind_up(4 * m + number)
        return ref[m, row] if row < LAT_CELLS else wind_down(3 * m + number)

    def winds_of(m, row, east_side):
        east = wind(east_ref, 0, m, row)
        return (
            east,
            west_of(east, east_side, place_of(0, row)),
            wind(north_ref, 2, m, row),
            wind(north_ref, 2, m, row - 1),
            wind(mixing_ref, 1, m, row),
        )

    m = moments[0]
    side_west, side_east = sides(m)
    for row in range(-1, LAT_CELLS + 1):
        local = winds_of(m, row, side_west)
        for t in range(TRACERS):
            slab, place = state(t, row), place_of(t, row)
            middle_ref[t, row + 1] = step(
                slab,
                west_of(slab, from_west, place),
                east_of(slab, from_east, place),
                state(t, row + 1),
                state(t, row - 1),
                *local,
            )

    def column(own, left, right, east, before, side):
        north = slot(side, 2)
        around = (rolled(own, -1, 1), rolled(own, 1, 1))
        return step(
            own, left, right, *around, east, before, north, rolled(north, 1, 1), slot(side, 1)
        )

    next_west = column(
        from_west, slot(from_west, 1), own_west, side_west, slot(side_west, 3), side_west
    )
    next_east = column(
        from_east, own_east, slot(from_east, 1), side_east, wind_east(m), side_east
    )
    m = moments[1]
    side_west, _ = sides(m)
    for row in range(LAT_CELLS):
        local = winds_of(m, row, side_west)
        for t in range(TRACERS):
            slab, place = middle_ref[t, row + 1], place_of(t, row)
            write(
                t,
                row,
                step(
                    slab,
                    west_of(slab, next_west, place),
                    east_of(slab, next_east, place),
                    middle_ref[t, row + 2],
                    middle_ref[t, row],
                    *local,
                ),
            )


def forward_body(
    state_ref, east_ref, north_ref, mixing_ref, own_east, own_west,
    up_ref, down_ref, from_west, from_east, field_ref, middle_ref, after_ref,
):
    def write(t, row, slab):
        after_ref[t, row] = slab

    two_steps(
        forward,
        (0, 1),
        lambda t, row: state_ref[t, row],
        (east_ref, north_ref, mixing_ref),
        lambda i: up_ref[6 + i],
        lambda i: down_ref[6 + i],
        lambda m: own_east[1 + m],
        lambda m: (from_west[1 + m], from_east[1 + m]),
        up_ref,
        down_ref,
        own_east[0],
        own_west[0],
        from_west[0],
        from_east[0],
        middle_ref,
        write,
    )
    for i in range(6):
        for low_row in range(2):
            slabs = []
            for p in (2 * i, 2 * i + 1):
                slabs.append(after_ref[p // 4, (p % 4) * 2 + low_row])
            both = jnp.concatenate(slabs, axis=0)
            high = both.astype(jnp.bfloat16)
            low = (both - high.astype(jnp.float32)).astype(jnp.bfloat16)
            lanes = slice(low_row * LANES, (low_row + 1) * LANES)
            field_ref[2 * i * PAIR : (2 * i + 1) * PAIR, lanes] = high
            field_ref[(2 * i + 1) * PAIR : (2 * i + 2) * PAIR, lanes] = low


def cell_slab(ref, t, row):
    first = (t * 4 + row // 2) * LEVELS
    return ref[first : first + LEVELS, (row % 2) * LANES : (row % 2 + 1) * LANES]


def adjoint_body(
    adjoint_ref, east_ref, north_ref, mixing_ref, wind_up, wind_down, wind_east, side_west, side_east,
    own_east, own_west, from_west, from_east, up_ref, down_ref, gradient_ref, middle_ref,
):
    def write(t, row, slab):
        gradient_ref[t, :, row, :] = slab

    two_steps(
        backward,
        (1, 0),
        lambda t, row: cell_slab(adjoint_ref, t, row),
        (east_ref, north_ref, mixing_ref),
        lambda i: wind_up[6 + i],
        lambda i: wind_down[6 + i],
        lambda m: wind_east[1 + m],
        lambda m: (side_west[1 + m], side_east[1 + m]),
        up_ref,
        down_ref,
        own_east[...],
        own_west[...],
        with_corners(from_west[...], up_ref[6], down_ref[6]),
        with_corners(from_east[...], up_ref[7], down_ref[7]),
        middle_ref,
        write,
    )


STATE = jax.ShapeDtypeStruct((TRACERS, LAT_CELLS, LEVELS, LANES), jnp.float32)
ROW_EDGE = jax.ShapeDtypeStruct((2 * TRACERS, LEVELS, LANES), jnp.float32)
COLUMN_EDGE = jax.ShapeDtypeStruct((LEVELS, LANES), jnp.float32)
EDGES = [ROW_EDGE, ROW_EDGE, COLUMN_EDGE, COLUMN_EDGE]
MIDDLE = pltpu.VMEM((TRACERS, LAT_CELLS + 2, LEVELS, LANES), jnp.float32)


def whole(body, outs, operands, name, scratch=(), scalars=0, flops=5000000, scalar_outs=0, in_hbm=(), steps=1, vmem_kib=65472):
    smem = pl.BlockSpec(memory_space=pltpu.SMEM)

    def vmem(array):
        zeros = (0,) * len(array.shape)
        return pl.BlockSpec(array.shape, lambda i: zeros, pipeline_mode=pl.Buffered(1))

    def spec(i, array):
        if i < scalars:
            return smem
        return pl.BlockSpec(memory_space=pl.ANY) if i in in_hbm else vmem(array)

    def out_spec(i, array):
        if i >= len(outs) - scalar_outs:
            return smem
        if i or steps == 1:
            return vmem(array)
        rest = array.shape[1:]
        return pl.BlockSpec(
            (array.shape[0] // steps,) + rest, lambda j: (j,) + (0,) * len(rest)
        )

    return pl.pallas_call(
        body,
        grid=(steps,),
        in_specs=[spec(i, array) for i, array in enumerate(operands)],
        out_specs=[out_spec(i, array) for i, array in enumerate(outs)],
        out_shape=outs,
        scratch_shapes=list(scratch),
        compiler_params=pltpu.CompilerParams(vmem_limit_bytes=vmem_kib << 10),
        cost_estimate=pl.CostEstimate(flops=flops, bytes_accessed=6000000, transcendentals=0),
        name=name,
    )(*operands)


def shifted(array, lat_by, lon_by):
    lat, lon = lax.axis_size("lat"), lax.axis_size("lon")
    if not lat_by:
        return lax.ppermute(array, "lon", [(j, (j + lon_by) % lon) for j in range(lon)])
    rows = [(i, i + lat_by) for i in range(lat) if 0 <= i + lat_by < lat]
    if not lon_by:
        return lax.ppermute(array, "lat", rows)
    pairs = [(i * lon + j, k * lon + (j + lon_by) % lon) for i, k in rows for j in range(lon)]
    return lax.ppermute(array, ("lat", "lon"), pairs)


def plan(targets_ref, counts_ref, columns_ref, place_ref, first_ref, second_ref, tally_ref):
    def clear(device, carry):
        first_ref[device] = -1
        second_ref[device] = -1
        return carry

    lax.fori_loop(0, first_ref.shape[0], clear, 0, unroll=8)

    def name(block, carry):
        target = targets_ref[block]
        known = first_ref[target]
        second_ref[target] = jnp.where(known < 0, -1, block)
        first_ref[target] = jnp.where(known < 0, block, known)
        return carry

    lax.fori_loop(0, targets_ref.shape[0], name, 0, unroll=8)
    part_id = lax.broadcasted_iota(jnp.int32, (16, LANES), 0)
    group = lax.broadcasted_iota(jnp.int32, (16, LANES), 1) * GROUP_PARTS
    of_group = (part_id >= group) & (part_id < group + GROUP_PARTS)
    lane = lax.broadcasted_iota(jnp.int32, (1, LANES), 1)
    row_id = lax.broadcasted_iota(jnp.int32, (8, LANES), 0)
    square = (LANES, 2 * LANES)
    earlier = lax.broadcasted_iota(jnp.int32, square, 0) < lax.broadcasted_iota(
        jnp.int32, square, 1
    )
    earlier = jnp.where(earlier, 1.0, 0.0).astype(jnp.bfloat16)

    def rank(eight, carry):
        parts = lax.shift_right_logical(columns_ref[pl.ds(eight * 8, 8), :], 8)
        rows = [parts[j : j + 1] for j in range(8)]
        lives = [lane < counts_ref[eight * 8 + j] for j in range(8)]
        members = [
            jnp.where((part_id == row) & live, 1.0, 0.0) for row, live in zip(rows, lives)
        ]
        sums = jnp.dot(
            jnp.concatenate(members, axis=0).astype(jnp.bfloat16),
            earlier,
            preferred_element_type=jnp.float32,
        )
        places = jnp.zeros((8, LANES), jnp.float32)
        tallies = jnp.zeros((8, LANES), jnp.float32)
        for j in range(8):
            own = sums[16 * j : 16 * j + 16]
            before = jnp.where(
                part_id == rows[j],
                own[:, :LANES],
                jnp.where(part_id < rows[j], own[:, LANES:], jnp.float32(0.0)),
            )
            place = jnp.sum(before, axis=0, keepdims=True)
            place = jnp.where(lives[j], place, jnp.float32(LANES))
            places = jnp.where(row_id == j, place, places)
            tally = jnp.sum(jnp.where(of_group, own[:, LANES:], 0.0), axis=0, keepdims=True)
            tallies = jnp.where(row_id == j, tally, tallies)
        place_ref[pl.ds(eight * 8, 8), :] = places
        tally_ref[pl.ds(eight * 8, 8), :] = tallies
        return carry

    lax.fori_loop(0, targets_ref.shape[0] // 8, rank, 0, unroll=4)


TOGETHER = 32


def widen(observed_ref, weight_ref, observed_wide, weight_wide, order_ref):
    observed_wide[...] = observed_ref[...].astype(jnp.float32)
    weight_wide[...] = weight_ref[...].astype(jnp.float32)
    order_ref[...] = (
        lax.broadcasted_iota(jnp.int32, (LANES, LANES), 0).astype(jnp.float32).astype(jnp.bfloat16)
    )


def pack(
    first, source_ref, kernel_ref, columns_ref, place_ref, tally_ref, out_ref, at,
    observed_wide, weight_wide, order_ref,
):
    row_id = lax.broadcasted_iota(jnp.int32, (8, LANES), 0)
    one, nil = jnp.bfloat16(1), jnp.bfloat16(0)

    def sorted_block(slot):
        source = source_ref[slot]
        block = jnp.maximum(source, 0)
        row = pl.ds(block, 1)
        cell = columns_ref[row, :]
        part = lax.shift_right_logical(cell, 8) + 1
        meta = jnp.where(row_id == 0, part.astype(jnp.float32), jnp.float32(0.0))
        meta = jnp.where(row_id == 1, (cell & 255).astype(jnp.float32), meta)
        meta = jnp.where(row_id == 2, observed_wide[row, :], meta)
        meta = jnp.where(row_id == 3, weight_wide[row, :], meta)
        rows = jnp.concatenate([kernel_ref[block].astype(jnp.float32), meta], axis=0)
        place = jnp.where(source >= 0, place_ref[row, :], jnp.float32(LANES)).astype(jnp.bfloat16)
        moved = jnp.where(order_ref[...] == jnp.broadcast_to(place, (LANES, LANES)), one, nil)
        result = lax.dot_general(
            rows.astype(jnp.bfloat16),
            moved,
            (((1,), (1,)), ((), ())),
            preferred_element_type=jnp.float32,
        )
        tally = jnp.where(source >= 0, tally_ref[row, :], jnp.float32(0.0))
        meta = jnp.where(row_id == 4, tally, result[LEVELS:])
        return jnp.concatenate([result[:LEVELS], meta], axis=0).astype(jnp.bfloat16)

    blocks = [sorted_block(first + j) for j in range(TOGETHER)]
    for j in range(TOGETHER):
        out_ref[at + j] = blocks[j]


def pack_second_body(
    source_ref, kernel_ref, columns_ref, observed_ref, weight_ref, place_ref, tally_ref, out_ref,
    *scratch,
):
    widen(observed_ref, weight_ref, *scratch)

    def step(i, carry):
        at = i * TOGETHER
        pack(
            at, source_ref, kernel_ref, columns_ref, place_ref, tally_ref, out_ref, at, *scratch
        )
        return carry

    lax.fori_loop(0, out_ref.shape[0] // TOGETHER, step, 0)


def pack_first_body(
    targets_ref, counts_ref, kernel_hbm, columns_ref, observed_ref, weight_ref,
    out_ref, place_ref, tally_ref, first_ref, second_ref,
    observed_wide, weight_wide, order_ref, kernel_ref, sem,
):
    scratch = (observed_wide, weight_wide, order_ref)

    @pl.when(pl.program_id(0) == 0)
    def _():
        copy = pltpu.make_async_copy(kernel_hbm, kernel_ref, sem)
        copy.start()
        widen(observed_ref, weight_ref, *scratch)
        plan(targets_ref, counts_ref, columns_ref, place_ref, first_ref, second_ref, tally_ref)
        copy.wait()

    pack(
        pl.program_id(0) * TOGETHER, first_ref, kernel_ref, columns_ref, place_ref, tally_ref,
        out_ref, 0, *scratch,
    )


def innovations_body(first_ref, second_ref, returned_ref, place_ref, out_ref, rows_ref):
    def one(device, carry):
        for rank, source_ref in enumerate((first_ref, second_ref)):
            source = source_ref[device]
            block = jnp.where(source >= 0, source, LANES)
            rows_ref[pl.ds(block, 1), :] = returned_ref[pl.ds(2 * device + rank, 1), :]
        return carry

    lax.fori_loop(0, first_ref.shape[0], one, 0, unroll=8)
    place = place_ref[...].astype(jnp.int32)
    live = place < LANES
    found = jnp.take_along_axis(
        rows_ref[: place.shape[0], :], jnp.where(live, place, 0), axis=1
    )
    out_ref[...] = jnp.where(live, found, jnp.float32(0.0))


def soundings(
    field_ref, block_ref, adjoint_ref, write_misfit, arrive,
    stream_ref, found_ref, cell_ref, tally_ref, count_ref, sem,
):
    n = WIDTH * LANES
    one, nil = jnp.bfloat16(1), jnp.bfloat16(0)
    lane = lax.broadcasted_iota(jnp.int32, (ROWS, LANES), 1)
    cell_ref[...] = (
        lax.broadcasted_iota(jnp.int32, (256, LANES), 0).astype(jnp.float32).astype(jnp.bfloat16)
    )
    empty = jnp.zeros((ROWS, LANES), jnp.bfloat16)
    eighth = lax.broadcasted_iota(jnp.int32, (8, LANES), 0)

    def tally(eight, carry):
        rows = jnp.zeros((8, LANES), jnp.float32)
        for j in range(8):
            meta = block_ref[eight * 8 + j][LEVELS:].astype(jnp.float32)
            rows = jnp.where(eighth == j, meta[4:5], rows)
        tally_ref[pl.ds(eight * 8, 8), :] = rows.astype(jnp.int32)
        return carry

    lax.fori_loop(0, block_ref.shape[0] // 8, tally, 0, unroll=4)
    copy = pltpu.make_async_copy(tally_ref, count_ref, sem)
    copy.start()
    copy.wait()

    def merge(block, carry):
        ends, tails = list(carry[0]), list(carry[1])
        values = block_ref[block]
        start = jnp.int32(0)
        for g in range(GROUPS):
            count = count_ref[block, g]
            tile, at = lax.shift_right_logical(ends[g], 7), ends[g] & (LANES - 1)
            turned = pltpu.roll(values, (at - start) & (LANES - 1), 1)
            joined = jnp.where(lane >= at, turned, tails[g])
            stream_ref[g, tile] = joined
            tails[g] = jnp.where(at + count >= LANES, turned, joined)
            ends[g] = ends[g] + count
            start = start + count
        return tuple(ends), tuple(tails)

    ends, tails = lax.fori_loop(
        0,
        block_ref.shape[0],
        merge,
        ((jnp.int32(0),) * GROUPS, (empty,) * GROUPS),
        unroll=8,
    )
    for g in range(GROUPS):
        tile, at = lax.shift_right_logical(ends[g], 7), ends[g] & (LANES - 1)
        stream_ref[g, tile] = jnp.where(lane < at, tails[g], empty)
        for j in range(1, WIDTH):
            stream_ref[g, tile + j] = empty

    arrive()

    def load(g, step):
        tiles = [stream_ref[g, step * WIDTH + i] for i in range(WIDTH)]
        profile = jnp.concatenate([t[:LEVELS] for t in tiles], axis=1)
        meta = jnp.concatenate([t[LEVELS:] for t in tiles], axis=1).astype(jnp.float32)
        part, cell, observed, weight = (meta[j : j + 1] for j in range(4))
        cell = cell.astype(jnp.bfloat16)
        hits = [
            cell_ref[...] == jnp.broadcast_to(cell[:, i * LANES : (i + 1) * LANES], (256, LANES))
            for i in range(WIDTH)
        ]
        pick = jnp.concatenate([jnp.where(hit, one, nil) for hit in hits], axis=1)
        return g, step, profile, part - 1.0, observed, weight, pick

    def gather(g, step, profile, part, observed, weight, pick):
        column = jnp.zeros((LEVELS, n), jnp.float32)
        for i in range(g * GROUP_PARTS // 2, (g + 1) * GROUP_PARTS // 2):
            found = jnp.dot(
                field_ref[2 * i * PAIR : 2 * (i + 1) * PAIR, :],
                pick,
                preferred_element_type=jnp.float32,
            )
            found = found[:PAIR] + found[PAIR:]
            column = jnp.where(part == 2.0 * i, found[:LEVELS], column)
            column = jnp.where(part == 2.0 * i + 1.0, found[LEVELS:], column)
        return column

    def force(column, g, step, profile, part, observed, weight, pick):
        wide = profile.astype(jnp.float32)
        model = jnp.sum(wide * column, axis=0, keepdims=True)
        misfit = model - observed
        for i in range(WIDTH):
            found_ref[g, step * WIDTH + i] = jnp.broadcast_to(
                misfit[:, i * LANES : (i + 1) * LANES], (8, LANES)
            )
        vector = wide * (weight * misfit)
        high = vector.astype(jnp.bfloat16)
        return high, (vector - high.astype(jnp.float32)).astype(jnp.bfloat16)

    def scatter(vector, g, step, profile, part, observed, weight, pick):
        high, low = (jnp.concatenate([term, term], axis=0) for term in vector)
        second = lax.broadcasted_iota(jnp.int32, (PAIR, n), 0) >= LEVELS
        part_row = (part - jnp.where(second, 1.0, 0.0)).astype(jnp.bfloat16)
        for i in range(g * GROUP_PARTS // 2, (g + 1) * GROUP_PARTS // 2):
            own = part_row == jnp.bfloat16(2 * i)
            sums = lax.dot_general(
                jnp.concatenate([jnp.where(own, high, nil), jnp.where(own, low, nil)], axis=0),
                pick,
                (((1,), (1,)), ((), ())),
                preferred_element_type=jnp.float32,
            )
            adjoint_ref[i * PAIR : (i + 1) * PAIR, :] += sums[:PAIR] + sums[PAIR:]

    def work(groups, step):
        loaded = [load(g, step) for g in groups]
        columns = [gather(*x) for x in loaded]
        vectors = [force(column, *x) for x, column in zip(loaded, columns)]
        for x, vector in zip(loaded, vectors):
            scatter(vector, *x)
        return 0

    steps = [lax.shift_right_logical(ends[g] + n - 1, n.bit_length() - 1) for g in range(GROUPS)]
    common = functools.reduce(jnp.minimum, steps)
    lax.fori_loop(0, common, lambda step, _: work(range(GROUPS), step), 0)
    for g in range(GROUPS):
        lax.fori_loop(common, steps[g], lambda step, _, g=g: work([g], step), 0)

    lane = lax.broadcasted_iota(jnp.int32, (8, LANES), 1)
    row_id = lax.broadcasted_iota(jnp.int32, (8, LANES), 0)

    def part_ways(eight, ends):
        ends = list(ends)
        rows = jnp.zeros((8, LANES), jnp.float32)
        for j in range(8):
            start = jnp.int32(0)
            row = jnp.zeros((8, LANES), jnp.float32)
            for g in range(GROUPS):
                count = count_ref[eight * 8 + j, g]
                tile, at = lax.shift_right_logical(ends[g], 7), ends[g] & (LANES - 1)
                values = jnp.where(lane >= at, found_ref[g, tile], found_ref[g, tile + 1])
                values = pltpu.roll(values, (start - at) & (LANES - 1), 1)
                row = jnp.where(lane >= start, values, row)
                ends[g] = ends[g] + count
                start = start + count
            rows = jnp.where(row_id == j, row, rows)
        write_misfit(eight, rows)
        return tuple(ends)

    lax.fori_loop(0, block_ref.shape[0] // 8, part_ways, (jnp.int32(0),) * GROUPS, unroll=2)


def first_soundings_body(
    field_hbm, block_ref, adjoint_ref, misfit_ref, field_ref, field_sem, *scratch
):
    copy = pltpu.make_async_copy(field_hbm, field_ref, field_sem)
    copy.start()
    adjoint_ref[...] = jnp.zeros_like(adjoint_ref)

    def write_misfit(eight, rows):
        misfit_ref[pl.ds(eight * 8, 8), :] = rows

    soundings(field_ref, block_ref, adjoint_ref, write_misfit, copy.wait, *scratch)


def second_soundings_body(
    field_hbm, block_ref, earlier_hbm, other_ref, adjoint_ref, misfit_ref, *rest
):
    edges, (field_ref, field_sem), scratch = rest[:4], rest[4:6], rest[6:-1]
    copies = [
        pltpu.make_async_copy(field_hbm, field_ref, field_sem),
        pltpu.make_async_copy(earlier_hbm, adjoint_ref, rest[-1]),
    ]
    for copy in copies:
        copy.start()

    def arrive():
        for copy in copies:
            copy.wait()

    def write_misfit(eight, rows):
        misfit_ref[pl.ds(eight * 16, 8, stride=2), :] = other_ref[pl.ds(eight * 8, 8), :]
        misfit_ref[pl.ds(eight * 16 + 1, 8, stride=2), :] = rows

    soundings(field_ref, block_ref, adjoint_ref, write_misfit, arrive, *scratch)
    write_edges(lambda t, row: cell_slab(adjoint_ref, t, row), *edges)


def observe(field, blocks, earlier=()):
    count = blocks.shape[0]
    tiles = count + WIDTH
    outs = [jax.ShapeDtypeStruct((PARTS * LEVELS, 256), jnp.float32)]
    outs += [jax.ShapeDtypeStruct((count * (2 if earlier else 1), LANES), jnp.float32)]
    return whole(
        second_soundings_body if earlier else first_soundings_body,
        outs + (EDGES if earlier else []),
        (field, blocks) + tuple(earlier),
        "second_soundings" if earlier else "first_soundings",
        in_hbm=(0, 2) if earlier else (0,),
        scratch=[
            pltpu.VMEM(field.shape, jnp.bfloat16),
            pltpu.SemaphoreType.DMA(()),
            pltpu.VMEM((GROUPS, tiles, ROWS, LANES), jnp.bfloat16),
            pltpu.VMEM((GROUPS, tiles, 8, LANES), jnp.float32),
            pltpu.VMEM((256, LANES), jnp.bfloat16),
            pltpu.VMEM((count, LANES), jnp.int32),
            pltpu.SMEM((count, LANES), jnp.int32),
            pltpu.SemaphoreType.DMA(()),
        ]
        + ([pltpu.SemaphoreType.DMA(())] if earlier else []),
        flops=15000000000,
    )


def per_device(
    initial, east_wind, north_wind, mixing, kernel, columns, observed, obs_weight, counts, targets
):
    lat_count = lax.axis_size("lat")
    lon_count = lax.axis_size("lon")
    sounds = kernel.shape[2]
    block_count = kernel.shape[0]
    device_count = lat_count * lon_count

    def exchange(array):
        return lax.all_to_all(array, ("lat", "lon"), split_axis=0, concat_axis=0, tiled=True)

    is_last = (lax.axis_index("lat") == lat_count - 1).astype(jnp.int32).reshape(1)
    winds_like = jax.ShapeDtypeStruct((2, LAT_CELLS, LEVELS, LANES), jnp.float32)

    def slabs_like(number):
        return jax.ShapeDtypeStruct((number, LEVELS, LANES), jnp.float32)

    grid = (is_last, initial, east_wind, north_wind, mixing)
    terms = [
        jax.ShapeDtypeStruct((14 + len(UP_LOW), LEVELS, LANES), jnp.bfloat16),
        jax.ShapeDtypeStruct((12 + len(DOWN_LOW), LEVELS, LANES), jnp.bfloat16),
    ]
    up, down = whole(rows_body, terms, grid, "rows", scalars=1)
    counts, up, down = lax.optimization_barrier((counts, up, down))
    from_south, from_north = shifted(up, 1, 0), shifted(down, -1, 0)
    slots = jax.ShapeDtypeStruct((device_count, ROWS, sounds), jnp.bfloat16)
    by_device = jax.ShapeDtypeStruct((device_count,), jnp.int32)
    heard = (kernel, columns, observed, obs_weight)
    scratch = [pltpu.VMEM((block_count, sounds), jnp.float32)] * 2
    scratch += [pltpu.VMEM((LANES, LANES), jnp.bfloat16)]
    by_block = jax.ShapeDtypeStruct((block_count, sounds), jnp.float32)
    out_first, place, tally, source_first, source_second = whole(
        pack_first_body,
        [slots, by_block, by_block, by_device, by_device],
        (targets[:, 0], counts) + heard,
        "pack_first",
        scratch=scratch
        + [pltpu.VMEM(kernel.shape, jnp.bfloat16), pltpu.SemaphoreType.DMA(())],
        scalars=2,
        scalar_outs=2,
        in_hbm=(2,),
        steps=device_count // TOGETHER,
    )
    (out_second,) = whole(
        pack_second_body,
        [slots],
        (source_second,) + heard + (place, tally),
        "pack_second",
        scratch=scratch,
        scalars=1,
    )
    out_first, from_south, from_north = lax.optimization_barrier(
        (out_first, from_south, from_north)
    )
    got_first = exchange(out_first)
    state, *rest = whole(
        arrange_body,
        [STATE, winds_like, winds_like, winds_like]
        + [slabs_like(3), slabs_like(3), slabs_like(14), slabs_like(12)],
        grid + (from_south, from_north),
        "arrange",
        scalars=1,
    )
    fields, (east, west, from_south, from_north) = tuple(rest[:3]), rest[3:]
    side_west, side_east = shifted(east, 0, 1), shifted(west, 0, -1)
    out_second, side_west, side_east = lax.optimization_barrier((out_second, side_west, side_east))
    got_second = exchange(out_second)
    (field,) = whole(
        forward_body,
        [jax.ShapeDtypeStruct((2 * PARTS * LEVELS, 256), jnp.bfloat16)],
        (state,) + fields + (east, west, from_south, from_north, side_west, side_east),
        "forward",
        scratch=[MIDDLE, pltpu.VMEM(STATE.shape, jnp.float32)],
    )
    earlier = observe(field, got_first)
    adjoint, misfit, up, down, own_east, own_west = observe(field, got_second, earlier)
    from_west, from_east = shifted(own_east, 0, 1), shifted(own_west, 0, -1)
    ends = jnp.stack([from_west, from_east])
    returned = exchange(misfit)
    (gradient,) = whole(
        adjoint_body,
        [jax.ShapeDtypeStruct(initial.shape, jnp.float32)],
        (adjoint,) + fields + (from_south, from_north, east, side_west, side_east)
        + (own_east, own_west, from_west, from_east)
        + (shifted(jnp.concatenate([up, ends]), 1, 0), shifted(jnp.concatenate([down, ends]), -1, 0)),
        "adjoint",
        scratch=[MIDDLE],
    )
    returned, gradient = lax.optimization_barrier((returned, gradient))
    (innovations,) = whole(
        innovations_body,
        [jax.ShapeDtypeStruct((block_count, sounds), jnp.float32)],
        (source_first, source_second, returned, place),
        "innovations",
        scratch=[pltpu.VMEM((block_count + 8, sounds), jnp.float32)],
        scalars=2,
    )
    return (gradient, innovations)


def solution(mesh):
    return jax.shard_map(
        per_device,
        mesh=mesh,
        in_specs=(
            P(None, None, "lat", "lon"),
            P(None, None, "lat", "lon"),
            P(None, None, "lat", "lon"),
            P(None, None, "lat", "lon"),
            P(("lat", "lon"), None, None),
            P(("lat", "lon"), None),
            P(("lat", "lon"), None),
            P(("lat", "lon"), None),
            P(("lat", "lon")),
            P(("lat", "lon"), None),
        ),
        out_specs=(P(None, None, "lat", "lon"), P(("lat", "lon"), None)),
        check_vma=False,
    )
```

```python
import functools

import jax
import jax.numpy as jnp
from jax import lax
from jax.experimental import pallas as pl
from jax.experimental.pallas import tpu as pltpu
from jax.sharding import PartitionSpec as P

LEVELS = 72
ROWS = 80
PAIR = 2 * LEVELS
TRACERS = 3
PARTS = 12
GROUPS = 6
GROUP_PARTS = PARTS // GROUPS
WIDTH = 4
LAT_CELLS = 8
LANES = 128


def lane_index():
    return lax.broadcasted_iota(jnp.int32, (LEVELS, LANES), 1)


def rolled(array, shift, axis):
    shift = shift % array.shape[axis]
    return pltpu.roll(array, shift, axis) if shift else array


def west_of(slab, halo, place):
    return jnp.where(lane_index() == 0, rolled(halo, -place, 1), rolled(slab, 1, 1))


def east_of(slab, halo, place):
    return jnp.where(
        lane_index() == LANES - 1, rolled(halo, LANES - 1 - place, 1), rolled(slab, -1, 1)
    )


SLOT = 32


def place_of(t, row):
    return t * 10 + row + 1


def packed(slabs, lane, base=0, first_row=0, rows=LAT_CELLS):
    out = jnp.zeros((LEVELS, LANES), jnp.float32)
    for i, slab in enumerate(slabs):
        place = base + place_of(i // rows, first_row + i % rows)
        out = jnp.where(lane_index() == place, rolled(slab, place - lane, 1), out)
    return out


def packed_wind(slabs, lane, base):
    one = packed(slabs, lane, base, -1, LAT_CELLS + 2)
    return one + rolled(one, 10, 1) + rolled(one, 20, 1)


def slot(array, number):
    return rolled(array, -SLOT * number, 1)


def with_corners(own, south, north):
    row = (lane_index() & (SLOT - 1)) % 10
    out = jnp.where(row == 0, rolled(south, -LAT_CELLS, 1), own)
    return jnp.where(row == 9, rolled(north, LAT_CELLS, 1), out)


def mixed(slab, coeff):
    upward = coeff * (rolled(slab, -1, 0) - slab)
    return upward - rolled(upward, 1, 0)


def forward(slab, left, right, above, below, east, before, north, south, coeff):
    zonal = jnp.maximum(east, 0.0) * slab + jnp.minimum(east, 0.0) * right
    zonal_before = jnp.maximum(before, 0.0) * left + jnp.minimum(before, 0.0) * slab
    merid = jnp.maximum(north, 0.0) * slab + jnp.minimum(north, 0.0) * above
    merid_before = jnp.maximum(south, 0.0) * below + jnp.minimum(south, 0.0) * slab
    return slab - (zonal - zonal_before) - (merid - merid_before) + mixed(slab, coeff)


def backward(slab, left, right, above, below, east, before, north, south, coeff):
    zonal = jnp.maximum(east, 0.0) * (right - slab) + jnp.minimum(before, 0.0) * (slab - left)
    merid = jnp.maximum(north, 0.0) * (above - slab) + jnp.minimum(south, 0.0) * (slab - below)
    return slab + zonal + merid + mixed(slab, coeff)


def write_edges(read, up_ref, down_ref, east_edge, west_edge):
    slabs = [read(t, row) for t in range(TRACERS) for row in range(LAT_CELLS)]
    for t in range(TRACERS):
        for i in range(2):
            up_ref[2 * t + i] = slabs[t * LAT_CELLS + LAT_CELLS - 2 + i]
            down_ref[2 * t + i] = slabs[t * LAT_CELLS + i]
    east_edge[...] = packed(slabs, LANES - 1) + packed(slabs, LANES - 2, SLOT)
    west_edge[...] = packed(slabs, 0) + packed(slabs, 1, SLOT)


def arrange_body(
    last_ref, initial_ref, east_ref, north_ref, mixing_ref, up_terms, down_terms,
    state_ref, east_out, north_out, mixing_out, east_edge, west_edge, up_ref, down_ref,
):
    joined_terms(up_terms, UP_LOW, up_ref)
    joined_terms(down_terms, DOWN_LOW, down_ref)
    slabs = []
    for t in range(TRACERS):
        slabs.append(up_ref[2 * t + 1])
        for row in range(LAT_CELLS):
            state_ref[t, row] = initial_ref[t, :, row, :]
            slabs.append(state_ref[t, row])
        slabs.append(down_ref[2 * t])
    rows = LAT_CELLS + 2
    east_edge[0] = packed(slabs, LANES - 1, 0, -1, rows) + packed(slabs, LANES - 2, SLOT, -1, rows)
    west_edge[0] = packed(slabs, 0, 0, -1, rows) + packed(slabs, 1, SLOT, -1, rows)
    for m in range(east_ref.shape[0]):
        for row in range(LAT_CELLS):
            east_out[m, row] = east_ref[m, :, row, :]
            north_out[m, row] = masked_north(last_ref, north_ref, m, row)
            mixing_out[m, row] = masked_mixing(mixing_ref, m, row)

        def column(ref, number):
            own = [ref[m, row] for row in range(LAT_CELLS)]
            return [up_ref[6 + 4 * m + number]] + own + [down_ref[6 + 3 * m + number]]

        east, mixing, north = column(east_out, 0), column(mixing_out, 1), column(north_out, 2)
        east_edge[1 + m] = (
            packed_wind(east, LANES - 1, 0)
            + packed_wind(mixing, LANES - 1, SLOT)
            + packed_wind(north, LANES - 1, 2 * SLOT)
            + packed_wind(east, LANES - 2, 3 * SLOT)
        )
        west_edge[1 + m] = (
            packed_wind(east, 0, 0)
            + packed_wind(mixing, 0, SLOT)
            + packed_wind(north, 0, 2 * SLOT)
        )


def masked_north(last_ref, north_ref, m, row):
    north = north_ref[m, :, row, :]
    if row == LAT_CELLS - 1:
        north = jnp.where(last_ref[0] > 0, jnp.float32(0.0), north)
    return north


def masked_mixing(mixing_ref, m, row):
    top = lax.broadcasted_iota(jnp.int32, (LEVELS, LANES), 0) == LEVELS - 1
    return jnp.where(top, jnp.float32(0.0), mixing_ref[m, :, row, :])


UP_LOW = (1, 3, 5, 8, 12)
DOWN_LOW = (0, 2, 4)


def rows_body(last_ref, initial_ref, east_ref, north_ref, mixing_ref, up_ref, down_ref):
    last = LAT_CELLS - 1
    up, down = [], []
    for t in range(TRACERS):
        for i in range(2):
            up.append(initial_ref[t, :, LAT_CELLS - 2 + i, :])
            down.append(initial_ref[t, :, i, :])
    for m in range(east_ref.shape[0]):
        for slabs, row in ((up, last), (down, 0)):
            slabs.append(east_ref[m, :, row, :])
            slabs.append(masked_mixing(mixing_ref, m, row))
            slabs.append(masked_north(last_ref, north_ref, m, row))
        up.append(masked_north(last_ref, north_ref, m, last - 1))
    for ref, slabs, lows in ((up_ref, up, UP_LOW), (down_ref, down, DOWN_LOW)):
        for i, slab in enumerate(slabs):
            high = slab.astype(jnp.bfloat16)
            ref[i] = high
            if i in lows:
                rest = slab - high.astype(jnp.float32)
                ref[len(slabs) + lows.index(i)] = rest.astype(jnp.bfloat16)


def joined_terms(terms_ref, lows, out_ref):
    count = out_ref.shape[0]
    for i in range(count):
        slab = terms_ref[i].astype(jnp.float32)
        if i in lows:
            slab = slab + terms_ref[count + lows.index(i)].astype(jnp.float32)
        out_ref[i] = slab


def two_steps(
    step, moments, read, winds, wind_up, wind_down, wind_east, sides,
    up_ref, down_ref, own_east, own_west, from_west, from_east, middle_ref, write,
):
    east_ref, north_ref, mixing_ref = winds

    def state(t, row):
        if row < 0:
            return up_ref[2 * t + row + 2]
        return read(t, row) if row < LAT_CELLS else down_ref[2 * t + row - LAT_CELLS]

    def wind(ref, number, m, row):
        if row < -1:
            return wind_up(4 * m + 3)
        if row < 0:
            return wind_up(4 * m + number)
        return ref[m, row] if row < LAT_CELLS else wind_down(3 * m + number)

    def winds_of(m, row, east_side):
        east = wind(east_ref, 0, m, row)
        return (
            east,
            west_of(east, east_side, place_of(0, row)),
            wind(north_ref, 2, m, row),
            wind(north_ref, 2, m, row - 1),
            wind(mixing_ref, 1, m, row),
        )

    m = moments[0]
    side_west, side_east = sides(m)
    for row in range(-1, LAT_CELLS + 1):
        local = winds_of(m, row, side_west)
        for t in range(TRACERS):
            slab, place = state(t, row), place_of(t, row)
            middle_ref[t, row + 1] = step(
                slab,
                west_of(slab, from_west, place),
                east_of(slab, from_east, place),
                state(t, row + 1),
                state(t, row - 1),
                *local,
            )

    def column(own, left, right, east, before, side):
        north = slot(side, 2)
        around = (rolled(own, -1, 1), rolled(own, 1, 1))
        return step(
            own, left, right, *around, east, before, north, rolled(north, 1, 1), slot(side, 1)
        )

    next_west = column(
        from_west, slot(from_west, 1), own_west, side_west, slot(side_west, 3), side_west
    )
    next_east = column(
        from_east, own_east, slot(from_east, 1), side_east, wind_east(m), side_east
    )
    m = moments[1]
    side_west, _ = sides(m)
    for row in range(LAT_CELLS):
        local = winds_of(m, row, side_west)
        for t in range(TRACERS):
            slab, place = middle_ref[t, row + 1], place_of(t, row)
            write(
                t,
                row,
                step(
                    slab,
                    west_of(slab, next_west, place),
                    east_of(slab, next_east, place),
                    middle_ref[t, row + 2],
                    middle_ref[t, row],
                    *local,
                ),
            )


def forward_body(
    state_ref, east_ref, north_ref, mixing_ref, own_east, own_west,
    up_ref, down_ref, from_west, from_east, field_ref, middle_ref, after_ref,
):
    def write(t, row, slab):
        after_ref[t, row] = slab

    two_steps(
        forward,
        (0, 1),
        lambda t, row: state_ref[t, row],
        (east_ref, north_ref, mixing_ref),
        lambda i: up_ref[6 + i],
        lambda i: down_ref[6 + i],
        lambda m: own_east[1 + m],
        lambda m: (from_west[1 + m], from_east[1 + m]),
        up_ref,
        down_ref,
        own_east[0],
        own_west[0],
        from_west[0],
        from_east[0],
        middle_ref,
        write,
    )
    for i in range(6):
        for low_row in range(2):
            slabs = []
            for p in (2 * i, 2 * i + 1):
                slabs.append(after_ref[p // 4, (p % 4) * 2 + low_row])
            both = jnp.concatenate(slabs, axis=0)
            high = both.astype(jnp.bfloat16)
            low = (both - high.astype(jnp.float32)).astype(jnp.bfloat16)
            lanes = slice(low_row * LANES, (low_row + 1) * LANES)
            field_ref[2 * i * PAIR : (2 * i + 1) * PAIR, lanes] = high
            field_ref[(2 * i + 1) * PAIR : (2 * i + 2) * PAIR, lanes] = low


def cell_slab(ref, t, row):
    first = (t * 4 + row // 2) * LEVELS
    return ref[first : first + LEVELS, (row % 2) * LANES : (row % 2 + 1) * LANES]


def adjoint_body(
    adjoint_ref, east_ref, north_ref, mixing_ref, wind_up, wind_down, wind_east, side_west, side_east,
    own_east, own_west, from_west, from_east, up_ref, down_ref, gradient_ref, middle_ref,
):
    def write(t, row, slab):
        gradient_ref[t, :, row, :] = slab

    two_steps(
        backward,
        (1, 0),
        lambda t, row: cell_slab(adjoint_ref, t, row),
        (east_ref, north_ref, mixing_ref),
        lambda i: wind_up[6 + i],
        lambda i: wind_down[6 + i],
        lambda m: wind_east[1 + m],
        lambda m: (side_west[1 + m], side_east[1 + m]),
        up_ref,
        down_ref,
        own_east[...],
        own_west[...],
        with_corners(from_west[...], up_ref[6], down_ref[6]),
        with_corners(from_east[...], up_ref[7], down_ref[7]),
        middle_ref,
        write,
    )


STATE = jax.ShapeDtypeStruct((TRACERS, LAT_CELLS, LEVELS, LANES), jnp.float32)
ROW_EDGE = jax.ShapeDtypeStruct((2 * TRACERS, LEVELS, LANES), jnp.float32)
COLUMN_EDGE = jax.ShapeDtypeStruct((LEVELS, LANES), jnp.float32)
EDGES = [ROW_EDGE, ROW_EDGE, COLUMN_EDGE, COLUMN_EDGE]
MIDDLE = pltpu.VMEM((TRACERS, LAT_CELLS + 2, LEVELS, LANES), jnp.float32)


def whole(body, outs, operands, name, scratch=(), scalars=0, flops=5000000, scalar_outs=0, in_hbm=(), steps=1, vmem_kib=65472):
    smem = pl.BlockSpec(memory_space=pltpu.SMEM)

    def vmem(array):
        zeros = (0,) * len(array.shape)
        return pl.BlockSpec(array.shape, lambda i: zeros, pipeline_mode=pl.Buffered(1))

    def spec(i, array):
        if i < scalars:
            return smem
        return pl.BlockSpec(memory_space=pl.ANY) if i in in_hbm else vmem(array)

    def out_spec(i, array):
        if i >= len(outs) - scalar_outs:
            return smem
        if i or steps == 1:
            return vmem(array)
        rest = array.shape[1:]
        return pl.BlockSpec(
            (array.shape[0] // steps,) + rest, lambda j: (j,) + (0,) * len(rest)
        )

    return pl.pallas_call(
        body,
        grid=(steps,),
        in_specs=[spec(i, array) for i, array in enumerate(operands)],
        out_specs=[out_spec(i, array) for i, array in enumerate(outs)],
        out_shape=outs,
        scratch_shapes=list(scratch),
        compiler_params=pltpu.CompilerParams(vmem_limit_bytes=vmem_kib << 10),
        cost_estimate=pl.CostEstimate(flops=flops, bytes_accessed=6000000, transcendentals=0),
        name=name,
    )(*operands)


def shifted(array, lat_by, lon_by):
    lat, lon = lax.axis_size("lat"), lax.axis_size("lon")
    if not lat_by:
        return lax.ppermute(array, "lon", [(j, (j + lon_by) % lon) for j in range(lon)])
    rows = [(i, i + lat_by) for i in range(lat) if 0 <= i + lat_by < lat]
    if not lon_by:
        return lax.ppermute(array, "lat", rows)
    pairs = [(i * lon + j, k * lon + (j + lon_by) % lon) for i, k in rows for j in range(lon)]
    return lax.ppermute(array, ("lat", "lon"), pairs)


def plan(targets_ref, counts_ref, columns_ref, place_ref, first_ref, second_ref, tally_ref):
    def clear(device, carry):
        first_ref[device] = -1
        second_ref[device] = -1
        return carry

    lax.fori_loop(0, first_ref.shape[0], clear, 0, unroll=8)

    def name(block, carry):
        target = targets_ref[block]
        known = first_ref[target]
        second_ref[target] = jnp.where(known < 0, -1, block)
        first_ref[target] = jnp.where(known < 0, block, known)
        return carry

    lax.fori_loop(0, targets_ref.shape[0], name, 0, unroll=8)
    part_id = lax.broadcasted_iota(jnp.int32, (16, LANES), 0)
    group = lax.broadcasted_iota(jnp.int32, (16, LANES), 1) * GROUP_PARTS
    of_group = (part_id >= group) & (part_id < group + GROUP_PARTS)
    lane = lax.broadcasted_iota(jnp.int32, (1, LANES), 1)
    row_id = lax.broadcasted_iota(jnp.int32, (8, LANES), 0)
    square = (LANES, 2 * LANES)
    earlier = lax.broadcasted_iota(jnp.int32, square, 0) < lax.broadcasted_iota(
        jnp.int32, square, 1
    )
    earlier = jnp.where(earlier, 1.0, 0.0).astype(jnp.bfloat16)

    def rank(eight, carry):
        parts = lax.shift_right_logical(columns_ref[pl.ds(eight * 8, 8), :], 8)
        rows = [parts[j : j + 1] for j in range(8)]
        lives = [lane < counts_ref[eight * 8 + j] for j in range(8)]
        members = [
            jnp.where((part_id == row) & live, 1.0, 0.0) for row, live in zip(rows, lives)
        ]
        sums = jnp.dot(
            jnp.concatenate(members, axis=0).astype(jnp.bfloat16),
            earlier,
            preferred_element_type=jnp.float32,
        )
        places = jnp.zeros((8, LANES), jnp.float32)
        tallies = jnp.zeros((8, LANES), jnp.float32)
        for j in range(8):
            own = sums[16 * j : 16 * j + 16]
            before = jnp.where(
                part_id == rows[j],
                own[:, :LANES],
                jnp.where(part_id < rows[j], own[:, LANES:], jnp.float32(0.0)),
            )
            place = jnp.sum(before, axis=0, keepdims=True)
            place = jnp.where(lives[j], place, jnp.float32(LANES))
            places = jnp.where(row_id == j, place, places)
            tally = jnp.sum(jnp.where(of_group, own[:, LANES:], 0.0), axis=0, keepdims=True)
            tallies = jnp.where(row_id == j, tally, tallies)
        place_ref[pl.ds(eight * 8, 8), :] = places
        tally_ref[pl.ds(eight * 8, 8), :] = tallies
        return carry

    lax.fori_loop(0, targets_ref.shape[0] // 8, rank, 0, unroll=4)


TOGETHER = 32


def widen(observed_ref, weight_ref, observed_wide, weight_wide, order_ref):
    observed_wide[...] = observed_ref[...].astype(jnp.float32)
    weight_wide[...] = weight_ref[...].astype(jnp.float32)
    order_ref[...] = (
        lax.broadcasted_iota(jnp.int32, (LANES, LANES), 0).astype(jnp.float32).astype(jnp.bfloat16)
    )


def pack(
    first, source_ref, kernel_ref, columns_ref, place_ref, tally_ref, out_ref, at,
    observed_wide, weight_wide, order_ref,
):
    row_id = lax.broadcasted_iota(jnp.int32, (8, LANES), 0)
    one, nil = jnp.bfloat16(1), jnp.bfloat16(0)

    def sorted_block(slot):
        source = source_ref[slot]
        block = jnp.maximum(source, 0)
        row = pl.ds(block, 1)
        cell = columns_ref[row, :]
        part = lax.shift_right_logical(cell, 8) + 1
        meta = jnp.where(row_id == 0, part.astype(jnp.float32), jnp.float32(0.0))
        meta = jnp.where(row_id == 1, (cell & 255).astype(jnp.float32), meta)
        meta = jnp.where(row_id == 2, observed_wide[row, :], meta)
        meta = jnp.where(row_id == 3, weight_wide[row, :], meta)
        rows = jnp.concatenate([kernel_ref[block].astype(jnp.float32), meta], axis=0)
        place = jnp.where(source >= 0, place_ref[row, :], jnp.float32(LANES)).astype(jnp.bfloat16)
        moved = jnp.where(order_ref[...] == jnp.broadcast_to(place, (LANES, LANES)), one, nil)
        result = lax.dot_general(
            rows.astype(jnp.bfloat16),
            moved,
            (((1,), (1,)), ((), ())),
            preferred_element_type=jnp.float32,
        )
        tally = jnp.where(source >= 0, tally_ref[row, :], jnp.float32(0.0))
        meta = jnp.where(row_id == 4, tally, result[LEVELS:])
        return jnp.concatenate([result[:LEVELS], meta], axis=0).astype(jnp.bfloat16)

    blocks = [sorted_block(first + j) for j in range(TOGETHER)]
    for j in range(TOGETHER):
        out_ref[at + j] = blocks[j]


def pack_second_body(
    source_ref, kernel_ref, columns_ref, observed_ref, weight_ref, place_ref, tally_ref, out_ref,
    *scratch,
):
    widen(observed_ref, weight_ref, *scratch)

    def step(i, carry):
        at = i * TOGETHER
        pack(
            at, source_ref, kernel_ref, columns_ref, place_ref, tally_ref, out_ref, at, *scratch
        )
        return carry

    lax.fori_loop(0, out_ref.shape[0] // TOGETHER, step, 0)


def pack_first_body(
    targets_ref, counts_ref, kernel_hbm, columns_ref, observed_ref, weight_ref,
    out_ref, place_ref, tally_ref, first_ref, second_ref,
    observed_wide, weight_wide, order_ref, kernel_ref, sem,
):
    scratch = (observed_wide, weight_wide, order_ref)

    @pl.when(pl.program_id(0) == 0)
    def _():
        copy = pltpu.make_async_copy(kernel_hbm, kernel_ref, sem)
        copy.start()
        widen(observed_ref, weight_ref, *scratch)
        plan(targets_ref, counts_ref, columns_ref, place_ref, first_ref, second_ref, tally_ref)
        copy.wait()

    pack(
        pl.program_id(0) * TOGETHER, first_ref, kernel_ref, columns_ref, place_ref, tally_ref,
        out_ref, 0, *scratch,
    )


def innovations_body(first_ref, second_ref, returned_ref, place_ref, out_ref, rows_ref):
    def one(device, carry):
        for rank, source_ref in enumerate((first_ref, second_ref)):
            source = source_ref[device]
            block = jnp.where(source >= 0, source, LANES)
            rows_ref[pl.ds(block, 1), :] = returned_ref[pl.ds(2 * device + rank, 1), :]
        return carry

    lax.fori_loop(0, first_ref.shape[0], one, 0, unroll=8)
    place = place_ref[...].astype(jnp.int32)
    live = place < LANES
    found = jnp.take_along_axis(
        rows_ref[: place.shape[0], :], jnp.where(live, place, 0), axis=1
    )
    out_ref[...] = jnp.where(live, found, jnp.float32(0.0))


def soundings(
    field_ref, block_ref, adjoint_ref, write_misfit, arrive,
    stream_ref, found_ref, cell_ref, tally_ref, count_ref, sem,
):
    n = WIDTH * LANES
    one, nil = jnp.bfloat16(1), jnp.bfloat16(0)
    lane = lax.broadcasted_iota(jnp.int32, (ROWS, LANES), 1)
    cell_ref[...] = (
        lax.broadcasted_iota(jnp.int32, (256, LANES), 0).astype(jnp.float32).astype(jnp.bfloat16)
    )
    empty = jnp.zeros((ROWS, LANES), jnp.bfloat16)
    eighth = lax.broadcasted_iota(jnp.int32, (8, LANES), 0)

    def tally(eight, carry):
        rows = jnp.zeros((8, LANES), jnp.float32)
        for j in range(8):
            meta = block_ref[eight * 8 + j][LEVELS:].astype(jnp.float32)
            rows = jnp.where(eighth == j, meta[4:5], rows)
        tally_ref[pl.ds(eight * 8, 8), :] = rows.astype(jnp.int32)
        return carry

    lax.fori_loop(0, block_ref.shape[0] // 8, tally, 0, unroll=4)
    copy = pltpu.make_async_copy(tally_ref, count_ref, sem)
    copy.start()
    copy.wait()

    def merge(block, carry):
        ends, tails = list(carry[0]), list(carry[1])
        values = block_ref[block]
        start = jnp.int32(0)
        for g in range(GROUPS):
            count = count_ref[block, g]
            tile, at = lax.shift_right_logical(ends[g], 7), ends[g] & (LANES - 1)
            turned = pltpu.roll(values, (at - start) & (LANES - 1), 1)
            joined = jnp.where(lane >= at, turned, tails[g])
            stream_ref[g, tile] = joined
            tails[g] = jnp.where(at + count >= LANES, turned, joined)
            ends[g] = ends[g] + count
            start = start + count
        return tuple(ends), tuple(tails)

    ends, tails = lax.fori_loop(
        0,
        block_ref.shape[0],
        merge,
        ((jnp.int32(0),) * GROUPS, (empty,) * GROUPS),
        unroll=16,
    )
    for g in range(GROUPS):
        tile, at = lax.shift_right_logical(ends[g], 7), ends[g] & (LANES - 1)
        stream_ref[g, tile] = jnp.where(lane < at, tails[g], empty)
        for j in range(1, WIDTH):
            stream_ref[g, tile + j] = empty

    arrive()

    def load(g, step):
        tiles = [stream_ref[g, step * WIDTH + i] for i in range(WIDTH)]
        profile = jnp.concatenate([t[:LEVELS] for t in tiles], axis=1)
        meta = jnp.concatenate([t[LEVELS:] for t in tiles], axis=1).astype(jnp.float32)
        part, cell, observed, weight = (meta[j : j + 1] for j in range(4))
        cell = cell.astype(jnp.bfloat16)
        hits = [
            cell_ref[...] == jnp.broadcast_to(cell[:, i * LANES : (i + 1) * LANES], (256, LANES))
            for i in range(WIDTH)
        ]
        pick = jnp.concatenate([jnp.where(hit, one, nil) for hit in hits], axis=1)
        return g, step, profile, part - 1.0, observed, weight, pick

    def gather(g, step, profile, part, observed, weight, pick):
        column = jnp.zeros((LEVELS, n), jnp.float32)
        for i in range(g * GROUP_PARTS // 2, (g + 1) * GROUP_PARTS // 2):
            found = jnp.dot(
                field_ref[2 * i * PAIR : 2 * (i + 1) * PAIR, :],
                pick,
                preferred_element_type=jnp.float32,
            )
            found = found[:PAIR] + found[PAIR:]
            column = jnp.where(part == 2.0 * i, found[:LEVELS], column)
            column = jnp.where(part == 2.0 * i + 1.0, found[LEVELS:], column)
        return column

    def force(column, g, step, profile, part, observed, weight, pick):
        wide = profile.astype(jnp.float32)
        model = jnp.sum(wide * column, axis=0, keepdims=True)
        misfit = model - observed
        for i in range(WIDTH):
            found_ref[g, step * WIDTH + i] = jnp.broadcast_to(
                misfit[:, i * LANES : (i + 1) * LANES], (8, LANES)
            )
        vector = wide * (weight * misfit)
        high = vector.astype(jnp.bfloat16)
        return high, (vector - high.astype(jnp.float32)).astype(jnp.bfloat16)

    def scatter(vector, g, step, profile, part, observed, weight, pick):
        high, low = (jnp.concatenate([term, term], axis=0) for term in vector)
        second = lax.broadcasted_iota(jnp.int32, (PAIR, n), 0) >= LEVELS
        part_row = (part - jnp.where(second, 1.0, 0.0)).astype(jnp.bfloat16)
        for i in range(g * GROUP_PARTS // 2, (g + 1) * GROUP_PARTS // 2):
            own = part_row == jnp.bfloat16(2 * i)
            sums = lax.dot_general(
                jnp.concatenate([jnp.where(own, high, nil), jnp.where(own, low, nil)], axis=0),
                pick,
                (((1,), (1,)), ((), ())),
                preferred_element_type=jnp.float32,
            )
            adjoint_ref[i * PAIR : (i + 1) * PAIR, :] += sums[:PAIR] + sums[PAIR:]

    def work(groups, step):
        loaded = [load(g, step) for g in groups]
        columns = [gather(*x) for x in loaded]
        vectors = [force(column, *x) for x, column in zip(loaded, columns)]
        for x, vector in zip(loaded, vectors):
            scatter(vector, *x)
        return 0

    steps = [lax.shift_right_logical(ends[g] + n - 1, n.bit_length() - 1) for g in range(GROUPS)]
    common = functools.reduce(jnp.minimum, steps)
    lax.fori_loop(0, common, lambda step, _: work(range(GROUPS), step), 0)
    for g in range(GROUPS):
        lax.fori_loop(common, steps[g], lambda step, _, g=g: work([g], step), 0)

    lane = lax.broadcasted_iota(jnp.int32, (8, LANES), 1)
    row_id = lax.broadcasted_iota(jnp.int32, (8, LANES), 0)

    def part_ways(eight, ends):
        ends = list(ends)
        rows = jnp.zeros((8, LANES), jnp.float32)
        for j in range(8):
            start = jnp.int32(0)
            row = jnp.zeros((8, LANES), jnp.float32)
            for g in range(GROUPS):
                count = count_ref[eight * 8 + j, g]
                tile, at = lax.shift_right_logical(ends[g], 7), ends[g] & (LANES - 1)
                values = jnp.where(lane >= at, found_ref[g, tile], found_ref[g, tile + 1])
                values = pltpu.roll(values, (start - at) & (LANES - 1), 1)
                row = jnp.where(lane >= start, values, row)
                ends[g] = ends[g] + count
                start = start + count
            rows = jnp.where(row_id == j, row, rows)
        write_misfit(eight, rows)
        return tuple(ends)

    lax.fori_loop(0, block_ref.shape[0] // 8, part_ways, (jnp.int32(0),) * GROUPS, unroll=4)


def first_soundings_body(
    field_hbm, block_ref, adjoint_ref, misfit_ref, field_ref, field_sem, *scratch
):
    copy = pltpu.make_async_copy(field_hbm, field_ref, field_sem)
    copy.start()
    adjoint_ref[...] = jnp.zeros_like(adjoint_ref)

    def write_misfit(eight, rows):
        misfit_ref[pl.ds(eight * 8, 8), :] = rows

    soundings(field_ref, block_ref, adjoint_ref, write_misfit, copy.wait, *scratch)


def second_soundings_body(
    field_hbm, block_ref, earlier_hbm, other_ref, adjoint_ref, misfit_ref, *rest
):
    edges, (field_ref, field_sem), scratch = rest[:4], rest[4:6], rest[6:-1]
    copies = [
        pltpu.make_async_copy(field_hbm, field_ref, field_sem),
        pltpu.make_async_copy(earlier_hbm, adjoint_ref, rest[-1]),
    ]
    for copy in copies:
        copy.start()

    def arrive():
        for copy in copies:
            copy.wait()

    def write_misfit(eight, rows):
        misfit_ref[pl.ds(eight * 16, 8, stride=2), :] = other_ref[pl.ds(eight * 8, 8), :]
        misfit_ref[pl.ds(eight * 16 + 1, 8, stride=2), :] = rows

    soundings(field_ref, block_ref, adjoint_ref, write_misfit, arrive, *scratch)
    write_edges(lambda t, row: cell_slab(adjoint_ref, t, row), *edges)


def observe(field, blocks, earlier=()):
    count = blocks.shape[0]
    tiles = count + WIDTH
    outs = [jax.ShapeDtypeStruct((PARTS * LEVELS, 256), jnp.float32)]
    outs += [jax.ShapeDtypeStruct((count * (2 if earlier else 1), LANES), jnp.float32)]
    return whole(
        second_soundings_body if earlier else first_soundings_body,
        outs + (EDGES if earlier else []),
        (field, blocks) + tuple(earlier),
        "second_soundings" if earlier else "first_soundings",
        in_hbm=(0, 2) if earlier else (0,),
        scratch=[
            pltpu.VMEM(field.shape, jnp.bfloat16),
            pltpu.SemaphoreType.DMA(()),
            pltpu.VMEM((GROUPS, tiles, ROWS, LANES), jnp.bfloat16),
            pltpu.VMEM((GROUPS, tiles, 8, LANES), jnp.float32),
            pltpu.VMEM((256, LANES), jnp.bfloat16),
            pltpu.VMEM((count, LANES), jnp.int32),
            pltpu.SMEM((count, LANES), jnp.int32),
            pltpu.SemaphoreType.DMA(()),
        ]
        + ([pltpu.SemaphoreType.DMA(())] if earlier else []),
        flops=15000000000,
    )


def per_device(
    initial, east_wind, north_wind, mixing, kernel, columns, observed, obs_weight, counts, targets
):
    lat_count = lax.axis_size("lat")
    lon_count = lax.axis_size("lon")
    sounds = kernel.shape[2]
    block_count = kernel.shape[0]
    device_count = lat_count * lon_count

    def exchange(array):
        return lax.all_to_all(array, ("lat", "lon"), split_axis=0, concat_axis=0, tiled=True)

    is_last = (lax.axis_index("lat") == lat_count - 1).astype(jnp.int32).reshape(1)
    winds_like = jax.ShapeDtypeStruct((2, LAT_CELLS, LEVELS, LANES), jnp.float32)

    def slabs_like(number):
        return jax.ShapeDtypeStruct((number, LEVELS, LANES), jnp.float32)

    grid = (is_last, initial, east_wind, north_wind, mixing)
    terms = [
        jax.ShapeDtypeStruct((14 + len(UP_LOW), LEVELS, LANES), jnp.bfloat16),
        jax.ShapeDtypeStruct((12 + len(DOWN_LOW), LEVELS, LANES), jnp.bfloat16),
    ]
    up, down = whole(rows_body, terms, grid, "rows", scalars=1)
    counts, up, down = lax.optimization_barrier((counts, up, down))
    from_south, from_north = shifted(up, 1, 0), shifted(down, -1, 0)
    slots = jax.ShapeDtypeStruct((device_count, ROWS, sounds), jnp.bfloat16)
    by_device = jax.ShapeDtypeStruct((device_count,), jnp.int32)
    heard = (kernel, columns, observed, obs_weight)
    scratch = [pltpu.VMEM((block_count, sounds), jnp.float32)] * 2
    scratch += [pltpu.VMEM((LANES, LANES), jnp.bfloat16)]
    by_block = jax.ShapeDtypeStruct((block_count, sounds), jnp.float32)
    out_first, place, tally, source_first, source_second = whole(
        pack_first_body,
        [slots, by_block, by_block, by_device, by_device],
        (targets[:, 0], counts) + heard,
        "pack_first",
        scratch=scratch
        + [pltpu.VMEM(kernel.shape, jnp.bfloat16), pltpu.SemaphoreType.DMA(())],
        scalars=2,
        scalar_outs=2,
        in_hbm=(2,),
        steps=device_count // TOGETHER,
    )
    (out_second,) = whole(
        pack_second_body,
        [slots],
        (source_second,) + heard + (place, tally),
        "pack_second",
        scratch=scratch,
        scalars=1,
    )
    out_first, from_south, from_north = lax.optimization_barrier(
        (out_first, from_south, from_north)
    )
    got_first = exchange(out_first)
    state, *rest = whole(
        arrange_body,
        [STATE, winds_like, winds_like, winds_like]
        + [slabs_like(3), slabs_like(3), slabs_like(14), slabs_like(12)],
        grid + (from_south, from_north),
        "arrange",
        scalars=1,
    )
    fields, (east, west, from_south, from_north) = tuple(rest[:3]), rest[3:]
    side_west, side_east = shifted(east, 0, 1), shifted(west, 0, -1)
    out_second, side_west, side_east = lax.optimization_barrier((out_second, side_west, side_east))
    got_second = exchange(out_second)
    (field,) = whole(
        forward_body,
        [jax.ShapeDtypeStruct((2 * PARTS * LEVELS, 256), jnp.bfloat16)],
        (state,) + fields + (east, west, from_south, from_north, side_west, side_east),
        "forward",
        scratch=[MIDDLE, pltpu.VMEM(STATE.shape, jnp.float32)],
    )
    earlier = observe(field, got_first)
    adjoint, misfit, up, down, own_east, own_west = observe(field, got_second, earlier)
    from_west, from_east = shifted(own_east, 0, 1), shifted(own_west, 0, -1)
    ends = jnp.stack([from_west, from_east])
    returned = exchange(misfit)
    (gradient,) = whole(
        adjoint_body,
        [jax.ShapeDtypeStruct(initial.shape, jnp.float32)],
        (adjoint,) + fields + (from_south, from_north, east, side_west, side_east)
        + (own_east, own_west, from_west, from_east)
        + (shifted(jnp.concatenate([up, ends]), 1, 0), shifted(jnp.concatenate([down, ends]), -1, 0)),
        "adjoint",
        scratch=[MIDDLE],
    )
    returned, gradient = lax.optimization_barrier((returned, gradient))
    (innovations,) = whole(
        innovations_body,
        [jax.ShapeDtypeStruct((block_count, sounds), jnp.float32)],
        (source_first, source_second, returned, place),
        "innovations",
        scratch=[pltpu.VMEM((block_count + 8, sounds), jnp.float32)],
        scalars=2,
    )
    return (gradient, innovations)


def solution(mesh):
    return jax.shard_map(
        per_device,
        mesh=mesh,
        in_specs=(
            P(None, None, "lat", "lon"),
            P(None, None, "lat", "lon"),
            P(None, None, "lat", "lon"),
            P(None, None, "lat", "lon"),
            P(("lat", "lon"), None, None),
            P(("lat", "lon"), None),
            P(("lat", "lon"), None),
            P(("lat", "lon"), None),
            P(("lat", "lon")),
            P(("lat", "lon"), None),
        ),
        out_specs=(P(None, None, "lat", "lon"), P(("lat", "lon"), None)),
        check_vma=False,
    )
```

```python
import functools

import jax
import jax.numpy as jnp
from jax import lax
from jax.experimental import pallas as pl
from jax.experimental.pallas import tpu as pltpu
from jax.sharding import PartitionSpec as P

LEVELS = 72
ROWS = 80
PAIR = 2 * LEVELS
TRACERS = 3
PARTS = 12
GROUPS = 6
GROUP_PARTS = PARTS // GROUPS
WIDTH = 4
LAT_CELLS = 8
LANES = 128


def lane_index():
    return lax.broadcasted_iota(jnp.int32, (LEVELS, LANES), 1)


def rolled(array, shift, axis):
    shift = shift % array.shape[axis]
    return pltpu.roll(array, shift, axis) if shift else array


def west_of(slab, halo, place):
    return jnp.where(lane_index() == 0, rolled(halo, -place, 1), rolled(slab, 1, 1))


def east_of(slab, halo, place):
    return jnp.where(
        lane_index() == LANES - 1, rolled(halo, LANES - 1 - place, 1), rolled(slab, -1, 1)
    )


SLOT = 32


def place_of(t, row):
    return t * 10 + row + 1


def packed(slabs, lane, base=0, first_row=0, rows=LAT_CELLS):
    out = jnp.zeros((LEVELS, LANES), jnp.float32)
    for i, slab in enumerate(slabs):
        place = base + place_of(i // rows, first_row + i % rows)
        out = jnp.where(lane_index() == place, rolled(slab, place - lane, 1), out)
    return out


def packed_wind(slabs, lane, base):
    one = packed(slabs, lane, base, -1, LAT_CELLS + 2)
    return one + rolled(one, 10, 1) + rolled(one, 20, 1)


def slot(array, number):
    return rolled(array, -SLOT * number, 1)


def with_corners(own, south, north):
    row = (lane_index() & (SLOT - 1)) % 10
    out = jnp.where(row == 0, rolled(south, -LAT_CELLS, 1), own)
    return jnp.where(row == 9, rolled(north, LAT_CELLS, 1), out)


def mixed(slab, coeff):
    upward = coeff * (rolled(slab, -1, 0) - slab)
    return upward - rolled(upward, 1, 0)


def forward(slab, left, right, above, below, east, before, north, south, coeff):
    zonal = jnp.maximum(east, 0.0) * slab + jnp.minimum(east, 0.0) * right
    zonal_before = jnp.maximum(before, 0.0) * left + jnp.minimum(before, 0.0) * slab
    merid = jnp.maximum(north, 0.0) * slab + jnp.minimum(north, 0.0) * above
    merid_before = jnp.maximum(south, 0.0) * below + jnp.minimum(south, 0.0) * slab
    return slab - (zonal - zonal_before) - (merid - merid_before) + mixed(slab, coeff)


def backward(slab, left, right, above, below, east, before, north, south, coeff):
    zonal = jnp.maximum(east, 0.0) * (right - slab) + jnp.minimum(before, 0.0) * (slab - left)
    merid = jnp.maximum(north, 0.0) * (above - slab) + jnp.minimum(south, 0.0) * (slab - below)
    return slab + zonal + merid + mixed(slab, coeff)


def write_edges(read, up_ref, down_ref, east_edge, west_edge):
    slabs = [read(t, row) for t in range(TRACERS) for row in range(LAT_CELLS)]
    for t in range(TRACERS):
        for i in range(2):
            up_ref[2 * t + i] = slabs[t * LAT_CELLS + LAT_CELLS - 2 + i]
            down_ref[2 * t + i] = slabs[t * LAT_CELLS + i]
    east_edge[...] = packed(slabs, LANES - 1) + packed(slabs, LANES - 2, SLOT)
    west_edge[...] = packed(slabs, 0) + packed(slabs, 1, SLOT)


def arrange_body(
    last_ref, initial_ref, east_ref, north_ref, mixing_ref, up_terms, down_terms,
    state_ref, east_out, north_out, mixing_out, east_edge, west_edge, up_ref, down_ref,
):
    joined_terms(up_terms, UP_LOW, up_ref)
    joined_terms(down_terms, DOWN_LOW, down_ref)
    slabs = []
    for t in range(TRACERS):
        slabs.append(up_ref[2 * t + 1])
        for row in range(LAT_CELLS):
            state_ref[t, row] = initial_ref[t, :, row, :]
            slabs.append(state_ref[t, row])
        slabs.append(down_ref[2 * t])
    rows = LAT_CELLS + 2
    east_edge[0] = packed(slabs, LANES - 1, 0, -1, rows) + packed(slabs, LANES - 2, SLOT, -1, rows)
    west_edge[0] = packed(slabs, 0, 0, -1, rows) + packed(slabs, 1, SLOT, -1, rows)
    for m in range(east_ref.shape[0]):
        for row in range(LAT_CELLS):
            east_out[m, row] = east_ref[m, :, row, :]
            north_out[m, row] = masked_north(last_ref, north_ref, m, row)
            mixing_out[m, row] = masked_mixing(mixing_ref, m, row)

        def column(ref, number):
            own = [ref[m, row] for row in range(LAT_CELLS)]
            return [up_ref[6 + 4 * m + number]] + own + [down_ref[6 + 3 * m + number]]

        east, mixing, north = column(east_out, 0), column(mixing_out, 1), column(north_out, 2)
        east_edge[1 + m] = (
            packed_wind(east, LANES - 1, 0)
            + packed_wind(mixing, LANES - 1, SLOT)
            + packed_wind(north, LANES - 1, 2 * SLOT)
            + packed_wind(east, LANES - 2, 3 * SLOT)
        )
        west_edge[1 + m] = (
            packed_wind(east, 0, 0)
            + packed_wind(mixing, 0, SLOT)
            + packed_wind(north, 0, 2 * SLOT)
        )


def masked_north(last_ref, north_ref, m, row):
    north = north_ref[m, :, row, :]
    if row == LAT_CELLS - 1:
        north = jnp.where(last_ref[0] > 0, jnp.float32(0.0), north)
    return north


def masked_mixing(mixing_ref, m, row):
    top = lax.broadcasted_iota(jnp.int32, (LEVELS, LANES), 0) == LEVELS - 1
    return jnp.where(top, jnp.float32(0.0), mixing_ref[m, :, row, :])


UP_LOW = (1, 3, 5, 8, 12)
DOWN_LOW = (0, 2, 4)


def rows_body(last_ref, initial_ref, east_ref, north_ref, mixing_ref, up_ref, down_ref):
    last = LAT_CELLS - 1
    up, down = [], []
    for t in range(TRACERS):
        for i in range(2):
            up.append(initial_ref[t, :, LAT_CELLS - 2 + i, :])
            down.append(initial_ref[t, :, i, :])
    for m in range(east_ref.shape[0]):
        for slabs, row in ((up, last), (down, 0)):
            slabs.append(east_ref[m, :, row, :])
            slabs.append(masked_mixing(mixing_ref, m, row))
            slabs.append(masked_north(last_ref, north_ref, m, row))
        up.append(masked_north(last_ref, north_ref, m, last - 1))
    for ref, slabs, lows in ((up_ref, up, UP_LOW), (down_ref, down, DOWN_LOW)):
        for i, slab in enumerate(slabs):
            high = slab.astype(jnp.bfloat16)
            ref[i] = high
            if i in lows:
                rest = slab - high.astype(jnp.float32)
                ref[len(slabs) + lows.index(i)] = rest.astype(jnp.bfloat16)


def joined_terms(terms_ref, lows, out_ref):
    count = out_ref.shape[0]
    for i in range(count):
        slab = terms_ref[i].astype(jnp.float32)
        if i in lows:
            slab = slab + terms_ref[count + lows.index(i)].astype(jnp.float32)
        out_ref[i] = slab


def two_steps(
    step, moments, read, winds, wind_up, wind_down, wind_east, sides,
    up_ref, down_ref, own_east, own_west, from_west, from_east, middle_ref, write,
):
    east_ref, north_ref, mixing_ref = winds

    def state(t, row):
        if row < 0:
            return up_ref[2 * t + row + 2]
        return read(t, row) if row < LAT_CELLS else down_ref[2 * t + row - LAT_CELLS]

    def wind(ref, number, m, row):
        if row < -1:
            return wind_up(4 * m + 3)
        if row < 0:
            return wind_up(4 * m + number)
        return ref[m, row] if row < LAT_CELLS else wind_down(3 * m + number)

    def winds_of(m, row, east_side):
        east = wind(east_ref, 0, m, row)
        return (
            east,
            west_of(east, east_side, place_of(0, row)),
            wind(north_ref, 2, m, row),
            wind(north_ref, 2, m, row - 1),
            wind(mixing_ref, 1, m, row),
        )

    m = moments[0]
    side_west, side_east = sides(m)
    for row in range(-1, LAT_CELLS + 1):
        local = winds_of(m, row, side_west)
        for t in range(TRACERS):
            slab, place = state(t, row), place_of(t, row)
            middle_ref[t, row + 1] = step(
                slab,
                west_of(slab, from_west, place),
                east_of(slab, from_east, place),
                state(t, row + 1),
                state(t, row - 1),
                *local,
            )

    def column(own, left, right, east, before, side):
        north = slot(side, 2)
        around = (rolled(own, -1, 1), rolled(own, 1, 1))
        return step(
            own, left, right, *around, east, before, north, rolled(north, 1, 1), slot(side, 1)
        )

    next_west = column(
        from_west, slot(from_west, 1), own_west, side_west, slot(side_west, 3), side_west
    )
    next_east = column(
        from_east, own_east, slot(from_east, 1), side_east, wind_east(m), side_east
    )
    m = moments[1]
    side_west, _ = sides(m)
    for row in range(LAT_CELLS):
        local = winds_of(m, row, side_west)
        for t in range(TRACERS):
            slab, place = middle_ref[t, row + 1], place_of(t, row)
            write(
                t,
                row,
                step(
                    slab,
                    west_of(slab, next_west, place),
                    east_of(slab, next_east, place),
                    middle_ref[t, row + 2],
                    middle_ref[t, row],
                    *local,
                ),
            )


def forward_body(
    state_ref, east_ref, north_ref, mixing_ref, own_east, own_west,
    up_ref, down_ref, from_west, from_east, field_ref, middle_ref, after_ref,
):
    def write(t, row, slab):
        after_ref[t, row] = slab

    two_steps(
        forward,
        (0, 1),
        lambda t, row: state_ref[t, row],
        (east_ref, north_ref, mixing_ref),
        lambda i: up_ref[6 + i],
        lambda i: down_ref[6 + i],
        lambda m: own_east[1 + m],
        lambda m: (from_west[1 + m], from_east[1 + m]),
        up_ref,
        down_ref,
        own_east[0],
        own_west[0],
        from_west[0],
        from_east[0],
        middle_ref,
        write,
    )
    for i in range(6):
        for low_row in range(2):
            slabs = []
            for p in (2 * i, 2 * i + 1):
                slabs.append(after_ref[p // 4, (p % 4) * 2 + low_row])
            both = jnp.concatenate(slabs, axis=0)
            high = both.astype(jnp.bfloat16)
            low = (both - high.astype(jnp.float32)).astype(jnp.bfloat16)
            lanes = slice(low_row * LANES, (low_row + 1) * LANES)
            field_ref[2 * i * PAIR : (2 * i + 1) * PAIR, lanes] = high
            field_ref[(2 * i + 1) * PAIR : (2 * i + 2) * PAIR, lanes] = low


def cell_slab(ref, t, row):
    first = (t * 4 + row // 2) * LEVELS
    return ref[first : first + LEVELS, (row % 2) * LANES : (row % 2 + 1) * LANES]


def adjoint_body(
    adjoint_ref, east_ref, north_ref, mixing_ref, wind_up, wind_down, wind_east, side_west, side_east,
    own_east, own_west, from_west, from_east, up_ref, down_ref, gradient_ref, middle_ref,
):
    def write(t, row, slab):
        gradient_ref[t, :, row, :] = slab

    two_steps(
        backward,
        (1, 0),
        lambda t, row: cell_slab(adjoint_ref, t, row),
        (east_ref, north_ref, mixing_ref),
        lambda i: wind_up[6 + i],
        lambda i: wind_down[6 + i],
        lambda m: wind_east[1 + m],
        lambda m: (side_west[1 + m], side_east[1 + m]),
        up_ref,
        down_ref,
        own_east[...],
        own_west[...],
        with_corners(from_west[...], up_ref[6], down_ref[6]),
        with_corners(from_east[...], up_ref[7], down_ref[7]),
        middle_ref,
        write,
    )


STATE = jax.ShapeDtypeStruct((TRACERS, LAT_CELLS, LEVELS, LANES), jnp.float32)
ROW_EDGE = jax.ShapeDtypeStruct((2 * TRACERS, LEVELS, LANES), jnp.float32)
COLUMN_EDGE = jax.ShapeDtypeStruct((LEVELS, LANES), jnp.float32)
EDGES = [ROW_EDGE, ROW_EDGE, COLUMN_EDGE, COLUMN_EDGE]
MIDDLE = pltpu.VMEM((TRACERS, LAT_CELLS + 2, LEVELS, LANES), jnp.float32)


def whole(body, outs, operands, name, scratch=(), scalars=0, flops=5000000, scalar_outs=0, in_hbm=(), steps=1, vmem_kib=65472):
    smem = pl.BlockSpec(memory_space=pltpu.SMEM)

    def vmem(array):
        zeros = (0,) * len(array.shape)
        return pl.BlockSpec(array.shape, lambda i: zeros, pipeline_mode=pl.Buffered(1))

    def spec(i, array):
        if i < scalars:
            return smem
        return pl.BlockSpec(memory_space=pl.ANY) if i in in_hbm else vmem(array)

    def out_spec(i, array):
        if i >= len(outs) - scalar_outs:
            return smem
        if i or steps == 1:
            return vmem(array)
        rest = array.shape[1:]
        return pl.BlockSpec(
            (array.shape[0] // steps,) + rest, lambda j: (j,) + (0,) * len(rest)
        )

    return pl.pallas_call(
        body,
        grid=(steps,),
        in_specs=[spec(i, array) for i, array in enumerate(operands)],
        out_specs=[out_spec(i, array) for i, array in enumerate(outs)],
        out_shape=outs,
        scratch_shapes=list(scratch),
        compiler_params=pltpu.CompilerParams(vmem_limit_bytes=vmem_kib << 10),
        cost_estimate=pl.CostEstimate(flops=flops, bytes_accessed=6000000, transcendentals=0),
        name=name,
    )(*operands)


def shifted(array, lat_by, lon_by):
    lat, lon = lax.axis_size("lat"), lax.axis_size("lon")
    if not lat_by:
        return lax.ppermute(array, "lon", [(j, (j + lon_by) % lon) for j in range(lon)])
    rows = [(i, i + lat_by) for i in range(lat) if 0 <= i + lat_by < lat]
    if not lon_by:
        return lax.ppermute(array, "lat", rows)
    pairs = [(i * lon + j, k * lon + (j + lon_by) % lon) for i, k in rows for j in range(lon)]
    return lax.ppermute(array, ("lat", "lon"), pairs)


def plan(targets_ref, counts_ref, columns_ref, place_ref, first_ref, second_ref, tally_ref):
    def clear(device, carry):
        first_ref[device] = -1
        second_ref[device] = -1
        return carry

    lax.fori_loop(0, first_ref.shape[0], clear, 0, unroll=8)

    def name(block, carry):
        target = targets_ref[block]
        known = first_ref[target]
        second_ref[target] = jnp.where(known < 0, -1, block)
        first_ref[target] = jnp.where(known < 0, block, known)
        return carry

    lax.fori_loop(0, targets_ref.shape[0], name, 0, unroll=8)
    part_id = lax.broadcasted_iota(jnp.int32, (16, LANES), 0)
    group = lax.broadcasted_iota(jnp.int32, (16, LANES), 1) * GROUP_PARTS
    of_group = (part_id >= group) & (part_id < group + GROUP_PARTS)
    lane = lax.broadcasted_iota(jnp.int32, (1, LANES), 1)
    row_id = lax.broadcasted_iota(jnp.int32, (8, LANES), 0)
    square = (LANES, 2 * LANES)
    earlier = lax.broadcasted_iota(jnp.int32, square, 0) < lax.broadcasted_iota(
        jnp.int32, square, 1
    )
    earlier = jnp.where(earlier, 1.0, 0.0).astype(jnp.bfloat16)

    def rank(eight, carry):
        parts = lax.shift_right_logical(columns_ref[pl.ds(eight * 8, 8), :], 8)
        rows = [parts[j : j + 1] for j in range(8)]
        lives = [lane < counts_ref[eight * 8 + j] for j in range(8)]
        members = [
            jnp.where((part_id == row) & live, 1.0, 0.0) for row, live in zip(rows, lives)
        ]
        sums = jnp.dot(
            jnp.concatenate(members, axis=0).astype(jnp.bfloat16),
            earlier,
            preferred_element_type=jnp.float32,
        )
        places = jnp.zeros((8, LANES), jnp.float32)
        tallies = jnp.zeros((8, LANES), jnp.float32)
        for j in range(8):
            own = sums[16 * j : 16 * j + 16]
            before = jnp.where(
                part_id == rows[j],
                own[:, :LANES],
                jnp.where(part_id < rows[j], own[:, LANES:], jnp.float32(0.0)),
            )
            place = jnp.sum(before, axis=0, keepdims=True)
            place = jnp.where(lives[j], place, jnp.float32(LANES))
            places = jnp.where(row_id == j, place, places)
            tally = jnp.sum(jnp.where(of_group, own[:, LANES:], 0.0), axis=0, keepdims=True)
            tallies = jnp.where(row_id == j, tally, tallies)
        place_ref[pl.ds(eight * 8, 8), :] = places
        tally_ref[pl.ds(eight * 8, 8), :] = tallies
        return carry

    lax.fori_loop(0, targets_ref.shape[0] // 8, rank, 0, unroll=8)


TOGETHER = 32


def widen(observed_ref, weight_ref, observed_wide, weight_wide, order_ref):
    observed_wide[...] = observed_ref[...].astype(jnp.float32)
    weight_wide[...] = weight_ref[...].astype(jnp.float32)
    order_ref[...] = (
        lax.broadcasted_iota(jnp.int32, (LANES, LANES), 0).astype(jnp.float32).astype(jnp.bfloat16)
    )


def pack(
    first, source_ref, kernel_ref, columns_ref, place_ref, tally_ref, out_ref, at,
    observed_wide, weight_wide, order_ref,
):
    row_id = lax.broadcasted_iota(jnp.int32, (8, LANES), 0)
    one, nil = jnp.bfloat16(1), jnp.bfloat16(0)

    def sorted_block(slot):
        source = source_ref[slot]
        block = jnp.maximum(source, 0)
        row = pl.ds(block, 1)
        cell = columns_ref[row, :]
        part = lax.shift_right_logical(cell, 8) + 1
        meta = jnp.where(row_id == 0, part.astype(jnp.float32), jnp.float32(0.0))
        meta = jnp.where(row_id == 1, (cell & 255).astype(jnp.float32), meta)
        meta = jnp.where(row_id == 2, observed_wide[row, :], meta)
        meta = jnp.where(row_id == 3, weight_wide[row, :], meta)
        rows = jnp.concatenate([kernel_ref[block].astype(jnp.float32), meta], axis=0)
        place = jnp.where(source >= 0, place_ref[row, :], jnp.float32(LANES)).astype(jnp.bfloat16)
        moved = jnp.where(order_ref[...] == jnp.broadcast_to(place, (LANES, LANES)), one, nil)
        result = lax.dot_general(
            rows.astype(jnp.bfloat16),
            moved,
            (((1,), (1,)), ((), ())),
            preferred_element_type=jnp.float32,
        )
        tally = jnp.where(source >= 0, tally_ref[row, :], jnp.float32(0.0))
        meta = jnp.where(row_id == 4, tally, result[LEVELS:])
        return jnp.concatenate([result[:LEVELS], meta], axis=0).astype(jnp.bfloat16)

    blocks = [sorted_block(first + j) for j in range(TOGETHER)]
    for j in range(TOGETHER):
        out_ref[at + j] = blocks[j]


def pack_second_body(
    source_ref, kernel_ref, columns_ref, observed_ref, weight_ref, place_ref, tally_ref, out_ref,
    *scratch,
):
    widen(observed_ref, weight_ref, *scratch)

    def step(i, carry):
        at = i * TOGETHER
        pack(
            at, source_ref, kernel_ref, columns_ref, place_ref, tally_ref, out_ref, at, *scratch
        )
        return carry

    lax.fori_loop(0, out_ref.shape[0] // TOGETHER, step, 0)


def pack_first_body(
    targets_ref, counts_ref, kernel_hbm, columns_ref, observed_ref, weight_ref,
    out_ref, place_ref, tally_ref, first_ref, second_ref,
    observed_wide, weight_wide, order_ref, kernel_ref, sem,
):
    scratch = (observed_wide, weight_wide, order_ref)

    @pl.when(pl.program_id(0) == 0)
    def _():
        copy = pltpu.make_async_copy(kernel_hbm, kernel_ref, sem)
        copy.start()
        widen(observed_ref, weight_ref, *scratch)
        plan(targets_ref, counts_ref, columns_ref, place_ref, first_ref, second_ref, tally_ref)
        copy.wait()

    pack(
        pl.program_id(0) * TOGETHER, first_ref, kernel_ref, columns_ref, place_ref, tally_ref,
        out_ref, 0, *scratch,
    )


def innovations_body(first_ref, second_ref, returned_ref, place_ref, out_ref, rows_ref):
    def one(device, carry):
        for rank, source_ref in enumerate((first_ref, second_ref)):
            source = source_ref[device]
            block = jnp.where(source >= 0, source, LANES)
            rows_ref[pl.ds(block, 1), :] = returned_ref[pl.ds(2 * device + rank, 1), :]
        return carry

    lax.fori_loop(0, first_ref.shape[0], one, 0, unroll=32)
    place = place_ref[...].astype(jnp.int32)
    live = place < LANES
    found = jnp.take_along_axis(
        rows_ref[: place.shape[0], :], jnp.where(live, place, 0), axis=1
    )
    out_ref[...] = jnp.where(live, found, jnp.float32(0.0))


def soundings(
    field_ref, block_ref, adjoint_ref, write_misfit, arrive,
    stream_ref, found_ref, cell_ref, tally_ref, count_ref, sem,
):
    n = WIDTH * LANES
    one, nil = jnp.bfloat16(1), jnp.bfloat16(0)
    lane = lax.broadcasted_iota(jnp.int32, (ROWS, LANES), 1)
    cell_ref[...] = (
        lax.broadcasted_iota(jnp.int32, (256, LANES), 0).astype(jnp.float32).astype(jnp.bfloat16)
    )
    empty = jnp.zeros((ROWS, LANES), jnp.bfloat16)
    eighth = lax.broadcasted_iota(jnp.int32, (8, LANES), 0)

    def tally(eight, carry):
        rows = jnp.zeros((8, LANES), jnp.float32)
        for j in range(8):
            meta = block_ref[eight * 8 + j][LEVELS:].astype(jnp.float32)
            rows = jnp.where(eighth == j, meta[4:5], rows)
        tally_ref[pl.ds(eight * 8, 8), :] = rows.astype(jnp.int32)
        return carry

    lax.fori_loop(0, block_ref.shape[0] // 8, tally, 0, unroll=8)
    copy = pltpu.make_async_copy(tally_ref, count_ref, sem)
    copy.start()
    copy.wait()

    def merge(block, carry):
        ends, tails = list(carry[0]), list(carry[1])
        values = block_ref[block]
        start = jnp.int32(0)
        for g in range(GROUPS):
            count = count_ref[block, g]
            tile, at = lax.shift_right_logical(ends[g], 7), ends[g] & (LANES - 1)
            turned = pltpu.roll(values, (at - start) & (LANES - 1), 1)
            joined = jnp.where(lane >= at, turned, tails[g])
            stream_ref[g, tile] = joined
            tails[g] = jnp.where(at + count >= LANES, turned, joined)
            ends[g] = ends[g] + count
            start = start + count
        return tuple(ends), tuple(tails)

    ends, tails = lax.fori_loop(
        0,
        block_ref.shape[0],
        merge,
        ((jnp.int32(0),) * GROUPS, (empty,) * GROUPS),
        unroll=16,
    )
    for g in range(GROUPS):
        tile, at = lax.shift_right_logical(ends[g], 7), ends[g] & (LANES - 1)
        stream_ref[g, tile] = jnp.where(lane < at, tails[g], empty)
        for j in range(1, WIDTH):
            stream_ref[g, tile + j] = empty

    arrive()

    def load(g, step):
        tiles = [stream_ref[g, step * WIDTH + i] for i in range(WIDTH)]
        profile = jnp.concatenate([t[:LEVELS] for t in tiles], axis=1)
        meta = jnp.concatenate([t[LEVELS:] for t in tiles], axis=1).astype(jnp.float32)
        part, cell, observed, weight = (meta[j : j + 1] for j in range(4))
        cell = cell.astype(jnp.bfloat16)
        hits = [
            cell_ref[...] == jnp.broadcast_to(cell[:, i * LANES : (i + 1) * LANES], (256, LANES))
            for i in range(WIDTH)
        ]
        pick = jnp.concatenate([jnp.where(hit, one, nil) for hit in hits], axis=1)
        return g, step, profile, part - 1.0, observed, weight, pick

    def gather(g, step, profile, part, observed, weight, pick):
        column = jnp.zeros((LEVELS, n), jnp.float32)
        for i in range(g * GROUP_PARTS // 2, (g + 1) * GROUP_PARTS // 2):
            found = jnp.dot(
                field_ref[2 * i * PAIR : 2 * (i + 1) * PAIR, :],
                pick,
                preferred_element_type=jnp.float32,
            )
            found = found[:PAIR] + found[PAIR:]
            column = jnp.where(part == 2.0 * i, found[:LEVELS], column)
            column = jnp.where(part == 2.0 * i + 1.0, found[LEVELS:], column)
        return column

    def force(column, g, step, profile, part, observed, weight, pick):
        wide = profile.astype(jnp.float32)
        model = jnp.sum(wide * column, axis=0, keepdims=True)
        misfit = model - observed
        for i in range(WIDTH):
            found_ref[g, step * WIDTH + i] = jnp.broadcast_to(
                misfit[:, i * LANES : (i + 1) * LANES], (8, LANES)
            )
        vector = wide * (weight * misfit)
        high = vector.astype(jnp.bfloat16)
        return high, (vector - high.astype(jnp.float32)).astype(jnp.bfloat16)

    def scatter(vector, g, step, profile, part, observed, weight, pick):
        high, low = (jnp.concatenate([term, term], axis=0) for term in vector)
        second = lax.broadcasted_iota(jnp.int32, (PAIR, n), 0) >= LEVELS
        part_row = (part - jnp.where(second, 1.0, 0.0)).astype(jnp.bfloat16)
        for i in range(g * GROUP_PARTS // 2, (g + 1) * GROUP_PARTS // 2):
            own = part_row == jnp.bfloat16(2 * i)
            sums = lax.dot_general(
                jnp.concatenate([jnp.where(own, high, nil), jnp.where(own, low, nil)], axis=0),
                pick,
                (((1,), (1,)), ((), ())),
                preferred_element_type=jnp.float32,
            )
            adjoint_ref[i * PAIR : (i + 1) * PAIR, :] += sums[:PAIR] + sums[PAIR:]

    def work(groups, step):
        loaded = [load(g, step) for g in groups]
        columns = [gather(*x) for x in loaded]
        vectors = [force(column, *x) for x, column in zip(loaded, columns)]
        for x, vector in zip(loaded, vectors):
            scatter(vector, *x)
        return 0

    steps = [lax.shift_right_logical(ends[g] + n - 1, n.bit_length() - 1) for g in range(GROUPS)]
    common = functools.reduce(jnp.minimum, steps)
    lax.fori_loop(0, common, lambda step, _: work(range(GROUPS), step), 0)
    for g in range(GROUPS):
        lax.fori_loop(common, steps[g], lambda step, _, g=g: work([g], step), 0)

    lane = lax.broadcasted_iota(jnp.int32, (8, LANES), 1)
    row_id = lax.broadcasted_iota(jnp.int32, (8, LANES), 0)

    def part_ways(eight, ends):
        ends = list(ends)
        rows = jnp.zeros((8, LANES), jnp.float32)
        for j in range(8):
            start = jnp.int32(0)
            row = jnp.zeros((8, LANES), jnp.float32)
            for g in range(GROUPS):
                count = count_ref[eight * 8 + j, g]
                tile, at = lax.shift_right_logical(ends[g], 7), ends[g] & (LANES - 1)
                values = jnp.where(lane >= at, found_ref[g, tile], found_ref[g, tile + 1])
                values = pltpu.roll(values, (start - at) & (LANES - 1), 1)
                row = jnp.where(lane >= start, values, row)
                ends[g] = ends[g] + count
                start = start + count
            rows = jnp.where(row_id == j, row, rows)
        write_misfit(eight, rows)
        return tuple(ends)

    lax.fori_loop(0, block_ref.shape[0] // 8, part_ways, (jnp.int32(0),) * GROUPS, unroll=4)


def first_soundings_body(
    field_hbm, block_ref, adjoint_ref, misfit_ref, field_ref, field_sem, *scratch
):
    copy = pltpu.make_async_copy(field_hbm, field_ref, field_sem)
    copy.start()
    adjoint_ref[...] = jnp.zeros_like(adjoint_ref)

    def write_misfit(eight, rows):
        misfit_ref[pl.ds(eight * 8, 8), :] = rows

    soundings(field_ref, block_ref, adjoint_ref, write_misfit, copy.wait, *scratch)


def second_soundings_body(
    field_hbm, block_ref, earlier_hbm, other_ref, adjoint_ref, misfit_ref, *rest
):
    edges, (field_ref, field_sem), scratch = rest[:4], rest[4:6], rest[6:-1]
    copies = [
        pltpu.make_async_copy(field_hbm, field_ref, field_sem),
        pltpu.make_async_copy(earlier_hbm, adjoint_ref, rest[-1]),
    ]
    for copy in copies:
        copy.start()

    def arrive():
        for copy in copies:
            copy.wait()

    def write_misfit(eight, rows):
        misfit_ref[pl.ds(eight * 16, 8, stride=2), :] = other_ref[pl.ds(eight * 8, 8), :]
        misfit_ref[pl.ds(eight * 16 + 1, 8, stride=2), :] = rows

    soundings(field_ref, block_ref, adjoint_ref, write_misfit, arrive, *scratch)
    write_edges(lambda t, row: cell_slab(adjoint_ref, t, row), *edges)


def observe(field, blocks, earlier=()):
    count = blocks.shape[0]
    tiles = count + WIDTH
    outs = [jax.ShapeDtypeStruct((PARTS * LEVELS, 256), jnp.float32)]
    outs += [jax.ShapeDtypeStruct((count * (2 if earlier else 1), LANES), jnp.float32)]
    return whole(
        second_soundings_body if earlier else first_soundings_body,
        outs + (EDGES if earlier else []),
        (field, blocks) + tuple(earlier),
        "second_soundings" if earlier else "first_soundings",
        in_hbm=(0, 2) if earlier else (0,),
        scratch=[
            pltpu.VMEM(field.shape, jnp.bfloat16),
            pltpu.SemaphoreType.DMA(()),
            pltpu.VMEM((GROUPS, tiles, ROWS, LANES), jnp.bfloat16),
            pltpu.VMEM((GROUPS, tiles, 8, LANES), jnp.float32),
            pltpu.VMEM((256, LANES), jnp.bfloat16),
            pltpu.VMEM((count, LANES), jnp.int32),
            pltpu.SMEM((count, LANES), jnp.int32),
            pltpu.SemaphoreType.DMA(()),
        ]
        + ([pltpu.SemaphoreType.DMA(())] if earlier else []),
        flops=15000000000,
    )


def per_device(
    initial, east_wind, north_wind, mixing, kernel, columns, observed, obs_weight, counts, targets
):
    lat_count = lax.axis_size("lat")
    lon_count = lax.axis_size("lon")
    sounds = kernel.shape[2]
    block_count = kernel.shape[0]
    device_count = lat_count * lon_count

    def exchange(array):
        return lax.all_to_all(array, ("lat", "lon"), split_axis=0, concat_axis=0, tiled=True)

    is_last = (lax.axis_index("lat") == lat_count - 1).astype(jnp.int32).reshape(1)
    winds_like = jax.ShapeDtypeStruct((2, LAT_CELLS, LEVELS, LANES), jnp.float32)

    def slabs_like(number):
        return jax.ShapeDtypeStruct((number, LEVELS, LANES), jnp.float32)

    grid = (is_last, initial, east_wind, north_wind, mixing)
    terms = [
        jax.ShapeDtypeStruct((14 + len(UP_LOW), LEVELS, LANES), jnp.bfloat16),
        jax.ShapeDtypeStruct((12 + len(DOWN_LOW), LEVELS, LANES), jnp.bfloat16),
    ]
    up, down = whole(rows_body, terms, grid, "rows", scalars=1)
    counts, up, down = lax.optimization_barrier((counts, up, down))
    from_south, from_north = shifted(up, 1, 0), shifted(down, -1, 0)
    slots = jax.ShapeDtypeStruct((device_count, ROWS, sounds), jnp.bfloat16)
    by_device = jax.ShapeDtypeStruct((device_count,), jnp.int32)
    heard = (kernel, columns, observed, obs_weight)
    scratch = [pltpu.VMEM((block_count, sounds), jnp.float32)] * 2
    scratch += [pltpu.VMEM((LANES, LANES), jnp.bfloat16)]
    by_block = jax.ShapeDtypeStruct((block_count, sounds), jnp.float32)
    out_first, place, tally, source_first, source_second = whole(
        pack_first_body,
        [slots, by_block, by_block, by_device, by_device],
        (targets[:, 0], counts) + heard,
        "pack_first",
        scratch=scratch
        + [pltpu.VMEM(kernel.shape, jnp.bfloat16), pltpu.SemaphoreType.DMA(())],
        scalars=2,
        scalar_outs=2,
        in_hbm=(2,),
        steps=device_count // TOGETHER,
    )
    (out_second,) = whole(
        pack_second_body,
        [slots],
        (source_second,) + heard + (place, tally),
        "pack_second",
        scratch=scratch,
        scalars=1,
    )
    out_first, from_south, from_north = lax.optimization_barrier(
        (out_first, from_south, from_north)
    )
    got_first = exchange(out_first)
    state, *rest = whole(
        arrange_body,
        [STATE, winds_like, winds_like, winds_like]
        + [slabs_like(3), slabs_like(3), slabs_like(14), slabs_like(12)],
        grid + (from_south, from_north),
        "arrange",
        scalars=1,
    )
    fields, (east, west, from_south, from_north) = tuple(rest[:3]), rest[3:]
    side_west, side_east = shifted(east, 0, 1), shifted(west, 0, -1)
    out_second, side_west, side_east = lax.optimization_barrier((out_second, side_west, side_east))
    got_second = exchange(out_second)
    (field,) = whole(
        forward_body,
        [jax.ShapeDtypeStruct((2 * PARTS * LEVELS, 256), jnp.bfloat16)],
        (state,) + fields + (east, west, from_south, from_north, side_west, side_east),
        "forward",
        scratch=[MIDDLE, pltpu.VMEM(STATE.shape, jnp.float32)],
    )
    earlier = observe(field, got_first)
    adjoint, misfit, up, down, own_east, own_west = observe(field, got_second, earlier)
    from_west, from_east = shifted(own_east, 0, 1), shifted(own_west, 0, -1)
    ends = jnp.stack([from_west, from_east])
    returned = exchange(misfit)
    (gradient,) = whole(
        adjoint_body,
        [jax.ShapeDtypeStruct(initial.shape, jnp.float32)],
        (adjoint,) + fields + (from_south, from_north, east, side_west, side_east)
        + (own_east, own_west, from_west, from_east)
        + (shifted(jnp.concatenate([up, ends]), 1, 0), shifted(jnp.concatenate([down, ends]), -1, 0)),
        "adjoint",
        scratch=[MIDDLE],
    )
    returned, gradient = lax.optimization_barrier((returned, gradient))
    (innovations,) = whole(
        innovations_body,
        [jax.ShapeDtypeStruct((block_count, sounds), jnp.float32)],
        (source_first, source_second, returned, place),
        "innovations",
        scratch=[pltpu.VMEM((block_count + 8, sounds), jnp.float32)],
        scalars=2,
    )
    return (gradient, innovations)


def solution(mesh):
    return jax.shard_map(
        per_device,
        mesh=mesh,
        in_specs=(
            P(None, None, "lat", "lon"),
            P(None, None, "lat", "lon"),
            P(None, None, "lat", "lon"),
            P(None, None, "lat", "lon"),
            P(("lat", "lon"), None, None),
            P(("lat", "lon"), None),
            P(("lat", "lon"), None),
            P(("lat", "lon"), None),
            P(("lat", "lon")),
            P(("lat", "lon"), None),
        ),
        out_specs=(P(None, None, "lat", "lon"), P(("lat", "lon"), None)),
        check_vma=False,
    )
```
